256 devices in a mesh: stream: 8 (over y_lo, x), radial: 8 (over z), span: 4 (over y_hi, core).
Axes of the slice: x: 4, y: 4 (y_hi: 2, y_lo: 2; y = y_hi * 2 + y_lo), z: 8, core: 2. Of those that a mesh axis runs over, the one named last changes fastest.
Arguments:
- log_conformation: float32 [6, 128, 64, 1024], P(None, 'radial', 'span', 'stream'), may hold values from -1 to 1
- velocity: float32 [3, 128, 64, 1024], P(None, 'radial', 'span', 'stream'), may hold values from -0.25 to 0.25
Outputs:
- next_conformation: float32 [6, 128, 64, 1024], P(None, 'radial', 'span', 'stream')
- pressure_modes: float32 [128, 64, 1024], P('radial', 'span', 'stream')
The draws below stay inside these ranges and needn't reach their ends.
All inputs are finite; a program needn't handle non-finite values.
Results may differ from the reference program's by a relative error of at most 0.0003.
Values sent between devices are 32-bit elements; how exact they have to be, the bound alone decides.
No kernel may reach another device: no remote copies, remote signals or barrier semaphores. Data moves between devices by JAX's collectives and lax.ppermute only.
A program may use at most 64 MiB of HBM per device.

```python
import math
import jax
import jax.numpy as jnp
from jax import lax

NX = 1024
NR = 128
NS = 64


def block_levels(stream_key, shape, cuts, smallest, largest):
    def one(dim, parts):
        draws = jax.random.uniform(jax.random.fold_in(jax.random.fold_in(stream_key, 6), dim), (parts,), jnp.float32, smallest / len(cuts), largest / len(cuts))
        return jnp.repeat(jnp.exp(draws), shape[dim] // parts).reshape((-1,) + (1,) * (len(shape) - dim - 1))

    factor_of = one(*cuts[0])
    for cut in cuts[1:]:
        factor_of = factor_of * one(*cut)
    return factor_of


def setup_inputs(seed: int = 0) -> dict:
    streams_of = jax.random.split(jax.random.key(seed), 3)
    log_conformation = jnp.clip(jax.random.uniform(streams_of[0], (6, NR, NS, NX), jnp.float32, -1.0, 1.0) * block_levels(streams_of[0], (6, NR, NS, NX), ((1, 8), (2, 4), (3, 8)), -0.4, 0.0), -1.0, 1.0)
    velocity = jnp.clip(jax.random.uniform(streams_of[1], (3, NR, NS, NX), jnp.float32, -0.25, 0.25) * block_levels(streams_of[1], (3, NR, NS, NX), ((1, 8), (2, 4), (3, 8)), -0.4, 0.0), -0.25, 0.25)
    return dict(log_conformation=log_conformation, velocity=velocity)


WEISSENBERG = 20.0
EXTENSIBILITY = 100.0
TIME_STEP = 2.0
EPSILON = 1e-6
SLOTS = ((0, 1, 2), (1, 3, 4), (2, 4, 5))
PAIRS = ((0, 0), (0, 1), (0, 2), (1, 1), (1, 2), (2, 2))
DIAGONAL = (0, 3, 5)
AXES = (2, 0, 1)
COSINES = tuple(math.cos((2 * number + 1) * math.pi / 12.0) for number in range(6))


def weno_blend(a, b, c, d, e):
    first = a / 3.0 - 7.0 * b / 6.0 + 11.0 * c / 6.0
    second = -b / 6.0 + 5.0 * c / 6.0 + d / 3.0
    third = c / 3.0 + 5.0 * d / 6.0 - e / 6.0
    rough_left = 13.0 / 12.0 * (a - 2.0 * b + c) ** 2 + 0.25 * (a - 4.0 * b + 3.0 * c) ** 2
    rough_middle = 13.0 / 12.0 * (b - 2.0 * c + d) ** 2 + 0.25 * (b - d) ** 2
    rough_right = 13.0 / 12.0 * (c - 2.0 * d + e) ** 2 + 0.25 * (3.0 * c - 4.0 * d + e) ** 2
    weight_left = 0.1 / (EPSILON + rough_left) ** 2
    weight_middle = 0.6 / (EPSILON + rough_middle) ** 2
    weight_right = 0.3 / (EPSILON + rough_right) ** 2
    return (weight_left * first + weight_middle * second + weight_right * third) / (weight_left + weight_middle + weight_right)


def upwind(padded, speeds, spatial):
    extent = speeds.shape[spatial]
    differences = jnp.diff(padded, axis=spatial)
    pieces = [lax.slice_in_dim(differences, offset, offset + extent, axis=spatial) for offset in range(6)]
    behind = weno_blend(pieces[0], pieces[1], pieces[2], pieces[3], pieces[4])
    forward = weno_blend(pieces[5], pieces[4], pieces[3], pieces[2], pieces[1])
    return jnp.where(speeds > 0, behind, forward)


def sym_product(left, right):
    output = []
    for upper_index, lower_index in PAIRS:
        running = left[SLOTS[upper_index][0]] * right[SLOTS[0][lower_index]]
        running = running + left[SLOTS[upper_index][1]] * right[SLOTS[1][lower_index]]
        running = running + left[SLOTS[upper_index][2]] * right[SLOTS[2][lower_index]]
        output.append(running)
    return output


def sym_exp(members, signed):
    scaled = [(signed * 0.125) * member for member in members]
    identity = [jnp.ones_like(members[0]) if position in DIAGONAL else jnp.zeros_like(members[0]) for position in range(6)]
    series = identity
    for degree in range(6, 0, -1):
        product = sym_product(scaled, series)
        series = [identity[position] + product[position] / degree for position in range(6)]
    for repeat in range(3):
        series = sym_product(series, series)
    return series


def conform(grown):
    trace_sum = grown[0] + grown[3] + grown[5]
    peterlin = (EXTENSIBILITY - 3.0) / (EXTENSIBILITY - trace_sum)
    stress = [peterlin * grown[position] - 1.0 if position in DIAGONAL else peterlin * grown[position] for position in range(6)]
    return peterlin, stress


def relaxation(shrunk, peterlin):
    return [shrunk[position] - peterlin if position in DIAGONAL else shrunk[position] for position in range(6)]


def central(quantity, spatial):
    extent = quantity.shape[spatial]
    return 0.5 * (lax.slice_in_dim(quantity, 2, extent, axis=spatial) - lax.slice_in_dim(quantity, 0, extent - 2, axis=spatial))


def shaved(quantity, spatial):
    extent = quantity.shape[spatial]
    return lax.slice_in_dim(quantity, 1, extent - 1, axis=spatial)


def flux_sum(columns):
    running = None
    for direction in range(3):
        contrib = central(columns[direction], AXES[direction])
        for another in range(3):
            if another != direction:
                contrib = shaved(contrib, AXES[another])
        running = contrib if running is None else running + contrib
    return running


def pressure_source(padded_stress):
    forcing = [flux_sum([padded_stress[SLOTS[row_dir][col_dir]] for col_dir in range(3)]) for row_dir in range(3)]
    return flux_sum(forcing)


def mode_weights(ordinal, period):
    midpoint = period // 2
    wavenumber = jnp.where(ordinal <= midpoint, ordinal, ordinal - midpoint)
    squared_wave = 4.0 * jnp.sin(math.pi * wavenumber.astype(jnp.float32) / period) ** 2
    diagonal = 4.0 + squared_wave
    ratio_term = 4.0 / diagonal
    upper_end = 1.0 + ratio_term
    lower_end = jnp.maximum(0.3, 1.0 - ratio_term)
    centre = 0.5 * (upper_end + lower_end)
    spread = 0.5 * (upper_end - lower_end)
    return diagonal, [1.0 / (centre + spread * cosine) for cosine in COSINES]


def relax(padded, source, diagonal, weighting):
    middle = padded[1:-1, 1:-1]
    beside_all = (padded[2:, 1:-1] + padded[:-2, 1:-1]) + (padded[1:-1, 2:] + padded[1:-1, :-2])
    return middle + weighting * (source - (diagonal * middle - beside_all)) / diagonal


def transport(quantity, velocity):
    wrapped = jnp.pad(quantity, ((0, 0), (0, 0), (3, 3)), mode="wrap")
    walled_radial = jnp.pad(quantity, ((3, 3), (0, 0), (0, 0)))
    walled_span = jnp.pad(quantity, ((0, 0), (3, 3), (0, 0)))
    slope_stream = upwind(wrapped, velocity[0], 2)
    slope_radial = upwind(walled_radial, velocity[1], 0)
    slope_span = upwind(walled_span, velocity[2], 1)
    return velocity[0] * slope_stream + velocity[1] * slope_radial + velocity[2] * slope_span


def reference(log_conformation, velocity):
    advection = lax.map(lambda quantity: transport(quantity, velocity), log_conformation)
    members = [log_conformation[position] for position in range(6)]
    grown = sym_exp(members, 1.0)
    shrunk = sym_exp(members, -1.0)
    peterlin, stress = conform(grown)
    next_conformation = log_conformation - TIME_STEP * advection + (TIME_STEP / WEISSENBERG) * jnp.stack(relaxation(shrunk, peterlin))
    padded_stress = [jnp.pad(jnp.pad(member, ((0, 0), (0, 0), (2, 2)), mode="wrap"), ((2, 2), (2, 2), (0, 0))) for member in stress]
    source_field = pressure_source(padded_stress)
    spectrum = jnp.fft.rfft(source_field, axis=2)
    midpoint = NX // 2
    cosine_part = jnp.real(spectrum) * NX ** -0.5
    sine_part = -jnp.imag(spectrum[:, :, 1:midpoint]) * NX ** -0.5
    mode_slab = jnp.concatenate([cosine_part, sine_part], axis=2).astype(jnp.float32)
    source = -mode_slab
    diagonal, omegas = mode_weights(jnp.arange(NX, dtype=jnp.int32), NX)
    solution = omegas[0] * source / diagonal
    for number in range(1, 6):
        solution = relax(jnp.pad(solution, ((1, 1), (1, 1), (0, 0))), source, diagonal, omegas[number])
    return next_conformation, solution
```

```python
import math

import jax
import jax.numpy as jnp
import ml_dtypes
import numpy as np
from jax import lax
from jax.experimental import pallas as pl
from jax.experimental.pallas import tpu as pltpu
from jax.sharding import PartitionSpec as P

NX = 1024
LANES = 128
BLOCK = 16
PARTS = 8
LINES = 60
ROWS = 64

WEISSENBERG = 20.0
EXTENSIBILITY = 100.0
TIME_STEP = 2.0
EPSILON = 1e-06
COSINES = tuple((math.cos((2 * number + 1) * math.pi / 12.0) for number in range(6)))
VMEM_LIMIT = 48 * 1024 * 1024


def split_bf16(table):
    high = table.astype(np.float32).astype(ml_dtypes.bfloat16)
    low = (table - high.astype(np.float64)).astype(np.float32).astype(ml_dtypes.bfloat16)
    return high, low


def tables():
    ordinal = np.arange(NX)
    wave = np.where(ordinal <= NX // 2, ordinal, ordinal - NX // 2)
    angle = 2.0 * np.pi / NX * ((ordinal[:, None] * wave[None, :]) % NX)
    fourier = -np.where((ordinal <= NX // 2)[None, :], np.cos(angle), np.sin(angle)) * NX**-0.5
    places = []
    for part in range(PARTS):
        start = part * LANES
        places += [start - 2, start - 1, start + LANES, start + LANES + 1]
    edges = fourier[np.array(places) % NX]
    return split_bf16(fourier) + split_bf16(edges)


def mode_table():
    ordinal = np.arange(NX)
    wave = np.where(ordinal <= NX // 2, ordinal, ordinal - NX // 2)
    diagonal = 4.0 + 4.0 * np.sin(np.pi * wave / NX) ** 2
    ratio = 4.0 / diagonal
    upper = 1.0 + ratio
    lower = np.maximum(0.3, 1.0 - ratio)
    rows = []
    for cosine in COSINES:
        omega = 1.0 / (0.5 * (upper + lower) + 0.5 * (upper - lower) * cosine)
        rows += [omega / diagonal, 1.0 - omega]
    rows += [np.zeros(NX)] * 4
    return np.stack(rows).astype(np.float32).reshape(16, PARTS, LANES).transpose(1, 0, 2)


TABLE_HIGH, TABLE_LOW, EDGE_HIGH, EDGE_LOW = tables()
MODES = mode_table()
PICK = np.zeros((8, LANES), np.float32)
for row, lane in enumerate((126, 127, 0, 1)):
    PICK[row, lane] = 1.0
ENDS = np.zeros((8, LANES), np.float32)
for row, lane in ((0, 0), (1, 1), (2, 2), (4, 125), (5, 126), (6, 127)):
    ENDS[row, lane] = 1.0


def params():
    return pltpu.CompilerParams(vmem_limit_bytes=VMEM_LIMIT)


VMEM = pl.BlockSpec(memory_space=pltpu.VMEM)
SMEM = pl.BlockSpec(memory_space=pltpu.SMEM)


def dot_nt(left, right):
    return lax.dot_general(
        left,
        right,
        (((1,), (1,)), ((), ())),
        precision=lax.Precision.HIGHEST,
        preferred_element_type=jnp.float32,
    )


def dot_tn(left, right, precision=None):
    return lax.dot_general(
        left,
        right,
        (((0,), (0,)), ((), ())),
        precision=precision,
        preferred_element_type=jnp.float32,
    )


def sym_square(m):
    a, b, c, d, e, f = m
    bb, cc, ee = b * b, c * c, e * e
    return [
        a * a + bb + cc,
        b * (a + d) + c * e,
        c * (a + f) + b * e,
        bb + d * d + ee,
        e * (d + f) + b * c,
        cc + ee + f * f,
    ]


def sym_times(m, n):
    a, b, c, d, e, f = m
    p, q, r, s, t, u = n
    return [
        a * p + b * q + c * r,
        a * q + b * s + c * t,
        a * r + b * t + c * u,
        b * q + d * s + e * t,
        b * r + d * t + e * u,
        c * r + e * t + f * u,
    ]


DIAG = (1.0, 0.0, 0.0, 1.0, 0.0, 1.0)


def with_diag(m, value):
    return [m[i] + value if DIAG[i] else m[i] for i in range(6)]


def exp_pair(psi):
    m = [0.125 * v for v in psi]
    m2 = sym_square(m)
    m3 = sym_times(m, m2)
    tail = [m[i] * (1.0 / 24) + m2[i] * (1.0 / 120) + m3[i] * (1.0 / 720) for i in range(6)]
    tail = sym_times(m3, with_diag(tail, 1.0 / 6))
    out = with_diag([m[i] + 0.5 * m2[i] + tail[i] for i in range(6)], 1.0)
    for _ in range(3):
        out = sym_square(out)
    a, b, c, d, e, f = out
    scale = jnp.exp(-(psi[0] + psi[3] + psi[5]))
    inverse = [
        (d * f - e * e) * scale,
        (c * e - b * f) * scale,
        (b * e - c * d) * scale,
        (a * f - c * c) * scale,
        (b * c - a * e) * scale,
        (a * d - b * b) * scale,
    ]
    return out, inverse


def source_kernel(psi_ref, pick_ref, ends_ref, send_ref, base_ref, left_ref, right_ref, up_ref, down_ref, stress, field, wrapped):
    zero = jnp.zeros((24, LANES), jnp.float32)
    for comp in (1, 3, 4):
        for row in (0, 1, 2, 3, 20, 21, 22, 23):
            stress[comp, row] = zero

    def relax_row(row, carry):
        psi = [psi_ref[comp, row] for comp in range(6)]
        grown, shrunk = exp_pair(psi)
        peterlin = (EXTENSIBILITY - 3.0) / (EXTENSIBILITY - (grown[0] + grown[3] + grown[5]))
        pad = jnp.zeros((8, LANES), jnp.float32)
        for comp in range(6):
            value = peterlin * grown[comp]
            back = shrunk[comp]
            if DIAG[comp]:
                value = value - 1.0
                back = back - peterlin
            stress[comp, row + 4, 0:16] = value
            stress[comp, row + 4, 16:24] = pad
            base_ref[comp, row] = psi[comp] + (TIME_STEP / WEISSENBERG) * back
        return carry

    lax.fori_loop(0, BLOCK, relax_row, 0)

    lane = lax.broadcasted_iota(jnp.int32, (24, LANES), 1)
    inner = [lane < LANES - 1, lane >= 1, lane < LANES - 2, lane >= 2]

    def along(value, shift):
        return pltpu.roll(value, shift % 24, 0)

    def shifted(value, shift):
        return pltpu.roll(value, shift % LANES, 1)

    def emit(row, plain, once, twice):
        parts = [shifted(once, -1), -shifted(once, 1), shifted(twice, -2), shifted(twice, 2)]
        total = plain - 2.0 * twice
        beyond = zero
        for part, mask in zip(parts, inner):
            kept = jnp.where(mask, part, 0.0)
            total = total + kept
            beyond = beyond + (part - kept)
        at = row * 24 if isinstance(row, int) else pl.multiple_of(row * 24, 8)
        field[pl.ds(at, 24)] = total
        wrapped[pl.ds(at, 24)] = beyond

    def body(row, carry):
        here = row + 2
        s11 = 0.25 * (stress[3, here + 2] - 2.0 * stress[3, here] + stress[3, here - 2])
        u12 = 0.5 * (stress[4, here + 1] - stress[4, here - 1])
        u01 = 0.5 * (stress[1, here + 1] - stress[1, here - 1])
        s22, s02, s00 = stress[5, here], stress[2, here], stress[0, here]
        c22 = 0.25 * (along(s22, -2) - 2.0 * s22 + along(s22, 2))
        c12 = along(u12, -1) - along(u12, 1)
        c02 = 0.5 * (along(s02, -1) - along(s02, 1))
        emit(row, s11 + c22 + c12, u01 + c02, 0.25 * s00)
        return carry

    lax.fori_loop(2, 18, body, 0)
    for row in (0, 1, 18, 19):
        here = row + 2
        other = here + 2 if row < 2 else here - 2
        s11 = 0.25 * stress[3, other]
        if row in (1, 18):
            near = here + 1 if row == 1 else here - 1
            sign = 0.5 if row == 1 else -0.5
            u12 = sign * stress[4, near]
            u01 = sign * stress[1, near]
            emit(row, s11 + along(u12, -1) - along(u12, 1), u01, zero)
        else:
            emit(row, s11, zero, zero)
    wrapped[480:488] = jnp.zeros((8, LANES), jnp.float32)
    pick = pick_ref[...]
    for part in range(PARTS):
        send_ref[part, 0:LINES] = field[part * LINES : part * LINES + LINES]
        lines = dot_nt(pick, wrapped[part * LINES : part * LINES + ROWS])
        send_ref[part, LINES:ROWS, 0:ROWS] = lines[0:4]
        send_ref[part, LINES:ROWS, ROWS:LANES] = jnp.zeros((4, LANES - ROWS), jnp.float32)

    ends = ends_ref[...]
    for comp in range(6):
        found = dot_nt(ends, psi_ref[comp].reshape(BLOCK * BLOCK, LANES))
        left_ref[comp * 4 : comp * 4 + 4] = found[0:4]
        right_ref[comp * 4 : comp * 4 + 4] = found[4:8]
        for near in range(3):
            down_ref[comp, near] = psi_ref[comp, :, near]
            up_ref[comp, near] = psi_ref[comp, :, BLOCK - 3 + near]


def local_source(psi):
    shape = jax.ShapeDtypeStruct
    return pl.pallas_call(
        source_kernel,
        out_shape=(
            shape((PARTS, ROWS, LANES), jnp.float32),
            shape(psi.shape, jnp.float32),
            shape((24, BLOCK * BLOCK), jnp.float32),
            shape((24, BLOCK * BLOCK), jnp.float32),
            shape((6, 3, BLOCK, LANES), jnp.float32),
            shape((6, 3, BLOCK, LANES), jnp.float32),
        ),
        in_specs=[VMEM] * 3,
        out_specs=[VMEM] * 6,
        scratch_shapes=[
            pltpu.VMEM((6, 24, 24, LANES), jnp.float32),
            pltpu.VMEM((480, LANES), jnp.float32),
            pltpu.VMEM((488, LANES), jnp.float32),
        ],
        compiler_params=params(),
        cost_estimate=pl.CostEstimate(flops=20_000_000, bytes_accessed=3_000_000, transcendentals=0),
        name="local_source",
    )(psi, jnp.asarray(PICK), jnp.asarray(ENDS))


def transform_kernel(lines_ref, high_ref, low_ref, edge_high_ref, edge_low_ref, out_ref):
    lines = jnp.concatenate([lines_ref[part] for part in range(PARTS)], axis=1)
    high = lines.astype(jnp.bfloat16)
    low = (lines - high.astype(jnp.float32)).astype(jnp.bfloat16)
    edges = jnp.concatenate([lines_ref[part, LINES:ROWS] for part in range(PARTS)], axis=0)
    edges_high = edges.astype(jnp.bfloat16).astype(jnp.float32)
    edges_low = edges - edges_high
    edges_high = edges_high.astype(jnp.bfloat16)
    edges_low = edges_low.astype(jnp.bfloat16)
    both = jnp.concatenate([high, low], axis=0)
    for part in range(PARTS):
        cols = slice(part * LANES, (part + 1) * LANES)
        table = high_ref[:, cols]
        first = jnp.dot(both, table, preferred_element_type=jnp.float32)
        second = jnp.dot(high, low_ref[:, cols], preferred_element_type=jnp.float32)
        edge_table = edge_high_ref[:, cols]
        third = dot_tn(edges_high, edge_table) + dot_tn(edges_low, edge_table)
        third = third + dot_tn(edges_high, edge_low_ref[:, cols])
        out_ref[part] = (first[0:ROWS] + third[0:ROWS]) + (first[ROWS:] + second)


def transform(lines):
    return pl.pallas_call(
        transform_kernel,
        out_shape=jax.ShapeDtypeStruct((PARTS, ROWS, LANES), jnp.float32),
        in_specs=[VMEM] * 5,
        out_specs=VMEM,
        compiler_params=params(),
        cost_estimate=pl.CostEstimate(flops=400_000_000, bytes_accessed=5_000_000, transcendentals=0),
        name="transform",
    )(lines, jnp.asarray(TABLE_HIGH), jnp.asarray(TABLE_LOW), jnp.asarray(EDGE_HIGH), jnp.asarray(EDGE_LOW))


def radial_kernel(place_ref, own_ref, low_ref, high_ref, out_ref, up_ref, down_ref, flat, flat_low, flat_high):
    for part in range(PARTS):
        flat[part * LINES : part * LINES + LINES] = own_ref[part, 0:LINES]
    for part in range(3):
        flat_low[part * LINES + 4 : part * LINES + 4 + LINES] = low_ref[part, 0:LINES]
        flat_high[part * LINES : part * LINES + LINES] = high_ref[part, 0:LINES]
    has_low = place_ref[1] > 0
    has_high = place_ref[1] < 7

    def own(row):
        return flat[row * 24 : row * 24 + 24]

    def low(row):
        at = (row - 13) * 24 + 16
        return jnp.where(has_low, flat_low[at : at + 24], 0.0)

    def high(row):
        return jnp.where(has_high, flat_high[row * 24 : row * 24 + 24], 0.0)

    for row in range(26):
        if row < 3:
            value = low(row + 13)
        elif row < 5:
            value = low(row + 13) + jnp.where(has_low, own(row - 3), 0.0)
        elif row < 7:
            value = low(row + 13) + own(row - 3)
        elif row < 19:
            value = own(row - 3)
        elif row < 21:
            value = own(row - 3) + high(row - 19)
        elif row < 23:
            value = jnp.where(has_high, own(row - 3), 0.0) + high(row - 19)
        else:
            value = high(row - 19)
        out_ref[row] = value
        up_ref[row] = pltpu.roll(value, 24 - 11, 0)[0:8]
        down_ref[row] = pltpu.roll(value, 2, 0)[0:8]


def radial_assembly(place, own, low, high):
    shape = jax.ShapeDtypeStruct
    return pl.pallas_call(
        radial_kernel,
        out_shape=(
            shape((26, 24, LANES), jnp.float32),
            shape((26, 8, LANES), jnp.float32),
            shape((26, 8, LANES), jnp.float32),
        ),
        in_specs=[SMEM] + [VMEM] * 3,
        out_specs=[VMEM] * 3,
        scratch_shapes=[
            pltpu.VMEM((480, LANES), jnp.float32),
            pltpu.VMEM((192, LANES), jnp.float32),
            pltpu.VMEM((184, LANES), jnp.float32),
        ],
        compiler_params=params(),
        cost_estimate=pl.CostEstimate(flops=300_000, bytes_accessed=1_000_000, transcendentals=0),
        name="radial_assembly",
    )(place, own, low, high)


def relax_kernel(place_ref, modes_ref, rows_ref, low_ref, high_ref, out_ref, source, even, odd):
    radial, span = place_ref[1], place_ref[2]
    has_low = span > 0
    has_high = span < 3
    sublane = lax.broadcasted_iota(jnp.int32, (8, LANES), 0)
    cell = lax.broadcasted_iota(jnp.int32, (32, LANES), 0)
    inside = ((cell < 16) | ((cell < 24) & has_high)) | ((cell >= 24) & has_low)
    modes = modes_ref[place_ref[0]]
    weights = [
        jnp.where(inside, jnp.broadcast_to(modes[2 * j : 2 * j + 1], (32, LANES)), 0.0) for j in range(6)
    ]
    keeps = [jnp.broadcast_to(modes[2 * j + 1 : 2 * j + 2], (32, LANES)) for j in range(6)]
    pad = jnp.zeros((24, LANES), jnp.float32)
    for row in range(26):
        own = rows_ref[row]
        tail = own[16:24]
        own = jnp.concatenate(
            [own[0:16], jnp.where(sublane < 2, tail, 0.0), jnp.where(sublane >= 6, tail, 0.0)], axis=0
        )
        low = jnp.concatenate([jnp.where(has_low, low_ref[row], 0.0), pad], axis=0)
        high = jnp.concatenate([jnp.where(has_high, high_ref[row], 0.0), pad], axis=0)
        value = own + pltpu.roll(low, 27, 0) + pltpu.roll(high, 14, 0)
        source[row] = value
        even[row] = value * weights[0]

    no_low = radial == 0
    no_high = radial == 7

    @pl.when(no_low)
    def _():
        for row in range(5):
            even[row] = jnp.zeros((32, LANES), jnp.float32)
            odd[row] = jnp.zeros((32, LANES), jnp.float32)

    @pl.when(no_high)
    def _():
        for row in range(21, 26):
            even[row] = jnp.zeros((32, LANES), jnp.float32)
            odd[row] = jnp.zeros((32, LANES), jnp.float32)

    old, new = even, odd
    for sweep in range(1, 6):
        weight, keep = weights[sweep], keeps[sweep]
        for row in range(sweep, 26 - sweep):
            middle = old[row]
            beside = (old[row - 1] + old[row + 1]) + (pltpu.roll(middle, 1, 0) + pltpu.roll(middle, 31, 0))
            value = keep * middle + weight * (source[row] + beside)
            if sweep == 5:
                out_ref[row - 5] = value[0:16]
            elif row < 5:
                new[row] = jnp.where(no_low, 0.0, value)
            elif row > 20:
                new[row] = jnp.where(no_high, 0.0, value)
            else:
                new[row] = value
        old, new = new, old


def relaxation(place, rows, low, high):
    return pl.pallas_call(
        relax_kernel,
        out_shape=jax.ShapeDtypeStruct((BLOCK, BLOCK, LANES), jnp.float32),
        in_specs=[SMEM] + [VMEM] * 4,
        out_specs=VMEM,
        scratch_shapes=[pltpu.VMEM((26, 32, LANES), jnp.float32)] * 3,
        compiler_params=params(),
        cost_estimate=pl.CostEstimate(flops=5_000_000, bytes_accessed=1_000_000, transcendentals=0),
        name="relaxation",
    )(place, jnp.asarray(MODES), rows, low, high)


def weno(positive, d):
    a = jnp.where(positive, d[0], d[5])
    b = jnp.where(positive, d[1], d[4])
    c = jnp.where(positive, d[2], d[3])
    e = jnp.where(positive, d[3], d[2])
    g = jnp.where(positive, d[4], d[1])
    p0, p1, p2, p3 = a - b, b - c, c - e, e - g
    t0, t1, t2 = p0 - p1, p1 - p2, p2 - p3
    h0, h1, h2 = t0 - 2.0 * p1, p1 + p2, t2 + 2.0 * p2
    q0 = (13.0 / 3.0) * (t0 * t0) + (h0 * h0 + 4.0 * EPSILON)
    q1 = (13.0 / 3.0) * (t1 * t1) + (h1 * h1 + 4.0 * EPSILON)
    q2 = (13.0 / 3.0) * (t2 * t2) + (h2 * h2 + 4.0 * EPSILON)
    q0, q1, q2 = q0 * q0, q1 * q1, q2 * q2
    w0 = q1 * q2
    w1 = 6.0 * (q0 * q2)
    w2 = 3.0 * (q0 * q1)
    top = w0 * (2.0 * p0 - 5.0 * p1) - w1 * (p1 + 2.0 * p2) + w2 * (p3 - 4.0 * p2)
    return c + top / (6.0 * (w0 + w1 + w2))


def advect_kernel(place_ref, ends_ref, psi_ref, velocity_ref, base_ref, low_ref, high_ref, down_ref, up_ref, left_ref, right_ref, out_ref, radial, beside, ahead):
    has_low, has_high = place_ref[1] > 0, place_ref[1] < 7
    has_down, has_up = place_ref[2] > 0, place_ref[2] < 3
    for comp in range(6):
        for near in range(3):
            radial[comp, near] = jnp.where(has_low, low_ref[comp, near], 0.0)
            radial[comp, 19 + near] = jnp.where(has_high, high_ref[comp, near], 0.0)
            beside[comp, :, near] = jnp.where(has_up, up_ref[comp, near], 0.0)
            beside[comp, :, 5 + near] = jnp.where(has_down, down_ref[comp, near], 0.0)
        for row in range(BLOCK):
            radial[comp, 3 + row] = psi_ref[comp, row]
        ends = jnp.concatenate([right_ref[comp * 4 : comp * 4 + 4], left_ref[comp * 4 : comp * 4 + 4]], axis=0)
        found = dot_tn(ends, ends_ref[...], lax.Precision.HIGHEST)
        ahead[comp] = found.reshape(BLOCK, BLOCK, LANES)
    lane = lax.broadcasted_iota(jnp.int32, (BLOCK, LANES), 1)

    def step(number, carry):
        comp, row = number // BLOCK, number % BLOCK
        speeds = [velocity_ref[direction, row] for direction in range(3)]
        psi = radial[comp, row + 3]
        lines = [radial[comp, row + k] for k in range(7)]
        total = speeds[1] * weno(speeds[1] > 0, [lines[k + 1] - lines[k] for k in range(6)])

        far = ahead[comp, row]
        lines = []
        for k in range(-3, 4):
            if k > 0:
                mixed = jnp.where(lane < k, far, psi)
            else:
                mixed = jnp.where(lane >= LANES + k, far, psi)
            lines.append(pltpu.roll(mixed, (-k) % LANES, 1) if k else psi)
        total = total + speeds[0] * weno(speeds[0] > 0, [lines[k + 1] - lines[k] for k in range(6)])

        column = jnp.concatenate([psi, beside[comp, row]], axis=0)
        column = pltpu.roll(column, 23, 0) - column
        steps = [pltpu.roll(column, (-k) % 24, 0)[0:16] if k else column[0:16] for k in range(-3, 3)]
        total = total + speeds[2] * weno(speeds[2] > 0, steps)
        out_ref[comp, row] = base_ref[comp, row] - TIME_STEP * total
        return carry

    lax.fori_loop(0, 6 * BLOCK, step, 0)


def advect(place, psi, velocity, base, low, high, down, up, left, right):
    return pl.pallas_call(
        advect_kernel,
        out_shape=jax.ShapeDtypeStruct(psi.shape, jnp.float32),
        in_specs=[SMEM] + [VMEM] * 10,
        out_specs=VMEM,
        scratch_shapes=[
            pltpu.VMEM((6, 22, BLOCK, LANES), jnp.float32),
            pltpu.VMEM((6, BLOCK, 8, LANES), jnp.float32),
            pltpu.VMEM((6, BLOCK, BLOCK, LANES), jnp.float32),
        ],
        compiler_params=params(),
        cost_estimate=pl.CostEstimate(flops=50_000_000, bytes_accessed=4_000_000, transcendentals=0),
        name="advect",
    )(place, jnp.asarray(ENDS), psi, velocity, base, low, high, down, up, left, right)


def ring(axis, step):
    count = lax.axis_size(axis)
    return [(i, (i + step) % count) for i in range(count)]


def exchange(to_next, to_previous, axis):
    return (
        lax.ppermute(to_next, axis, ring(axis, 1)),
        lax.ppermute(to_previous, axis, ring(axis, -1)),
    )


def shards(psi, velocity):
    place = jnp.stack([lax.axis_index(axis) for axis in ("stream", "radial", "span")]).astype(jnp.int32)
    send, base, ends_left, ends_right, up, down = local_source(psi)
    low, high = exchange(psi[:, BLOCK - 3 :], psi[:, :3], "radial")
    from_down, from_up = exchange(up, down, "span")
    from_left, from_right = exchange(ends_right, ends_left, "stream")

    lines = lax.all_to_all(send, "stream", split_axis=0, concat_axis=0, tiled=True)
    spectrum = transform(lines)
    own = lax.all_to_all(spectrum, "stream", split_axis=0, concat_axis=0, tiled=True)
    below, above = exchange(own[5:], own[:3], "radial")
    rows, rows_up, rows_down = radial_assembly(place, own, below, above)
    before, after = exchange(rows_up, rows_down, "span")
    modes = relaxation(place, rows, before, after)
    following = advect(place, psi, velocity, base, low, high, from_down, from_up, from_left, from_right)
    return following, modes


def solution(mesh):
    return jax.shard_map(
        shards,
        mesh=mesh,
        in_specs=(P(None, "radial", "span", "stream"), P(None, "radial", "span", "stream")),
        out_specs=(P(None, "radial", "span", "stream"), P("radial", "span", "stream")),
        check_vma=False,
    )
```

```python
import functools
import math

import jax
import jax.numpy as jnp
import ml_dtypes
import numpy as np
from jax import lax
from jax.experimental import pallas as pl
from jax.experimental.pallas import tpu as pltpu
from jax.sharding import PartitionSpec as P

NX = 1024
LANES = 128
BLOCK = 16
PARTS = 8
FULL = (6, BLOCK, BLOCK, LANES)
LINES = 60
ROWS = 64

WEISSENBERG = 20.0
EXTENSIBILITY = 100.0
TIME_STEP = 2.0
EPSILON = 1e-06
COSINES = tuple((math.cos((2 * number + 1) * math.pi / 12.0) for number in range(6)))
QUARTER = NX // 4
VMEM_LIMIT = 16 * 1024 * 1024


def split_bf16(table):
    high = table.astype(np.float32).astype(ml_dtypes.bfloat16)
    low = (table - high.astype(np.float64)).astype(np.float32).astype(ml_dtypes.bfloat16)
    return high, low


def tables():
    ordinal = np.arange(NX)
    wave = np.where(ordinal <= NX // 2, ordinal, ordinal - NX // 2)
    angle = 2.0 * np.pi / NX * ((ordinal[:, None] * wave[None, :]) % NX)
    fourier = -np.where((ordinal <= NX // 2)[None, :], np.cos(angle), np.sin(angle)) * NX**-0.5
    places = []
    for part in range(PARTS):
        start = part * LANES
        places += [start - 2, start - 1, start + LANES, start + LANES + 1]
    high, low = split_bf16(fourier[:QUARTER])
    edge_high, edge_low = split_bf16(fourier[np.array(places) % NX])
    return high, low, np.concatenate([edge_high, edge_high, edge_low])


def mode_table():
    ordinal = np.arange(NX)
    wave = np.where(ordinal <= NX // 2, ordinal, ordinal - NX // 2)
    diagonal = 4.0 + 4.0 * np.sin(np.pi * wave / NX) ** 2
    ratio = 4.0 / diagonal
    upper = 1.0 + ratio
    lower = np.maximum(0.3, 1.0 - ratio)
    rows = []
    for cosine in COSINES:
        omega = 1.0 / (0.5 * (upper + lower) + 0.5 * (upper - lower) * cosine)
        rows += [omega / diagonal, 1.0 - omega]
    modes = np.stack(rows).reshape(12, PARTS, LANES).transpose(1, 0, 2)
    found = np.zeros((PARTS, 8, 4, 24, LANES), np.float32)
    found[:, :, :, 0:12] = modes[:, None, None]
    found[:, 1:, :, 16] = 1.0
    found[:, :7, :, 17] = 1.0
    found[:, :, 1:, 18] = 1.0
    found[:, :, :3, 19] = 1.0
    found[:, :, ::2, 20] = 1.0
    return found.reshape(PARTS * 32, 24, LANES)


def flag(place_ref, number, rows=8):
    return jnp.broadcast_to(place_ref[16 + number : 17 + number], (rows, LANES)) > 0.5


TABLE = tables()
PLACES = mode_table()


def params(limit=VMEM_LIMIT):
    return pltpu.CompilerParams(vmem_limit_bytes=limit)


def cost(microseconds):
    return pl.CostEstimate(
        flops=int(microseconds * 1.1e9), bytes_accessed=int(microseconds * 3.6e6), transcendentals=0
    )


VMEM = pl.BlockSpec(memory_space=pltpu.VMEM)
SMEM = pl.BlockSpec(memory_space=pltpu.SMEM)
HBM = pl.BlockSpec(memory_space=pltpu.HBM)
ANY = pl.BlockSpec(memory_space=pl.ANY)


def dot_nt(left, right):
    return lax.dot_general(left, right, (((1,), (1,)), ((), ())), preferred_element_type=jnp.float32)


def dot_tn(left, right):
    return lax.dot_general(left, right, (((0,), (0,)), ((), ())), preferred_element_type=jnp.float32)


def pieces(value, count):
    found = []
    for _ in range(count):
        found.append(value.astype(jnp.bfloat16))
        value = value - found[-1].astype(jnp.float32)
    return found


def selection(shape, pairs):
    row = lax.broadcasted_iota(jnp.int32, shape, 0)
    column = lax.broadcasted_iota(jnp.int32, shape, 1)
    hit = None
    for first, last, shift in pairs:
        here = (row >= first) & (row <= last) & (column == row + shift)
        hit = here if hit is None else hit | here
    return jnp.where(hit, 1.0, 0.0).astype(jnp.bfloat16)


def sym_square(m):
    a, b, c, d, e, f = m
    bb, cc, ee = b * b, c * c, e * e
    return [
        a * a + bb + cc,
        b * (a + d) + c * e,
        c * (a + f) + b * e,
        bb + d * d + ee,
        e * (d + f) + b * c,
        cc + ee + f * f,
    ]


def sym_times(m, n):
    a, b, c, d, e, f = m
    p, q, r, s, t, u = n
    return [
        a * p + b * q + c * r,
        a * q + b * s + c * t,
        a * r + b * t + c * u,
        b * q + d * s + e * t,
        b * r + d * t + e * u,
        c * r + e * t + f * u,
    ]


DIAG = (1.0, 0.0, 0.0, 1.0, 0.0, 1.0)


def with_diag(m, value):
    return [m[i] + value if DIAG[i] else m[i] for i in range(6)]


def sym_exp(psi):
    m = [0.125 * v for v in psi]
    m2 = sym_square(m)
    m3 = sym_times(m, m2)
    tail = [m[i] * (1.0 / 24) + m2[i] * (1.0 / 120) + m3[i] * (1.0 / 720) for i in range(6)]
    tail = sym_times(m3, with_diag(tail, 1.0 / 6))
    out = with_diag([m[i] + 0.5 * m2[i] + tail[i] for i in range(6)], 1.0)
    for _ in range(3):
        out = sym_square(out)
    return out


def sym_inverse(grown, psi):
    a, b, c, d, e, f = grown
    scale = jnp.exp(-(psi[0] + psi[3] + psi[5]))
    return [
        (d * f - e * e) * scale,
        (c * e - b * f) * scale,
        (b * e - c * d) * scale,
        (a * f - c * c) * scale,
        (b * c - a * e) * scale,
        (a * d - b * b) * scale,
    ]


def spring(grown):
    return (EXTENSIBILITY - 3.0) / (EXTENSIBILITY - (grown[0] + grown[3] + grown[5]))


def source_kernel(psi_ref, send_ref, token_ref, stress, field, wrapped):
    token_ref[...] = jnp.zeros_like(token_ref)
    zero = jnp.zeros((24, LANES), jnp.float32)
    for comp in (1, 3, 4):
        for row in (0, 1, 2, 3, 20, 21, 22, 23):
            stress[comp, row] = zero

    def relax_row(row, carry):
        psi = [psi_ref[comp, row] for comp in range(6)]
        grown = sym_exp(psi)
        peterlin = spring(grown)
        pad = jnp.zeros((8, LANES), jnp.float32)
        for comp in range(6):
            value = peterlin * grown[comp]
            stress[comp, row + 4, 0:16] = value - 1.0 if DIAG[comp] else value
            stress[comp, row + 4, 16:24] = pad
        return carry

    lax.fori_loop(0, BLOCK, relax_row, 0, unroll=EXP_UNROLL)

    lane = lax.broadcasted_iota(jnp.int32, (24, LANES), 1)
    inner = [lane < LANES - 1, lane >= 1, lane < LANES - 2, lane >= 2]

    def along(value, shift):
        return pltpu.roll(value, shift % 24, 0)

    def shifted(value, shift):
        return pltpu.roll(value, shift % LANES, 1)

    def emit(row, plain, once, twice):
        parts = [shifted(once, -1), -shifted(once, 1), shifted(twice, -2), shifted(twice, 2)]
        total = plain - 2.0 * twice
        beyond = zero
        for part, mask in zip(parts, inner):
            kept = jnp.where(mask, part, 0.0)
            total = total + kept
            beyond = beyond + (part - kept)
        at = row * 24 if isinstance(row, int) else pl.multiple_of(row * 24, 8)
        field[pl.ds(at, 24)] = total
        wrapped[pl.ds(at, 24)] = beyond

    def body(row, carry):
        here = row + 2
        s11 = 0.25 * (stress[3, here + 2] - 2.0 * stress[3, here] + stress[3, here - 2])
        u12 = 0.5 * (stress[4, here + 1] - stress[4, here - 1])
        u01 = 0.5 * (stress[1, here + 1] - stress[1, here - 1])
        s22, s02, s00 = stress[5, here], stress[2, here], stress[0, here]
        c22 = 0.25 * (along(s22, -2) - 2.0 * s22 + along(s22, 2))
        c12 = along(u12, -1) - along(u12, 1)
        c02 = 0.5 * (along(s02, -1) - along(s02, 1))
        emit(row, s11 + c22 + c12, u01 + c02, 0.25 * s00)
        return carry

    lax.fori_loop(2, 18, body, 0, unroll=SOURCE_UNROLL)
    for row in (0, 1, 18, 19):
        here = row + 2
        other = here + 2 if row < 2 else here - 2
        s11 = 0.25 * stress[3, other]
        if row in (1, 18):
            near = here + 1 if row == 1 else here - 1
            sign = 0.5 if row == 1 else -0.5
            u12 = sign * stress[4, near]
            u01 = sign * stress[1, near]
            emit(row, s11 + along(u12, -1) - along(u12, 1), u01, zero)
        else:
            emit(row, s11, zero, zero)
    wrapped[480:488] = jnp.zeros((8, LANES), jnp.float32)
    pick = selection((8, 2 * LANES), ((0, 1, 126), (2, 3, -2)))
    pick = pick + selection((8, 2 * LANES), ((0, 1, 126 + LANES), (2, 3, LANES - 2)))
    for part in range(PARTS):
        send_ref[part, 0:LINES] = field[part * LINES : part * LINES + LINES]
        lines = jnp.concatenate(pieces(wrapped[part * LINES : part * LINES + ROWS], 2), axis=1)
        lines = dot_nt(pick, lines)
        send_ref[part, LINES:ROWS, 0:ROWS] = lines[0:4]
        send_ref[part, LINES:ROWS, ROWS:LANES] = jnp.zeros((4, LANES - ROWS), jnp.float32)


EXP_UNROLL = 2
SOURCE_UNROLL = 4


def local_source(psi):
    shape = jax.ShapeDtypeStruct
    return pl.pallas_call(
        source_kernel,
        out_shape=(
            shape((PARTS, ROWS, LANES), jnp.float32),
            shape((8, LANES), jnp.float32),
        ),
        in_specs=[VMEM],
        out_specs=[VMEM] * 2,
        scratch_shapes=[
            pltpu.VMEM((6, 24, 24, LANES), jnp.float32),
            pltpu.VMEM((480, LANES), jnp.float32),
            pltpu.VMEM((488, LANES), jnp.float32),
        ],
        compiler_params=params(),
        cost_estimate=cost(3.0),
        name="local_source",
    )(psi)


def message_kernel(place_ref, psi_ref, after_ref, left_ref, right_ref, first_ref, second_ref, high_ref, low_ref):
    even = flag(place_ref, 4, BLOCK)
    ends = sum(
        (selection((8, 3 * LANES), ((0, 2, k * LANES), (4, 6, k * LANES + 121))) for k in range(1, 3)),
        selection((8, 3 * LANES), ((0, 2, 0), (4, 6, 121))),
    )
    for comp in range(6):
        lines = jnp.concatenate(pieces(psi_ref[comp].reshape(BLOCK * BLOCK, LANES), 3), axis=1)
        found = dot_nt(ends, lines)
        left_ref[comp * 4 : comp * 4 + 4] = found[0:4]
        right_ref[comp * 4 : comp * 4 + 4] = found[4:8]
        for near in range(3):
            down = psi_ref[comp, :, near]
            up = psi_ref[comp, :, BLOCK - 3 + near]
            first_ref[comp, near] = jnp.where(even, up, down)
            second_ref[comp, near] = jnp.where(even, down, up)
            low_ref[comp, near] = psi_ref[comp, near]
            high_ref[comp, near] = psi_ref[comp, BLOCK - 3 + near]


def messages(place, psi, after):
    shape = jax.ShapeDtypeStruct
    return pl.pallas_call(
        message_kernel,
        out_shape=[shape((24, BLOCK * BLOCK), jnp.float32)] * 2
        + [shape((6, 3, BLOCK, LANES), jnp.float32)] * 4,
        in_specs=[VMEM, VMEM, ANY],
        out_specs=[VMEM] * 6,
        compiler_params=params(),
        cost_estimate=cost(4.0),
        name="messages",
    )(place, psi, after)


def transform_kernel(lines_ref, high_ref, low_ref, edge_ref, *rest):
    out_ref = rest[-1]
    quarter = [jnp.concatenate([lines_ref[2 * k], lines_ref[2 * k + 1]], axis=1) for k in range(4)]
    even = [quarter[k] + quarter[k + 2] for k in range(2)]
    odd = [quarter[k] - quarter[k + 2] for k in range(2)]
    high, low = pieces(jnp.concatenate([even[0] + even[1], even[0] - even[1]] + odd, axis=0), 2)
    both = jnp.concatenate([high, low], axis=0)
    edges = jnp.concatenate([lines_ref[part, LINES:ROWS] for part in range(PARTS)], axis=0)
    edges_high, edges_low = pieces(jnp.transpose(edges)[0:ROWS], 2)
    edges = jnp.concatenate([edges_high, edges_low, edges_high], axis=1)
    wide = 2 * LANES
    found = []
    for part in range(4):
        cols = slice(part * wide, (part + 1) * wide)
        first = jnp.dot(both, high_ref[:, cols], preferred_element_type=jnp.float32)
        second = jnp.dot(high, low_ref[:, cols], preferred_element_type=jnp.float32)
        found.append(first[0 : 4 * ROWS] + (first[4 * ROWS :] + second))
    phase = lax.broadcasted_iota(jnp.int32, (ROWS, wide), 1) % 4
    turn = jnp.where(phase == 1, -1.0, 1.0)
    for part in range(4):
        cols = slice(part * wide, (part + 1) * wide)
        beyond = jnp.dot(edges, edge_ref[:, cols], preferred_element_type=jnp.float32)
        crossed = turn * found[(part + 2) % 4][3 * ROWS :]
        straight = found[part][2 * ROWS : 3 * ROWS]
        total = straight + crossed if part < 2 else straight - crossed
        total = jnp.where(phase == 0, found[part][0:ROWS], total)
        total = jnp.where(phase == 2, found[part][ROWS : 2 * ROWS], total) + beyond
        out_ref[2 * part] = total[:, 0:LANES]
        out_ref[2 * part + 1] = total[:, LANES:]


def transform(lines, after):
    return pl.pallas_call(
        transform_kernel,
        out_shape=jax.ShapeDtypeStruct((PARTS, ROWS, LANES), jnp.float32),
        in_specs=[VMEM] * 4 + [ANY] * len(after),
        out_specs=VMEM,
        compiler_params=params(),
        cost_estimate=cost(1.5),
        name="transform",
    )(lines, *(jnp.asarray(table) for table in TABLE), *after)


def radial_kernel(place_ref, own_ref, low_ref, high_ref, after_ref, out_ref, first_ref, second_ref, flat, flat_low, flat_high):
    for part in range(PARTS):
        flat[part * LINES : part * LINES + LINES] = own_ref[part, 0:LINES]
    for part in range(3):
        flat_low[part * LINES + 4 : part * LINES + 4 + LINES] = low_ref[part, 0:LINES]
        flat_high[part * LINES : part * LINES + LINES] = high_ref[part, 0:LINES]
    has_low, has_high = flag(place_ref, 0, 24), flag(place_ref, 1, 24)
    even = flag(place_ref, 4)

    def own(row):
        return flat[row * 24 : row * 24 + 24]

    def low(row):
        at = (row - 13) * 24 + 16
        return jnp.where(has_low, flat_low[at : at + 24], 0.0)

    def high(row):
        return jnp.where(has_high, flat_high[row * 24 : row * 24 + 24], 0.0)

    for row in range(26):
        if row < 3:
            value = low(row + 13)
        elif row < 5:
            value = low(row + 13) + jnp.where(has_low, own(row - 3), 0.0)
        elif row < 7:
            value = low(row + 13) + own(row - 3)
        elif row < 19:
            value = own(row - 3)
        elif row < 21:
            value = own(row - 3) + high(row - 19)
        elif row < 23:
            value = jnp.where(has_high, own(row - 3), 0.0) + high(row - 19)
        else:
            value = high(row - 19)
        out_ref[row] = value
        up = pltpu.roll(value, 24 - 11, 0)[0:8]
        down = pltpu.roll(value, 2, 0)[0:8]
        first_ref[row] = jnp.where(even, up, down)
        second_ref[row] = jnp.where(even, down, up)


def radial_assembly(place, own, low, high, after):
    shape = jax.ShapeDtypeStruct
    return pl.pallas_call(
        radial_kernel,
        out_shape=(
            shape((26, 24, LANES), jnp.float32),
            shape((26, 8, LANES), jnp.float32),
            shape((26, 8, LANES), jnp.float32),
        ),
        in_specs=[VMEM] * 4 + [ANY],
        out_specs=[VMEM] * 3,
        scratch_shapes=[
            pltpu.VMEM((480, LANES), jnp.float32),
            pltpu.VMEM((192, LANES), jnp.float32),
            pltpu.VMEM((184, LANES), jnp.float32),
        ],
        compiler_params=params(),
        cost_estimate=cost(0.6),
        name="radial_assembly",
    )(place, own, low, high, after)


def relax_kernel(place_ref, rows_ref, first_ref, second_ref, *rest):
    whole_ref, out_ref, following_hbm, source, even, odd, sem = rest
    copy = pltpu.make_async_copy(whole_ref, following_hbm, sem)
    copy.start()
    has_low, has_high, even_span = (flag(place_ref, number) for number in (2, 3, 4))
    open_low, open_high = flag(place_ref, 0, 32), flag(place_ref, 1, 32)
    sublane = lax.broadcasted_iota(jnp.int32, (8, LANES), 0)
    always = sublane >= 0
    inside = jnp.concatenate(
        [jnp.where(part, 1.0, 0.0) for part in (always, always, has_high, has_low)], axis=0
    )
    modes = place_ref[0:12]
    weights = [
        inside * jnp.broadcast_to(modes[2 * j : 2 * j + 1], (32, LANES)) for j in range(6)
    ]
    keeps = [jnp.broadcast_to(modes[2 * j + 1 : 2 * j + 2], (32, LANES)) for j in range(6)]
    pad = jnp.zeros((24, LANES), jnp.float32)
    for row in range(26):
        own = rows_ref[row]
        tail = own[16:24]
        own = jnp.concatenate(
            [own[0:16], jnp.where(sublane < 2, tail, 0.0), jnp.where(sublane >= 6, tail, 0.0)], axis=0
        )
        first, other = first_ref[row], second_ref[row]
        low = jnp.where(has_low, jnp.where(even_span, other, first), 0.0)
        high = jnp.where(has_high, jnp.where(even_span, first, other), 0.0)
        low = jnp.concatenate([low, pad], axis=0)
        high = jnp.concatenate([high, pad], axis=0)
        value = own + pltpu.roll(low, 27, 0) + pltpu.roll(high, 14, 0)
        source[row] = value
        value = value * weights[0]
        if row < 5:
            value = jnp.where(open_low, value, 0.0)
        elif row > 20:
            value = jnp.where(open_high, value, 0.0)
        even[row] = value

    old, new = even, odd
    for sweep in range(1, 6):
        weight, keep = weights[sweep], keeps[sweep]
        for row in range(sweep, 26 - sweep):
            middle = old[row]
            beside = (old[row - 1] + old[row + 1]) + (pltpu.roll(middle, 1, 0) + pltpu.roll(middle, 31, 0))
            value = keep * middle + weight * (source[row] + beside)
            if sweep == 5:
                out_ref[row - 5] = value[0:16]
            elif row < 5:
                new[row] = jnp.where(open_low, value, 0.0)
            elif row > 20:
                new[row] = jnp.where(open_high, value, 0.0)
            else:
                new[row] = value
        old, new = new, old
    copy.wait()


def relaxation(place, rows, low, high, whole):
    shape = jax.ShapeDtypeStruct
    return pl.pallas_call(
        relax_kernel,
        out_shape=(
            shape((BLOCK, BLOCK, LANES), jnp.float32),
            shape((6, BLOCK, BLOCK, LANES), jnp.float32),
        ),
        in_specs=[VMEM] * 5,
        out_specs=(VMEM, HBM),
        scratch_shapes=[pltpu.VMEM((26, 32, LANES), jnp.float32)] * 3 + [pltpu.SemaphoreType.DMA],
        compiler_params=params(),
        cost_estimate=cost(1.8),
        name="relaxation",
    )(place, rows, low, high, whole)


def weno(positive, p):
    p0 = jnp.where(positive, p[0], p[4])
    p1 = jnp.where(positive, p[1], p[3])
    p2 = p[2]
    p3 = jnp.where(positive, p[3], p[1])
    k1 = (0.609375 * p1) * p1 + 0.75 * EPSILON
    k2 = (0.609375 * p2) * p2 + 0.75 * EPSILON
    r0 = p0 - 1.375 * p1
    r1 = p1 - 0.625 * p2
    r2 = p3 - 1.375 * p2
    q0, q1, q2 = r0 * r0 + k1, r1 * r1 + k2, r2 * r2 + k2
    q01, q02, q12 = q0 * q1, q0 * q2, q1 * q2
    w0, w1, w2 = q12 * q12, 6.0 * (q02 * q02), 3.0 * (q01 * q01)
    middle = p1 - p2
    t0 = (p0 - p1) - middle
    t2 = middle - (p2 - p3)
    total = (w0 + w1) + w2
    guess = pl_reciprocal(total, approx=True)
    inverse = guess * (2.0 - total * guess)
    return ((w0 + w0) * t0 + w2 * t2) * inverse - p1


pl_reciprocal = pltpu.reciprocal


def wind(velocity_ref, direction, row):
    speed = velocity_ref[direction, row]
    positive = speed > 0
    straight = TIME_STEP * speed
    bent = (TIME_STEP / 6) * jnp.abs(speed)
    return positive, straight, bent, jnp.where(positive, 1.0 / 3, 2.0 / 3)


def advected(blow, behind, p):
    positive, straight, bent, side = blow
    return straight * (behind - side * p[2]) + bent * weno(positive, p)


def stream_kernel(psi_ref, velocity_ref, left_ref, right_ref, *rest):
    out_ref, ahead = rest[-2:]
    spread = []
    for comp in range(6):
        ends = jnp.concatenate([right_ref[comp * 4 : comp * 4 + 4], left_ref[comp * 4 : comp * 4 + 4]], axis=0)
        spread += pieces(ends, 3)
    spread = jnp.concatenate([v.astype(jnp.float32) for v in spread], axis=0)
    spread = jnp.transpose(spread).astype(jnp.bfloat16)
    for comp in range(6):
        pairs = []
        for piece in range(3):
            start = comp * 24 + piece * 8
            pairs += [(start, start + 2, -start), (start + 4, start + 6, 121 - start)]
        found = jnp.dot(spread, selection((144, LANES), pairs), preferred_element_type=jnp.float32)
        ahead[comp] = found.reshape(BLOCK, BLOCK, LANES)
    lane = lax.broadcasted_iota(jnp.int32, (BLOCK, LANES), 1)

    def step(row, carry):
        blow = wind(velocity_ref, 0, row)
        tensor = [psi_ref[comp, row] for comp in range(6)]
        grown = sym_exp(tensor)
        peterlin = spring(grown)
        shrunk = sym_inverse(grown, tensor)
        for comp in range(6):
            back = shrunk[comp] - peterlin if DIAG[comp] else shrunk[comp]
            psi = tensor[comp]
            far = ahead[comp, row]
            lines = []
            for j in range(-3, 4):
                if j > 0:
                    mixed = jnp.where(lane < j, far, psi)
                else:
                    mixed = jnp.where(lane >= LANES + j, far, psi)
                lines.append(pltpu.roll(mixed, (-j) % LANES, 1) if j else psi)
            steps = [lines[j + 1] - lines[j] for j in range(6)]
            change = advected(blow, steps[2], [steps[j] - steps[j + 1] for j in range(5)])
            out_ref[comp, row] = (psi + (TIME_STEP / WEISSENBERG) * back) - change
        return carry

    lax.fori_loop(0, BLOCK, step, 0, unroll=STEP_UNROLL)


def span_kernel(place_ref, psi_ref, velocity_ref, base_ref, first_ref, second_ref, *rest):
    out_ref, column, second = rest[-3:]
    has_down, has_up, even = (flag(place_ref, number, BLOCK) for number in (2, 3, 4))
    for comp in range(6):
        for near in range(3):
            first, other = first_ref[comp, near], second_ref[comp, near]
            column[comp, :, 5 + near] = jnp.where(has_down, jnp.where(even, other, first), 0.0)
            column[comp, :, 24 + near] = jnp.where(has_up, jnp.where(even, first, other), 0.0)

    def bend(row, carry):
        for comp in range(6):
            column[comp, row, 8:24] = psi_ref[comp, row]
            one, two, three = column[comp, row, 5:25], column[comp, row, 6:26], column[comp, row, 7:27]
            second[comp, row, 5:25] = (two - one) - (three - two)
        return carry

    lax.fori_loop(0, BLOCK, bend, 0)

    def step(row, carry):
        blow = wind(velocity_ref, 2, row)
        for comp in range(6):
            behind = psi_ref[comp, row] - column[comp, row, 7:23]
            change = advected(blow, behind, [second[comp, row, 5 + j : 21 + j] for j in range(5)])
            out_ref[comp, row] = base_ref[comp, row] - change
        return carry

    lax.fori_loop(0, BLOCK, step, 0, unroll=STEP_UNROLL)


def radial_kernel_step(place_ref, psi_ref, velocity_ref, base_ref, low_ref, high_ref, *rest):
    out_ref, column, second = rest[-3:]
    has_low, has_high = flag(place_ref, 0, BLOCK), flag(place_ref, 1, BLOCK)
    for comp in range(6):
        for near in range(3):
            column[comp, near] = jnp.where(has_low, low_ref[comp, near], 0.0)
            column[comp, 19 + near] = jnp.where(has_high, high_ref[comp, near], 0.0)

    def copy_in(row, carry):
        for comp in range(6):
            column[comp, row + 3] = psi_ref[comp, row]
        return carry

    lax.fori_loop(0, BLOCK, copy_in, 0)

    def bend(row, carry):
        for comp in range(6):
            one, two, three = column[comp, row], column[comp, row + 1], column[comp, row + 2]
            second[comp, row] = (two - one) - (three - two)
        return carry

    lax.fori_loop(0, 20, bend, 0)

    def step(row, carry):
        blow = wind(velocity_ref, 1, row)
        for comp in range(6):
            behind = column[comp, row + 3] - column[comp, row + 2]
            change = advected(blow, behind, [second[comp, row + j] for j in range(5)])
            out_ref[comp, row] = base_ref[comp, row] - change
        return carry

    lax.fori_loop(0, BLOCK, step, 0, unroll=STEP_UNROLL)


STEP_UNROLL = 1


def advect(kernel, name, scratch, arrays, after):
    return pl.pallas_call(
        kernel,
        out_shape=jax.ShapeDtypeStruct(FULL, jnp.float32),
        in_specs=[VMEM] * len(arrays) + [ANY] * len(after),
        out_specs=VMEM,
        scratch_shapes=[pltpu.VMEM(shape, jnp.float32) for shape in scratch],
        compiler_params=params(),
        cost_estimate=cost(2.5),
        name=name,
    )(*arrays, *after)


def ring(axis, step):
    count = lax.axis_size(axis)
    return [(i, (i + step) % count) for i in range(count)]


def exchange(to_next, to_previous, axis):
    return (
        lax.ppermute(to_next, axis, ring(axis, 1)),
        lax.ppermute(to_previous, axis, ring(axis, -1)),
    )


def trade(first, second, axis):
    count = lax.axis_size(axis)
    inner = [(i, i ^ 1) for i in range(count)]
    outer = [(i, (i - 1) % count if i % 2 == 0 else (i + 1) % count) for i in range(count)]
    return lax.ppermute(first, axis, inner), lax.ppermute(second, axis, outer)


def shards(psi, velocity):
    number = (lax.axis_index("stream") * 8 + lax.axis_index("radial")) * 4 + lax.axis_index("span")
    place = lax.dynamic_index_in_dim(jnp.asarray(PLACES), number, 0, keepdims=False)
    wide = (6, BLOCK, 32, LANES)
    tall = [(6, 22, BLOCK, LANES), (6, 20, BLOCK, LANES)]
    send, token = local_source(psi)
    lines = lax.all_to_all(send, "stream", split_axis=0, concat_axis=0, tiled=True)
    to_left, to_right, to_first, to_second, to_high, to_low = messages(place, psi, token)
    ends = exchange(to_right, to_left, "stream")
    sides = trade(to_first, to_second, "span")
    spectrum = transform(lines, ends)
    own = lax.all_to_all(spectrum, "stream", split_axis=0, concat_axis=0, tiled=True)
    state = advect(stream_kernel, "advect_stream", [FULL], (psi, velocity) + ends, (spectrum,))
    below, above = exchange(own[5:], own[:3], "radial")
    to_high, to_low = lax.optimization_barrier((to_high, to_low, spectrum))[:2]
    walls = exchange(to_high, to_low, "radial")
    state = advect(span_kernel, "advect_span", [wide, wide], (place, psi, velocity, state) + sides, (own,))
    rows, rows_first, rows_second = radial_assembly(place, own, below, above, state)
    first, second = trade(rows_first, rows_second, "span")
    state = advect(radial_kernel_step, "advect_radial", tall, (place, psi, velocity, state) + walls, (rows,))
    modes, following = relaxation(place, rows, first, second, state)
    return following, modes


def solution(mesh):
    return jax.shard_map(
        shards,
        mesh=mesh,
        in_specs=(P(None, "radial", "span", "stream"), P(None, "radial", "span", "stream")),
        out_specs=(P(None, "radial", "span", "stream"), P("radial", "span", "stream")),
        check_vma=False,
    )
```

```python
import functools
import math

import jax
import jax.numpy as jnp
import ml_dtypes
import numpy as np
from jax import lax
from jax.experimental import pallas as pl
from jax.experimental.pallas import tpu as pltpu
from jax.sharding import PartitionSpec as P

NX = 1024
LANES = 128
BLOCK = 16
PARTS = 8
FULL = (6, BLOCK, BLOCK, LANES)
LINES = 60
ROWS = 64

WEISSENBERG = 20.0
EXTENSIBILITY = 100.0
TIME_STEP = 2.0
EPSILON = 1e-06
COSINES = tuple((math.cos((2 * number + 1) * math.pi / 12.0) for number in range(6)))
VMEM_LIMIT = 16 * 1024 * 1024
SOURCE_VMEM = 62 * 1024 * 1024


def split_bf16(table):
    high = table.astype(np.float32).astype(ml_dtypes.bfloat16)
    low = (table - high.astype(np.float64)).astype(np.float32).astype(ml_dtypes.bfloat16)
    return high, low


def tables():
    ordinal = np.arange(NX)
    wave = np.where(ordinal <= NX // 2, ordinal, ordinal - NX // 2)
    angle = 2.0 * np.pi / NX * ((ordinal[:, None] * wave[None, :]) % NX)
    fourier = -np.where((ordinal <= NX // 2)[None, :], np.cos(angle), np.sin(angle)) * NX**-0.5
    return split_bf16(fourier[:LANES])


def mode_table():
    ordinal = np.arange(NX)
    wave = np.where(ordinal <= NX // 2, ordinal, ordinal - NX // 2)
    diagonal = 4.0 + 4.0 * np.sin(np.pi * wave / NX) ** 2
    ratio = 4.0 / diagonal
    upper = 1.0 + ratio
    lower = np.maximum(0.3, 1.0 - ratio)
    rows = []
    for cosine in COSINES:
        omega = 1.0 / (0.5 * (upper + lower) + 0.5 * (upper - lower) * cosine)
        rows += [omega / diagonal, 1.0 - omega]
    modes = np.stack(rows).reshape(12, PARTS, LANES).transpose(1, 0, 2)
    found = np.zeros((PARTS, 8, 4, 24, LANES), np.float32)
    found[:, :, :, 0:12] = modes[:, None, None]
    found[:, 1:, :, 16] = 1.0
    found[:, :7, :, 17] = 1.0
    found[:, :, 1:, 18] = 1.0
    found[:, :, :3, 19] = 1.0
    found[:, :, ::2, 20] = 1.0
    return found.reshape(PARTS * 32, 24, LANES)


def flag(place_ref, number, rows=8):
    return jnp.broadcast_to(place_ref[16 + number : 17 + number], (rows, LANES)) > 0.5


TABLE = tables()
PLACES = mode_table()


def params(limit=VMEM_LIMIT):
    return pltpu.CompilerParams(vmem_limit_bytes=limit)


def cost(microseconds):
    return pl.CostEstimate(
        flops=int(microseconds * 1.1e9), bytes_accessed=int(microseconds * 3.6e6), transcendentals=0
    )


VMEM = pl.BlockSpec(memory_space=pltpu.VMEM)
SMEM = pl.BlockSpec(memory_space=pltpu.SMEM)
HBM = pl.BlockSpec(memory_space=pltpu.HBM)
ANY = pl.BlockSpec(memory_space=pl.ANY)


def dot_nt(left, right):
    return lax.dot_general(left, right, (((1,), (1,)), ((), ())), preferred_element_type=jnp.float32)


def dot_tn(left, right):
    return lax.dot_general(left, right, (((0,), (0,)), ((), ())), preferred_element_type=jnp.float32)


def pieces(value, count):
    found = []
    for _ in range(count):
        found.append(value.astype(jnp.bfloat16))
        value = value - found[-1].astype(jnp.float32)
    return found


def selection(shape, pairs):
    row = lax.broadcasted_iota(jnp.int32, shape, 0)
    column = lax.broadcasted_iota(jnp.int32, shape, 1)
    hit = None
    for first, last, shift in pairs:
        here = (row >= first) & (row <= last) & (column == row + shift)
        hit = here if hit is None else hit | here
    return jnp.where(hit, 1.0, 0.0).astype(jnp.bfloat16)


def sym_square(m):
    a, b, c, d, e, f = m
    bb, cc, ee = b * b, c * c, e * e
    return [
        a * a + bb + cc,
        b * (a + d) + c * e,
        c * (a + f) + b * e,
        bb + d * d + ee,
        e * (d + f) + b * c,
        cc + ee + f * f,
    ]


def sym_times(m, n):
    a, b, c, d, e, f = m
    p, q, r, s, t, u = n
    return [
        a * p + b * q + c * r,
        a * q + b * s + c * t,
        a * r + b * t + c * u,
        b * q + d * s + e * t,
        b * r + d * t + e * u,
        c * r + e * t + f * u,
    ]


DIAG = (1.0, 0.0, 0.0, 1.0, 0.0, 1.0)


def with_diag(m, value):
    return [m[i] + value if DIAG[i] else m[i] for i in range(6)]


def sym_exp(psi):
    m = [0.125 * v for v in psi]
    m2 = sym_square(m)
    m3 = sym_times(m, m2)
    tail = [m[i] * (1.0 / 24) + m2[i] * (1.0 / 120) + m3[i] * (1.0 / 720) for i in range(6)]
    tail = sym_times(m3, with_diag(tail, 1.0 / 6))
    out = with_diag([m[i] + 0.5 * m2[i] + tail[i] for i in range(6)], 1.0)
    for _ in range(3):
        out = sym_square(out)
    return out


def sym_inverse(grown, psi):
    a, b, c, d, e, f = grown
    scale = jnp.exp(-(psi[0] + psi[3] + psi[5]))
    return [
        (d * f - e * e) * scale,
        (c * e - b * f) * scale,
        (b * e - c * d) * scale,
        (a * f - c * c) * scale,
        (b * c - a * e) * scale,
        (a * d - b * b) * scale,
    ]


def spring(grown):
    return (EXTENSIBILITY - 3.0) / (EXTENSIBILITY - (grown[0] + grown[3] + grown[5]))


def source_kernel(psi_hbm, send_ref, psi_ref, stress, field, wrapped, sems):
    chunk = BLOCK // SOURCE_CHUNKS
    arrivals = []
    for part in range(SOURCE_CHUNKS):
        rows = pl.ds(part * chunk, chunk)
        arrivals.append(pltpu.make_async_copy(psi_hbm.at[:, rows], psi_ref.at[:, rows], sems.at[part]))
        arrivals[-1].start()
    zero = jnp.zeros((24, LANES), jnp.float32)
    for comp in (1, 3, 4):
        for row in (0, 1, 2, 3, 20, 21, 22, 23):
            stress[comp, row] = zero

    def relax_row(row, carry):
        psi = [psi_ref[comp, row] for comp in range(6)]
        grown = sym_exp(psi)
        peterlin = spring(grown)
        pad = jnp.zeros((8, LANES), jnp.float32)
        for comp in range(6):
            value = peterlin * grown[comp]
            stress[comp, row + 4, 0:16] = value - 1.0 if DIAG[comp] else value
            stress[comp, row + 4, 16:24] = pad
        return carry

    for part in range(SOURCE_CHUNKS):
        arrivals[part].wait()
        lax.fori_loop(part * chunk, part * chunk + chunk, relax_row, 0, unroll=EXP_UNROLL)

    lane = lax.broadcasted_iota(jnp.int32, (24, LANES), 1)
    inner = [lane < LANES - 1, lane >= 1, lane < LANES - 2, lane >= 2]

    def along(value, shift):
        return pltpu.roll(value, shift % 24, 0)

    def shifted(value, shift):
        return pltpu.roll(value, shift % LANES, 1)

    def emit(row, plain, once, twice):
        parts = [shifted(once, -1), -shifted(once, 1), shifted(twice, -2), shifted(twice, 2)]
        total = plain - 2.0 * twice
        beyond = zero
        for part, mask in zip(parts, inner):
            kept = jnp.where(mask, part, 0.0)
            total = total + kept
            beyond = beyond + (part - kept)
        at = row * 24 if isinstance(row, int) else pl.multiple_of(row * 24, 8)
        field[pl.ds(at, 24)] = total
        wrapped[pl.ds(at, 24)] = beyond

    def body(row, carry):
        here = row + 2
        s11 = 0.25 * (stress[3, here + 2] - 2.0 * stress[3, here] + stress[3, here - 2])
        u12 = 0.5 * (stress[4, here + 1] - stress[4, here - 1])
        u01 = 0.5 * (stress[1, here + 1] - stress[1, here - 1])
        s22, s02, s00 = stress[5, here], stress[2, here], stress[0, here]
        c22 = 0.25 * (along(s22, -2) - 2.0 * s22 + along(s22, 2))
        c12 = along(u12, -1) - along(u12, 1)
        c02 = 0.5 * (along(s02, -1) - along(s02, 1))
        emit(row, s11 + c22 + c12, u01 + c02, 0.25 * s00)
        return carry

    lax.fori_loop(2, 18, body, 0, unroll=SOURCE_UNROLL)
    for row in (0, 1, 18, 19):
        here = row + 2
        other = here + 2 if row < 2 else here - 2
        s11 = 0.25 * stress[3, other]
        if row in (1, 18):
            near = here + 1 if row == 1 else here - 1
            sign = 0.5 if row == 1 else -0.5
            u12 = sign * stress[4, near]
            u01 = sign * stress[1, near]
            emit(row, s11 + along(u12, -1) - along(u12, 1), u01, zero)
        else:
            emit(row, s11, zero, zero)
    wrapped[480:488] = jnp.zeros((8, LANES), jnp.float32)
    pick = selection((8, 2 * LANES), ((0, 1, 126), (2, 3, -2)))
    pick = pick + selection((8, 2 * LANES), ((0, 1, 126 + LANES), (2, 3, LANES - 2)))
    for part in range(PARTS):
        send_ref[part, 0:LINES] = field[part * LINES : part * LINES + LINES]
        lines = jnp.concatenate(pieces(wrapped[part * LINES : part * LINES + ROWS], 2), axis=1)
        lines = dot_nt(pick, lines)
        send_ref[part, LINES:ROWS, 0:ROWS] = lines[0:4]
        send_ref[part, LINES:ROWS, ROWS:LANES] = jnp.zeros((4, LANES - ROWS), jnp.float32)


EXP_UNROLL = 2
SOURCE_CHUNKS = 4
SOURCE_UNROLL = 8


def local_source(psi):
    shape = jax.ShapeDtypeStruct
    return pl.pallas_call(
        source_kernel,
        out_shape=shape((PARTS, ROWS, LANES), jnp.float32),
        in_specs=[HBM],
        out_specs=VMEM,
        scratch_shapes=[
            pltpu.VMEM(FULL, jnp.float32),
            pltpu.VMEM((6, 24, 24, LANES), jnp.float32),
            pltpu.VMEM((480, LANES), jnp.float32),
            pltpu.VMEM((488, LANES), jnp.float32),
            pltpu.SemaphoreType.DMA((SOURCE_CHUNKS,)),
        ],
        compiler_params=params(SOURCE_VMEM),
        cost_estimate=cost(3.0),
        name="local_source",
    )(psi)


def message_kernel(place_ref, psi_ref, left_ref, right_ref, first_ref, second_ref, high_ref, low_ref):
    even = flag(place_ref, 4, BLOCK)
    ends = sum(
        (selection((8, 3 * LANES), ((0, 2, k * LANES), (4, 6, k * LANES + 121))) for k in range(1, 3)),
        selection((8, 3 * LANES), ((0, 2, 0), (4, 6, 121))),
    )
    for comp in range(6):
        lines = jnp.concatenate(pieces(psi_ref[comp].reshape(BLOCK * BLOCK, LANES), 3), axis=1)
        found = dot_nt(ends, lines)
        left_ref[comp * 4 : comp * 4 + 4] = found[0:4]
        right_ref[comp * 4 : comp * 4 + 4] = found[4:8]
        for near in range(3):
            down = psi_ref[comp, :, near]
            up = psi_ref[comp, :, BLOCK - 3 + near]
            first_ref[comp, near] = jnp.where(even, up, down)
            second_ref[comp, near] = jnp.where(even, down, up)
            low_ref[comp, near] = psi_ref[comp, near]
            high_ref[comp, near] = psi_ref[comp, BLOCK - 3 + near]


def messages(place, psi):
    shape = jax.ShapeDtypeStruct
    return pl.pallas_call(
        message_kernel,
        out_shape=[shape((24, BLOCK * BLOCK), jnp.float32)] * 2
        + [shape((6, 3, BLOCK, LANES), jnp.float32)] * 4,
        in_specs=[VMEM, VMEM],
        out_specs=[VMEM] * 6,
        compiler_params=params(),
        cost_estimate=cost(4.0),
        name="messages",
    )(place, psi)


def transform_kernel(lines_ref, high_ref, low_ref, *rest):
    out_ref = rest[-1]
    edges = jnp.concatenate([lines_ref[part, LINES:ROWS] for part in range(PARTS)], axis=0)
    edges = jnp.concatenate(pieces(jnp.transpose(edges)[0:ROWS], 2), axis=1)
    row = lax.broadcasted_iota(jnp.int32, (8 * PARTS, NX), 0) & (4 * PARTS - 1)
    lane = lax.broadcasted_iota(jnp.int32, (8 * PARTS, NX), 1)
    offset = jnp.where((row & 3) < 2, (row & 3) - 2, (row & 3) + LANES - 2)
    target = ((row >> 2) * LANES + offset + NX) & (NX - 1)
    target = jnp.where(lane == target, 1.0, 0.0).astype(jnp.bfloat16)
    beyond = jnp.dot(edges, target, preferred_element_type=jnp.float32)
    f = [lines_ref[part] + beyond[:, part * LANES : (part + 1) * LANES] for part in range(PARTS)]
    s = [f[k] + f[k + 4] for k in range(4)]
    o = [f[k] - f[k + 4] for k in range(4)]
    half = math.sqrt(0.5)
    p0, p1, q0, q1 = s[0] + s[2], s[1] + s[3], s[0] - s[2], s[1] - s[3]
    minus, plus = half * (o[1] - o[3]), half * (o[1] + o[3])
    left = [p0 + p1, p0 - p1, q0, o[0] + minus, o[0] - minus, q1, plus + o[2], plus - o[2]]
    high, low = pieces(jnp.concatenate(left, axis=0), 2)
    both = jnp.concatenate([high, low], axis=1)
    wide = 2 * LANES
    found = []
    for part in range(4):
        cols = slice(part * wide, (part + 1) * wide)
        table = jnp.concatenate([high_ref[:, cols]] * 2, axis=0)
        first = jnp.dot(both, table, preferred_element_type=jnp.float32)
        second = jnp.dot(high, low_ref[:, cols], preferred_element_type=jnp.float32)
        found.append([first[k * ROWS : (k + 1) * ROWS] + second[k * ROWS : (k + 1) * ROWS] for k in range(8)])
    phase = lax.broadcasted_iota(jnp.int32, (ROWS, wide), 1) % 8
    outer = (phase == 1) | (phase == 7)
    middle = phase % 4 == 2
    turn = jnp.where(phase % 4 == 0, 0.0, jnp.where(phase < 4, 1.0, -1.0))
    for part in range(4):
        here, there = found[part], found[(part + 2) % 4]
        straight = jnp.where(middle, here[2], jnp.where(outer, here[3], here[4]))
        straight = jnp.where(phase == 0, here[0], jnp.where(phase == 4, here[1], straight))
        crossed = turn * jnp.where(middle, there[5], jnp.where(outer, there[6], there[7]))
        total = straight - crossed if part < 2 else straight + crossed
        out_ref[2 * part] = total[:, 0:LANES]
        out_ref[2 * part + 1] = total[:, LANES:]


def transform(lines, after):
    return pl.pallas_call(
        transform_kernel,
        out_shape=jax.ShapeDtypeStruct((PARTS, ROWS, LANES), jnp.float32),
        in_specs=[VMEM] * 3 + [ANY] * len(after),
        out_specs=VMEM,
        compiler_params=params(),
        cost_estimate=cost(1.5),
        name="transform",
    )(lines, *(jnp.asarray(table) for table in TABLE), *after)


def radial_kernel(place_ref, own_ref, low_ref, high_ref, after_ref, out_ref, first_ref, second_ref, flat, flat_low, flat_high):
    for part in range(PARTS):
        flat[part * LINES : part * LINES + LINES] = own_ref[part, 0:LINES]
    for part in range(3):
        flat_low[part * LINES + 4 : part * LINES + 4 + LINES] = low_ref[part, 0:LINES]
        flat_high[part * LINES : part * LINES + LINES] = high_ref[part, 0:LINES]
    has_low, has_high = flag(place_ref, 0, 24), flag(place_ref, 1, 24)
    even = flag(place_ref, 4)

    def own(row):
        return flat[row * 24 : row * 24 + 24]

    def low(row):
        at = (row - 13) * 24 + 16
        return jnp.where(has_low, flat_low[at : at + 24], 0.0)

    def high(row):
        return jnp.where(has_high, flat_high[row * 24 : row * 24 + 24], 0.0)

    for row in range(26):
        if row < 3:
            value = low(row + 13)
        elif row < 5:
            value = low(row + 13) + jnp.where(has_low, own(row - 3), 0.0)
        elif row < 7:
            value = low(row + 13) + own(row - 3)
        elif row < 19:
            value = own(row - 3)
        elif row < 21:
            value = own(row - 3) + high(row - 19)
        elif row < 23:
            value = jnp.where(has_high, own(row - 3), 0.0) + high(row - 19)
        else:
            value = high(row - 19)
        out_ref[row] = value
        up = pltpu.roll(value, 24 - 11, 0)[0:8]
        down = pltpu.roll(value, 2, 0)[0:8]
        first_ref[row] = jnp.where(even, up, down)
        second_ref[row] = jnp.where(even, down, up)


def radial_assembly(place, own, low, high, after):
    shape = jax.ShapeDtypeStruct
    return pl.pallas_call(
        radial_kernel,
        out_shape=(
            shape((26, 24, LANES), jnp.float32),
            shape((26, 8, LANES), jnp.float32),
            shape((26, 8, LANES), jnp.float32),
        ),
        in_specs=[VMEM] * 4 + [ANY],
        out_specs=[VMEM] * 3,
        scratch_shapes=[
            pltpu.VMEM((480, LANES), jnp.float32),
            pltpu.VMEM((192, LANES), jnp.float32),
            pltpu.VMEM((184, LANES), jnp.float32),
        ],
        compiler_params=params(),
        cost_estimate=cost(0.6),
        name="radial_assembly",
    )(place, own, low, high, after)


def relax_kernel(place_ref, rows_ref, second_ref, first_ref, *rest):
    whole_ref, out_ref, following_hbm, source, even, odd, sem = rest
    copy = pltpu.make_async_copy(whole_ref, following_hbm, sem)
    copy.start()
    has_low, has_high, even_span = (flag(place_ref, number) for number in (2, 3, 4))
    open_low, open_high = flag(place_ref, 0, 32), flag(place_ref, 1, 32)
    sublane = lax.broadcasted_iota(jnp.int32, (8, LANES), 0)
    always = sublane >= 0
    inside = jnp.concatenate(
        [jnp.where(part, 1.0, 0.0) for part in (always, always, has_high, has_low)], axis=0
    )
    modes = place_ref[0:12]
    weights = [
        inside * jnp.broadcast_to(modes[2 * j : 2 * j + 1], (32, LANES)) for j in range(6)
    ]
    keeps = [jnp.broadcast_to(modes[2 * j + 1 : 2 * j + 2], (32, LANES)) for j in range(6)]
    pad = jnp.zeros((24, LANES), jnp.float32)
    for row in range(26):
        own = rows_ref[row]
        tail = own[16:24]
        own = jnp.concatenate(
            [own[0:16], jnp.where(sublane < 2, tail, 0.0), jnp.where(sublane >= 6, tail, 0.0)], axis=0
        )
        first, other = first_ref[row], second_ref[row]
        low = jnp.where(has_low, jnp.where(even_span, other, first), 0.0)
        high = jnp.where(has_high, jnp.where(even_span, first, other), 0.0)
        low = jnp.concatenate([low, pad], axis=0)
        high = jnp.concatenate([high, pad], axis=0)
        value = own + pltpu.roll(low, 27, 0) + pltpu.roll(high, 14, 0)
        source[row] = value
        value = value * weights[0]
        if row < 5:
            value = jnp.where(open_low, value, 0.0)
        elif row > 20:
            value = jnp.where(open_high, value, 0.0)
        even[row] = value

    old, new = even, odd
    for sweep in range(1, 6):
        weight, keep = weights[sweep], keeps[sweep]
        for row in range(sweep, 26 - sweep):
            middle = old[row]
            beside = (old[row - 1] + old[row + 1]) + (pltpu.roll(middle, 1, 0) + pltpu.roll(middle, 31, 0))
            value = keep * middle + weight * (source[row] + beside)
            if sweep == 5:
                out_ref[row - 5] = value[0:16]
            elif row < 5:
                new[row] = jnp.where(open_low, value, 0.0)
            elif row > 20:
                new[row] = jnp.where(open_high, value, 0.0)
            else:
                new[row] = value
        old, new = new, old
    copy.wait()


def relaxation(place, rows, low, high, whole):
    shape = jax.ShapeDtypeStruct
    return pl.pallas_call(
        relax_kernel,
        out_shape=(
            shape((BLOCK, BLOCK, LANES), jnp.float32),
            shape((6, BLOCK, BLOCK, LANES), jnp.float32),
        ),
        in_specs=[VMEM] * 5,
        out_specs=(VMEM, HBM),
        scratch_shapes=[pltpu.VMEM((26, 32, LANES), jnp.float32)] * 3 + [pltpu.SemaphoreType.DMA],
        compiler_params=params(),
        cost_estimate=cost(1.8),
        name="relaxation",
    )(place, rows, low, high, whole)


def weno(positive, p):
    p0 = jnp.where(positive, p[0], p[4])
    p1 = jnp.where(positive, p[1], p[3])
    p2 = p[2]
    p3 = jnp.where(positive, p[3], p[1])
    k1 = (0.609375 * p1) * p1 + 0.75 * EPSILON
    k2 = (0.609375 * p2) * p2 + 0.75 * EPSILON
    r0 = p0 - 1.375 * p1
    r1 = p1 - 0.625 * p2
    r2 = p3 - 1.375 * p2
    q0, q1, q2 = r0 * r0 + k1, r1 * r1 + k2, r2 * r2 + k2
    q01, q02, q12 = q0 * q1, q0 * q2, q1 * q2
    w0, w1, w2 = q12 * q12, 6.0 * (q02 * q02), 3.0 * (q01 * q01)
    middle = p1 - p2
    t0 = (p0 - p1) - middle
    t2 = middle - (p2 - p3)
    total = (w0 + w1) + w2
    guess = pl_reciprocal(total, approx=True)
    inverse = guess * (2.0 - total * guess)
    return ((w0 + w0) * t0 + w2 * t2) * inverse - p1


pl_reciprocal = pltpu.reciprocal


def wind(velocity_ref, direction, row):
    speed = velocity_ref[direction, row]
    positive = speed > 0
    straight = TIME_STEP * speed
    bent = (TIME_STEP / 6) * jnp.abs(speed)
    return positive, straight, bent, jnp.where(positive, 1.0 / 3, 2.0 / 3)


def advected(blow, behind, p):
    positive, straight, bent, side = blow
    return straight * (behind - side * p[2]) + bent * weno(positive, p)


def stream_kernel(psi_ref, velocity_ref, left_ref, right_ref, *rest):
    out_ref, ahead = rest[-2:]
    spread = []
    for comp in range(6):
        ends = jnp.concatenate([right_ref[comp * 4 : comp * 4 + 4], left_ref[comp * 4 : comp * 4 + 4]], axis=0)
        spread += pieces(ends, 3)
    spread = jnp.concatenate([v.astype(jnp.float32) for v in spread], axis=0)
    spread = jnp.transpose(spread).astype(jnp.bfloat16)
    for comp in range(6):
        pairs = []
        for piece in range(3):
            start = comp * 24 + piece * 8
            pairs += [(start, start + 2, -start), (start + 4, start + 6, 121 - start)]
        found = jnp.dot(spread, selection((144, LANES), pairs), preferred_element_type=jnp.float32)
        ahead[comp] = found.reshape(BLOCK, BLOCK, LANES)
    lane = lax.broadcasted_iota(jnp.int32, (BLOCK, LANES), 1)

    def step(row, carry):
        blow = wind(velocity_ref, 0, row)
        for comp in range(6):
            psi = psi_ref[comp, row]
            far = ahead[comp, row]
            lines = []
            for j in range(-3, 4):
                if j > 0:
                    mixed = jnp.where(lane < j, far, psi)
                else:
                    mixed = jnp.where(lane >= LANES + j, far, psi)
                lines.append(pltpu.roll(mixed, (-j) % LANES, 1) if j else psi)
            steps = [lines[j + 1] - lines[j] for j in range(6)]
            change = advected(blow, steps[2], [steps[j] - steps[j + 1] for j in range(5)])
            out_ref[comp, row] = psi - change
        return carry

    lax.fori_loop(0, BLOCK, step, 0, unroll=STEP_UNROLL)


def span_kernel(place_ref, psi_ref, velocity_ref, base_ref, first_ref, second_ref, *rest):
    out_ref, column, second = rest[-3:]
    has_down, has_up, even = (flag(place_ref, number, BLOCK) for number in (2, 3, 4))
    for comp in range(6):
        for near in range(3):
            first, other = first_ref[comp, near], second_ref[comp, near]
            column[comp, :, 5 + near] = jnp.where(has_down, jnp.where(even, other, first), 0.0)
            column[comp, :, 24 + near] = jnp.where(has_up, jnp.where(even, first, other), 0.0)

    def bend(row, carry):
        for comp in range(6):
            column[comp, row, 8:24] = psi_ref[comp, row]
            one, two, three = column[comp, row, 5:25], column[comp, row, 6:26], column[comp, row, 7:27]
            second[comp, row, 5:25] = (two - one) - (three - two)
        return carry

    lax.fori_loop(0, BLOCK, bend, 0)

    def step(row, carry):
        blow = wind(velocity_ref, 2, row)
        for comp in range(6):
            behind = psi_ref[comp, row] - column[comp, row, 7:23]
            change = advected(blow, behind, [second[comp, row, 5 + j : 21 + j] for j in range(5)])
            out_ref[comp, row] = base_ref[comp, row] - change
        return carry

    lax.fori_loop(0, BLOCK, step, 0, unroll=STEP_UNROLL)


def radial_kernel_step(place_ref, psi_ref, velocity_ref, base_ref, low_ref, high_ref, *rest):
    out_ref, column, second = rest[-3:]
    has_low, has_high = flag(place_ref, 0, BLOCK), flag(place_ref, 1, BLOCK)
    for comp in range(6):
        for near in range(3):
            column[comp, near] = jnp.where(has_low, low_ref[comp, near], 0.0)
            column[comp, 19 + near] = jnp.where(has_high, high_ref[comp, near], 0.0)

    def copy_in(row, carry):
        for comp in range(6):
            column[comp, row + 3] = psi_ref[comp, row]
        return carry

    lax.fori_loop(0, BLOCK, copy_in, 0)

    def bend(row, carry):
        for comp in range(6):
            one, two, three = column[comp, row], column[comp, row + 1], column[comp, row + 2]
            second[comp, row] = (two - one) - (three - two)
        return carry

    lax.fori_loop(0, 20, bend, 0)

    def step(row, carry):
        blow = wind(velocity_ref, 1, row)
        tensor = [psi_ref[comp, row] for comp in range(6)]
        grown = sym_exp(tensor)
        peterlin = spring(grown)
        shrunk = sym_inverse(grown, tensor)
        for comp in range(6):
            back = shrunk[comp] - peterlin if DIAG[comp] else shrunk[comp]
            behind = tensor[comp] - column[comp, row + 2]
            change = advected(blow, behind, [second[comp, row + j] for j in range(5)])
            out_ref[comp, row] = (base_ref[comp, row] + (TIME_STEP / WEISSENBERG) * back) - change
        return carry

    lax.fori_loop(0, BLOCK, step, 0, unroll=STEP_UNROLL)


STEP_UNROLL = 2


def advect(kernel, name, scratch, arrays, after):
    return pl.pallas_call(
        kernel,
        out_shape=jax.ShapeDtypeStruct(FULL, jnp.float32),
        in_specs=[VMEM] * len(arrays) + [ANY] * len(after),
        out_specs=VMEM,
        scratch_shapes=[pltpu.VMEM(shape, jnp.float32) for shape in scratch],
        compiler_params=params(),
        cost_estimate=cost(2.5),
        name=name,
    )(*arrays, *after)


def ring(axis, step):
    count = lax.axis_size(axis)
    return [(i, (i + step) % count) for i in range(count)]


def exchange(to_next, to_previous, axis):
    return (
        lax.ppermute(to_next, axis, ring(axis, 1)),
        lax.ppermute(to_previous, axis, ring(axis, -1)),
    )


def trade(first, second, axis):
    count = lax.axis_size(axis)
    inner = [(i, i ^ 1) for i in range(count)]
    outer = [(i, (i - 1) % count if i % 2 == 0 else (i + 1) % count) for i in range(count)]
    second = lax.ppermute(second, axis, outer)
    return lax.ppermute(first, axis, inner), second


def shards(psi, velocity):
    number = (lax.axis_index("stream") * 8 + lax.axis_index("radial")) * 4 + lax.axis_index("span")
    place = lax.dynamic_index_in_dim(jnp.asarray(PLACES), number, 0, keepdims=False)
    wide = (6, BLOCK, 32, LANES)
    tall = [(6, 22, BLOCK, LANES), (6, 20, BLOCK, LANES)]
    send = local_source(psi)
    later, send = lax.optimization_barrier((psi, send))
    lines = lax.all_to_all(send, "stream", split_axis=0, concat_axis=0, tiled=True)
    to_left, to_right, to_first, to_second, to_high, to_low = messages(place, later)
    ends = exchange(to_right, to_left, "stream")
    sides = trade(to_first, to_second, "span")
    spectrum = transform(lines, (to_left,))
    own = lax.all_to_all(spectrum, "stream", split_axis=0, concat_axis=0, tiled=True)
    state = advect(stream_kernel, "advect_stream", [FULL], (psi, velocity) + ends, (spectrum,))
    below, above = exchange(own[5:], own[:3], "radial")
    to_high, to_low = lax.optimization_barrier((to_high, to_low, spectrum))[:2]
    walls = exchange(to_high, to_low, "radial")
    state = advect(span_kernel, "advect_span", [wide, wide], (place, psi, velocity, state) + sides, (own,))
    rows, rows_first, rows_second = radial_assembly(place, own, below, above, state)
    first, second = trade(rows_first, rows_second, "span")
    state = advect(radial_kernel_step, "advect_radial", tall, (place, psi, velocity, state) + walls, (rows,))
    modes, following = relaxation(place, rows, second, first, state)
    return following, modes


def solution(mesh):
    return jax.shard_map(
        shards,
        mesh=mesh,
        in_specs=(P(None, "radial", "span", "stream"), P(None, "radial", "span", "stream")),
        out_specs=(P(None, "radial", "span", "stream"), P("radial", "span", "stream")),
        check_vma=False,
    )
```

```python
import functools
import math

import jax
import jax.numpy as jnp
import ml_dtypes
import numpy as np
from jax import lax
from jax.experimental import pallas as pl
from jax.experimental.pallas import tpu as pltpu
from jax.sharding import PartitionSpec as P

NX = 1024
LANES = 128
BLOCK = 16
PARTS = 8
FULL = (6, BLOCK, BLOCK, LANES)
LINES = 60
ROWS = 64

WEISSENBERG = 20.0
EXTENSIBILITY = 100.0
TIME_STEP = 2.0
EPSILON = 1e-06
COSINES = tuple((math.cos((2 * number + 1) * math.pi / 12.0) for number in range(6)))
VMEM_LIMIT = 16 * 1024 * 1024
SOURCE_VMEM = 62 * 1024 * 1024


def split_bf16(table):
    high = table.astype(np.float32).astype(ml_dtypes.bfloat16)
    low = (table - high.astype(np.float64)).astype(np.float32).astype(ml_dtypes.bfloat16)
    return high, low


def tables():
    ordinal = np.arange(NX)
    wave = np.where(ordinal <= NX // 2, ordinal, ordinal - NX // 2)
    angle = 2.0 * np.pi / NX * ((ordinal[:, None] * wave[None, :]) % NX)
    fourier = -np.where((ordinal <= NX // 2)[None, :], np.cos(angle), np.sin(angle)) * NX**-0.5
    return split_bf16(fourier[:LANES])


def mode_table():
    ordinal = np.arange(NX)
    wave = np.where(ordinal <= NX // 2, ordinal, ordinal - NX // 2)
    diagonal = 4.0 + 4.0 * np.sin(np.pi * wave / NX) ** 2
    ratio = 4.0 / diagonal
    upper = 1.0 + ratio
    lower = np.maximum(0.3, 1.0 - ratio)
    rows = []
    for cosine in COSINES:
        omega = 1.0 / (0.5 * (upper + lower) + 0.5 * (upper - lower) * cosine)
        rows += [omega / diagonal, 1.0 - omega]
    rows += [np.zeros(NX)] * 4
    return np.stack(rows).astype(np.float32).reshape(16, PARTS, LANES).transpose(1, 0, 2)


def flag(place_ref, number, rows=8):
    return jnp.broadcast_to(place_ref[number : number + 1], (rows, LANES)) > 0.5


TABLE = tables()
MODES = mode_table()


def params(limit=VMEM_LIMIT):
    return pltpu.CompilerParams(vmem_limit_bytes=limit)


def cost(microseconds):
    return pl.CostEstimate(
        flops=int(microseconds * 1.1e9), bytes_accessed=int(microseconds * 3.6e6), transcendentals=0
    )


VMEM = pl.BlockSpec(memory_space=pltpu.VMEM)
SMEM = pl.BlockSpec(memory_space=pltpu.SMEM)
HBM = pl.BlockSpec(memory_space=pltpu.HBM)
ANY = pl.BlockSpec(memory_space=pl.ANY)


def dot_nt(left, right):
    return lax.dot_general(left, right, (((1,), (1,)), ((), ())), preferred_element_type=jnp.float32)


def dot_tn(left, right):
    return lax.dot_general(left, right, (((0,), (0,)), ((), ())), preferred_element_type=jnp.float32)


def pieces(value, count):
    found = []
    for _ in range(count):
        found.append(value.astype(jnp.bfloat16))
        value = value - found[-1].astype(jnp.float32)
    return found


def selection(shape, pairs):
    row = lax.broadcasted_iota(jnp.int32, shape, 0)
    column = lax.broadcasted_iota(jnp.int32, shape, 1)
    hit = None
    for first, last, shift in pairs:
        here = (row >= first) & (row <= last) & (column == row + shift)
        hit = here if hit is None else hit | here
    return jnp.where(hit, 1.0, 0.0).astype(jnp.bfloat16)


def sym_square(m):
    a, b, c, d, e, f = m
    bb, cc, ee = b * b, c * c, e * e
    return [
        a * a + bb + cc,
        b * (a + d) + c * e,
        c * (a + f) + b * e,
        bb + d * d + ee,
        e * (d + f) + b * c,
        cc + ee + f * f,
    ]


def sym_times(m, n):
    a, b, c, d, e, f = m
    p, q, r, s, t, u = n
    return [
        a * p + b * q + c * r,
        a * q + b * s + c * t,
        a * r + b * t + c * u,
        b * q + d * s + e * t,
        b * r + d * t + e * u,
        c * r + e * t + f * u,
    ]


DIAG = (1.0, 0.0, 0.0, 1.0, 0.0, 1.0)


def with_diag(m, value):
    return [m[i] + value if DIAG[i] else m[i] for i in range(6)]


def sym_exp(psi):
    m = [0.125 * v for v in psi]
    m2 = sym_square(m)
    m3 = sym_times(m, m2)
    tail = [m[i] * (1.0 / 24) + m2[i] * (1.0 / 120) + m3[i] * (1.0 / 720) for i in range(6)]
    tail = sym_times(m3, with_diag(tail, 1.0 / 6))
    out = with_diag([m[i] + 0.5 * m2[i] + tail[i] for i in range(6)], 1.0)
    for _ in range(3):
        out = sym_square(out)
    return out


def sym_inverse(grown, psi):
    a, b, c, d, e, f = grown
    scale = jnp.exp(-(psi[0] + psi[3] + psi[5]))
    return [
        (d * f - e * e) * scale,
        (c * e - b * f) * scale,
        (b * e - c * d) * scale,
        (a * f - c * c) * scale,
        (b * c - a * e) * scale,
        (a * d - b * b) * scale,
    ]


def spring(grown):
    return (EXTENSIBILITY - 3.0) / (EXTENSIBILITY - (grown[0] + grown[3] + grown[5]))


def source_kernel(psi_hbm, send_ref, psi_ref, stress, field, wrapped, sems):
    chunk = BLOCK // SOURCE_CHUNKS
    arrivals = []
    for part in range(SOURCE_CHUNKS):
        rows = pl.ds(part * chunk, chunk)
        arrivals.append(pltpu.make_async_copy(psi_hbm.at[:, rows], psi_ref.at[:, rows], sems.at[part]))
        arrivals[-1].start()
    zero = jnp.zeros((24, LANES), jnp.float32)
    for comp in (1, 3, 4):
        for row in (0, 1, 2, 3, 20, 21, 22, 23):
            stress[comp, row] = zero

    def relax_row(row, carry):
        psi = [psi_ref[comp, row] for comp in range(6)]
        grown = sym_exp(psi)
        peterlin = spring(grown)
        pad = jnp.zeros((8, LANES), jnp.float32)
        for comp in range(6):
            value = peterlin * grown[comp]
            stress[comp, row + 4, 0:16] = value - 1.0 if DIAG[comp] else value
            stress[comp, row + 4, 16:24] = pad
        return carry

    for part in range(SOURCE_CHUNKS):
        arrivals[part].wait()
        lax.fori_loop(part * chunk, part * chunk + chunk, relax_row, 0, unroll=EXP_UNROLL)

    lane = lax.broadcasted_iota(jnp.int32, (24, LANES), 1)
    inner = [lane < LANES - 1, lane >= 1, lane < LANES - 2, lane >= 2]

    def along(value, shift):
        return pltpu.roll(value, shift % 24, 0)

    def shifted(value, shift):
        return pltpu.roll(value, shift % LANES, 1)

    def emit(row, plain, once, twice):
        parts = [shifted(once, -1), -shifted(once, 1), shifted(twice, -2), shifted(twice, 2)]
        total = plain - 2.0 * twice
        beyond = zero
        for part, mask in zip(parts, inner):
            kept = jnp.where(mask, part, 0.0)
            total = total + kept
            beyond = beyond + (part - kept)
        at = row * 24 if isinstance(row, int) else pl.multiple_of(row * 24, 8)
        field[pl.ds(at, 24)] = total
        wrapped[pl.ds(at, 24)] = beyond

    def body(row, carry):
        here = row + 2
        s11 = 0.25 * (stress[3, here + 2] - 2.0 * stress[3, here] + stress[3, here - 2])
        u12 = 0.5 * (stress[4, here + 1] - stress[4, here - 1])
        u01 = 0.5 * (stress[1, here + 1] - stress[1, here - 1])
        s22, s02, s00 = stress[5, here], stress[2, here], stress[0, here]
        c22 = 0.25 * (along(s22, -2) - 2.0 * s22 + along(s22, 2))
        c12 = along(u12, -1) - along(u12, 1)
        c02 = 0.5 * (along(s02, -1) - along(s02, 1))
        emit(row, s11 + c22 + c12, u01 + c02, 0.25 * s00)
        return carry

    lax.fori_loop(2, 18, body, 0, unroll=SOURCE_UNROLL)
    for row in (0, 1, 18, 19):
        here = row + 2
        other = here + 2 if row < 2 else here - 2
        s11 = 0.25 * stress[3, other]
        if row in (1, 18):
            near = here + 1 if row == 1 else here - 1
            sign = 0.5 if row == 1 else -0.5
            u12 = sign * stress[4, near]
            u01 = sign * stress[1, near]
            emit(row, s11 + along(u12, -1) - along(u12, 1), u01, zero)
        else:
            emit(row, s11, zero, zero)
    wrapped[480:488] = jnp.zeros((8, LANES), jnp.float32)
    pick = selection((8, 2 * LANES), ((0, 1, 126), (2, 3, -2)))
    pick = pick + selection((8, 2 * LANES), ((0, 1, 126 + LANES), (2, 3, LANES - 2)))
    for part in range(PARTS):
        send_ref[part, 0:LINES] = field[part * LINES : part * LINES + LINES]
        lines = jnp.concatenate(pieces(wrapped[part * LINES : part * LINES + ROWS], 2), axis=1)
        lines = dot_nt(pick, lines)
        send_ref[part, LINES:ROWS, 0:ROWS] = lines[0:4]
        send_ref[part, LINES:ROWS, ROWS:LANES] = jnp.zeros((4, LANES - ROWS), jnp.float32)


EXP_UNROLL = 2
SOURCE_CHUNKS = 4
SOURCE_UNROLL = 8


def local_source(psi):
    shape = jax.ShapeDtypeStruct
    return pl.pallas_call(
        source_kernel,
        out_shape=shape((PARTS, ROWS, LANES), jnp.float32),
        in_specs=[HBM],
        out_specs=VMEM,
        scratch_shapes=[
            pltpu.VMEM(FULL, jnp.float32),
            pltpu.VMEM((6, 24, 24, LANES), jnp.float32),
            pltpu.VMEM((480, LANES), jnp.float32),
            pltpu.VMEM((488, LANES), jnp.float32),
            pltpu.SemaphoreType.DMA((SOURCE_CHUNKS,)),
        ],
        compiler_params=params(SOURCE_VMEM),
        cost_estimate=cost(3.0),
        name="local_source",
    )(psi)


def message_kernel(place_ref, psi_ref, left_ref, right_ref, first_ref, second_ref, high_ref, low_ref):
    even = flag(place_ref, 4, BLOCK)
    ends = sum(
        (selection((8, 3 * LANES), ((0, 2, k * LANES), (4, 6, k * LANES + 121))) for k in range(1, 3)),
        selection((8, 3 * LANES), ((0, 2, 0), (4, 6, 121))),
    )
    for comp in range(6):
        lines = jnp.concatenate(pieces(psi_ref[comp].reshape(BLOCK * BLOCK, LANES), 3), axis=1)
        found = dot_nt(ends, lines)
        left_ref[comp * 4 : comp * 4 + 4] = found[0:4]
        right_ref[comp * 4 : comp * 4 + 4] = found[4:8]
        for near in range(3):
            down = psi_ref[comp, :, near]
            up = psi_ref[comp, :, BLOCK - 3 + near]
            first_ref[comp, near] = jnp.where(even, up, down)
            second_ref[comp, near] = jnp.where(even, down, up)
            low_ref[comp, near] = psi_ref[comp, near]
            high_ref[comp, near] = psi_ref[comp, BLOCK - 3 + near]


def messages(place, psi):
    shape = jax.ShapeDtypeStruct
    return pl.pallas_call(
        message_kernel,
        out_shape=[shape((24, BLOCK * BLOCK), jnp.float32)] * 2
        + [shape((6, 3, BLOCK, LANES), jnp.float32)] * 4,
        in_specs=[VMEM, VMEM],
        out_specs=[VMEM] * 6,
        compiler_params=params(),
        cost_estimate=cost(4.0),
        name="messages",
    )(place, psi)


def transform_kernel(lines_ref, high_ref, low_ref, *rest):
    out_ref = rest[-1]
    edges = jnp.concatenate([lines_ref[part, LINES:ROWS] for part in range(PARTS)], axis=0)
    edges = jnp.concatenate(pieces(jnp.transpose(edges)[0:ROWS], 2), axis=1)
    row = lax.broadcasted_iota(jnp.int32, (8 * PARTS, NX), 0) & (4 * PARTS - 1)
    lane = lax.broadcasted_iota(jnp.int32, (8 * PARTS, NX), 1)
    offset = jnp.where((row & 3) < 2, (row & 3) - 2, (row & 3) + LANES - 2)
    target = ((row >> 2) * LANES + offset + NX) & (NX - 1)
    target = jnp.where(lane == target, 1.0, 0.0).astype(jnp.bfloat16)
    beyond = jnp.dot(edges, target, preferred_element_type=jnp.float32)
    f = [lines_ref[part] + beyond[:, part * LANES : (part + 1) * LANES] for part in range(PARTS)]
    s = [f[k] + f[k + 4] for k in range(4)]
    o = [f[k] - f[k + 4] for k in range(4)]
    half = math.sqrt(0.5)
    p0, p1, q0, q1 = s[0] + s[2], s[1] + s[3], s[0] - s[2], s[1] - s[3]
    minus, plus = half * (o[1] - o[3]), half * (o[1] + o[3])
    left = [p0 + p1, p0 - p1, q0, o[0] + minus, o[0] - minus, q1, plus + o[2], plus - o[2]]
    high, low = pieces(jnp.concatenate(left, axis=0), 2)
    both = jnp.concatenate([high, low], axis=1)
    wide = 2 * LANES
    found = []
    for part in range(4):
        cols = slice(part * wide, (part + 1) * wide)
        table = jnp.concatenate([high_ref[:, cols]] * 2, axis=0)
        first = jnp.dot(both, table, preferred_element_type=jnp.float32)
        second = jnp.dot(high, low_ref[:, cols], preferred_element_type=jnp.float32)
        found.append([first[k * ROWS : (k + 1) * ROWS] + second[k * ROWS : (k + 1) * ROWS] for k in range(8)])
    phase = lax.broadcasted_iota(jnp.int32, (ROWS, wide), 1) % 8
    outer = (phase == 1) | (phase == 7)
    middle = phase % 4 == 2
    turn = jnp.where(phase % 4 == 0, 0.0, jnp.where(phase < 4, 1.0, -1.0))
    for part in range(4):
        here, there = found[part], found[(part + 2) % 4]
        straight = jnp.where(middle, here[2], jnp.where(outer, here[3], here[4]))
        straight = jnp.where(phase == 0, here[0], jnp.where(phase == 4, here[1], straight))
        crossed = turn * jnp.where(middle, there[5], jnp.where(outer, there[6], there[7]))
        total = straight - crossed if part < 2 else straight + crossed
        out_ref[2 * part] = total[:, 0:LANES]
        out_ref[2 * part + 1] = total[:, LANES:]


def transform(lines, after):
    return pl.pallas_call(
        transform_kernel,
        out_shape=jax.ShapeDtypeStruct((PARTS, ROWS, LANES), jnp.float32),
        in_specs=[VMEM] * 3 + [ANY] * len(after),
        out_specs=VMEM,
        compiler_params=params(),
        cost_estimate=cost(1.5),
        name="transform",
    )(lines, *(jnp.asarray(table) for table in TABLE), *after)


def radial_message_kernel(own_ref, up_ref, down_ref):
    def copy(to, at, line, count):
        while count:
            part, row = divmod(line, LINES)
            some = min(count, LINES - row)
            to[at : at + some] = own_ref[part, row : row + some]
            at, line, count = at + some, line + some, count - some

    for k in range(7):
        for to, row in ((down_ref, k), (up_ref, k + 13)):
            copy(to, k * 20, row * 24, 18)
            copy(to, k * 20 + 18, row * 24 + 22, 2)
    for to in (down_ref, up_ref):
        to[140:144] = jnp.zeros((4, LANES), jnp.float32)


def radial_messages(own):
    return pl.pallas_call(
        radial_message_kernel,
        out_shape=[jax.ShapeDtypeStruct((144, LANES), jnp.float32)] * 2,
        in_specs=[VMEM],
        out_specs=[VMEM] * 2,
        compiler_params=params(),
        cost_estimate=cost(0.3),
        name="radial_messages",
    )(own)


def radial_kernel(place_ref, own_ref, low_ref, high_ref, after_ref, out_ref, first_ref, second_ref, flat, flat_low, flat_high):
    for part in range(PARTS):
        flat[part * LINES : part * LINES + LINES] = own_ref[part, 0:LINES]
    flat_low[...] = jnp.zeros_like(flat_low)
    flat_high[...] = jnp.zeros_like(flat_high)
    for k in range(7):
        for to, message in ((flat_low, low_ref), (flat_high, high_ref)):
            to[k * 24 : k * 24 + 18] = message[k * 20 : k * 20 + 18]
            to[k * 24 + 22 : k * 24 + 24] = message[k * 20 + 18 : k * 20 + 20]
    has_low, has_high = flag(place_ref, 0, 24), flag(place_ref, 1, 24)
    even = flag(place_ref, 4)

    def own(row):
        return flat[row * 24 : row * 24 + 24]

    def low(row):
        at = (row - 13) * 24
        return jnp.where(has_low, flat_low[at : at + 24], 0.0)

    def high(row):
        return jnp.where(has_high, flat_high[row * 24 : row * 24 + 24], 0.0)

    for row in range(26):
        if row < 3:
            value = low(row + 13)
        elif row < 5:
            value = low(row + 13) + jnp.where(has_low, own(row - 3), 0.0)
        elif row < 7:
            value = low(row + 13) + own(row - 3)
        elif row < 19:
            value = own(row - 3)
        elif row < 21:
            value = own(row - 3) + high(row - 19)
        elif row < 23:
            value = jnp.where(has_high, own(row - 3), 0.0) + high(row - 19)
        else:
            value = high(row - 19)
        out_ref[row] = value
        up = pltpu.roll(value, 24 - 11, 0)[0:8]
        down = pltpu.roll(value, 2, 0)[0:8]
        first_ref[row] = jnp.where(even, up, down)
        second_ref[row] = jnp.where(even, down, up)


def radial_assembly(place, own, low, high, after):
    shape = jax.ShapeDtypeStruct
    return pl.pallas_call(
        radial_kernel,
        out_shape=(
            shape((26, 24, LANES), jnp.float32),
            shape((26, 8, LANES), jnp.float32),
            shape((26, 8, LANES), jnp.float32),
        ),
        in_specs=[VMEM] * 4 + [ANY],
        out_specs=[VMEM] * 3,
        scratch_shapes=[
            pltpu.VMEM((480, LANES), jnp.float32),
            pltpu.VMEM((168, LANES), jnp.float32),
            pltpu.VMEM((168, LANES), jnp.float32),
        ],
        compiler_params=params(),
        cost_estimate=cost(0.6),
        name="radial_assembly",
    )(place, own, low, high, after)


def relax_kernel(place_ref, modes_ref, rows_ref, second_ref, first_ref, *rest):
    whole_ref, out_ref, following_hbm, source, even, odd, sem = rest
    copy = pltpu.make_async_copy(whole_ref, following_hbm, sem)
    copy.start()
    has_low, has_high, even_span = (flag(place_ref, number) for number in (2, 3, 4))
    open_low, open_high = flag(place_ref, 0, 32), flag(place_ref, 1, 32)
    sublane = lax.broadcasted_iota(jnp.int32, (8, LANES), 0)
    always = sublane >= 0
    inside = jnp.concatenate(
        [jnp.where(part, 1.0, 0.0) for part in (always, always, has_high, has_low)], axis=0
    )
    modes = sum(modes_ref[k] * jnp.broadcast_to(place_ref[8 + k : 9 + k], (16, LANES)) for k in range(PARTS))
    weights = [
        inside * jnp.broadcast_to(modes[2 * j : 2 * j + 1], (32, LANES)) for j in range(6)
    ]
    keeps = [jnp.broadcast_to(modes[2 * j + 1 : 2 * j + 2], (32, LANES)) for j in range(6)]
    pad = jnp.zeros((24, LANES), jnp.float32)
    for row in range(26):
        own = rows_ref[row]
        tail = own[16:24]
        own = jnp.concatenate(
            [own[0:16], jnp.where(sublane < 2, tail, 0.0), jnp.where(sublane >= 6, tail, 0.0)], axis=0
        )
        first, other = first_ref[row], second_ref[row]
        low = jnp.where(has_low, jnp.where(even_span, other, first), 0.0)
        high = jnp.where(has_high, jnp.where(even_span, first, other), 0.0)
        low = jnp.concatenate([low, pad], axis=0)
        high = jnp.concatenate([high, pad], axis=0)
        value = own + pltpu.roll(low, 27, 0) + pltpu.roll(high, 14, 0)
        source[row] = value
        value = value * weights[0]
        if row < 5:
            value = jnp.where(open_low, value, 0.0)
        elif row > 20:
            value = jnp.where(open_high, value, 0.0)
        even[row] = value

    old, new = even, odd
    for sweep in range(1, 6):
        weight, keep = weights[sweep], keeps[sweep]
        for row in range(sweep, 26 - sweep):
            middle = old[row]
            beside = (old[row - 1] + old[row + 1]) + (pltpu.roll(middle, 1, 0) + pltpu.roll(middle, 31, 0))
            value = keep * middle + weight * (source[row] + beside)
            if sweep == 5:
                out_ref[row - 5] = value[0:16]
            elif row < 5:
                new[row] = jnp.where(open_low, value, 0.0)
            elif row > 20:
                new[row] = jnp.where(open_high, value, 0.0)
            else:
                new[row] = value
        old, new = new, old
    copy.wait()


def relaxation(place, rows, low, high, whole):
    shape = jax.ShapeDtypeStruct
    return pl.pallas_call(
        relax_kernel,
        out_shape=(
            shape((BLOCK, BLOCK, LANES), jnp.float32),
            shape((6, BLOCK, BLOCK, LANES), jnp.float32),
        ),
        in_specs=[VMEM] * 6,
        out_specs=(VMEM, HBM),
        scratch_shapes=[pltpu.VMEM((26, 32, LANES), jnp.float32)] * 3 + [pltpu.SemaphoreType.DMA],
        compiler_params=params(),
        cost_estimate=cost(1.8),
        name="relaxation",
    )(place, jnp.asarray(MODES), rows, low, high, whole)


def weno(positive, p):
    p0 = jnp.where(positive, p[0], p[4])
    p1 = jnp.where(positive, p[1], p[3])
    p2 = p[2]
    p3 = jnp.where(positive, p[3], p[1])
    k1 = (0.609375 * p1) * p1 + 0.75 * EPSILON
    k2 = (0.609375 * p2) * p2 + 0.75 * EPSILON
    r0 = p0 - 1.375 * p1
    r1 = p1 - 0.625 * p2
    r2 = p3 - 1.375 * p2
    q0, q1, q2 = r0 * r0 + k1, r1 * r1 + k2, r2 * r2 + k2
    q01, q02, q12 = q0 * q1, q0 * q2, q1 * q2
    w0, w1, w2 = q12 * q12, 6.0 * (q02 * q02), 3.0 * (q01 * q01)
    middle = p1 - p2
    t0 = (p0 - p1) - middle
    t2 = middle - (p2 - p3)
    total = (w0 + w1) + w2
    guess = pl_reciprocal(total, approx=True)
    inverse = guess * (2.0 - total * guess)
    return ((w0 + w0) * t0 + w2 * t2) * inverse - p1


pl_reciprocal = pltpu.reciprocal


def wind(velocity_ref, direction, row):
    speed = velocity_ref[direction, row]
    positive = speed > 0
    straight = TIME_STEP * speed
    bent = (TIME_STEP / 6) * jnp.abs(speed)
    return positive, straight, bent, jnp.where(positive, 1.0 / 3, 2.0 / 3)


def advected(blow, behind, p):
    positive, straight, bent, side = blow
    return straight * (behind - side * p[2]) + bent * weno(positive, p)


def stream_kernel(psi_ref, velocity_ref, left_ref, right_ref, *rest):
    out_ref, ahead = rest[-2:]
    spread = []
    for comp in range(6):
        ends = jnp.concatenate([right_ref[comp * 4 : comp * 4 + 4], left_ref[comp * 4 : comp * 4 + 4]], axis=0)
        spread += pieces(ends, 3)
    spread = jnp.concatenate([v.astype(jnp.float32) for v in spread], axis=0)
    spread = jnp.transpose(spread).astype(jnp.bfloat16)
    place = selection((8, LANES), ((0, 2, 0), (4, 6, 121))).astype(jnp.float32)
    for comp in range(6):
        rows = [place] * 3
        if comp > 0:
            rows = [jnp.zeros((comp * 24, LANES), jnp.float32)] + rows
        if comp < 5:
            rows = rows + [jnp.zeros((120 - comp * 24, LANES), jnp.float32)]
        rows = jnp.concatenate(rows, axis=0).astype(jnp.bfloat16)
        found = jnp.dot(spread, rows, preferred_element_type=jnp.float32)
        ahead[comp] = found.reshape(BLOCK, BLOCK, LANES)
    lane = lax.broadcasted_iota(jnp.int32, (BLOCK, LANES), 1)

    def step(row, carry):
        blow = wind(velocity_ref, 0, row)
        for comp in range(6):
            psi = psi_ref[comp, row]
            far = ahead[comp, row]
            lines = []
            for j in range(-3, 4):
                if j > 0:
                    mixed = jnp.where(lane < j, far, psi)
                else:
                    mixed = jnp.where(lane >= LANES + j, far, psi)
                lines.append(pltpu.roll(mixed, (-j) % LANES, 1) if j else psi)
            steps = [lines[j + 1] - lines[j] for j in range(6)]
            change = advected(blow, steps[2], [steps[j] - steps[j + 1] for j in range(5)])
            out_ref[comp, row] = psi - change
        return carry

    lax.fori_loop(0, BLOCK, step, 0, unroll=STEP_UNROLL)


def span_kernel(place_ref, psi_ref, velocity_ref, base_ref, first_ref, second_ref, *rest):
    out_ref, column, second = rest[-3:]
    has_down, has_up, even = (flag(place_ref, number, BLOCK) for number in (2, 3, 4))
    for comp in range(6):
        for near in range(3):
            first, other = first_ref[comp, near], second_ref[comp, near]
            column[comp, :, 5 + near] = jnp.where(has_down, jnp.where(even, other, first), 0.0)
            column[comp, :, 24 + near] = jnp.where(has_up, jnp.where(even, first, other), 0.0)

    def bend(row, carry):
        for comp in range(6):
            column[comp, row, 8:24] = psi_ref[comp, row]
            one, two, three = column[comp, row, 5:25], column[comp, row, 6:26], column[comp, row, 7:27]
            second[comp, row, 5:25] = (two - one) - (three - two)
        return carry

    lax.fori_loop(0, BLOCK, bend, 0)

    def step(row, carry):
        blow = wind(velocity_ref, 2, row)
        for comp in range(6):
            behind = psi_ref[comp, row] - column[comp, row, 7:23]
            change = advected(blow, behind, [second[comp, row, 5 + j : 21 + j] for j in range(5)])
            out_ref[comp, row] = base_ref[comp, row] - change
        return carry

    lax.fori_loop(0, BLOCK, step, 0, unroll=STEP_UNROLL)


def radial_kernel_step(place_ref, psi_ref, velocity_ref, base_ref, low_ref, high_ref, *rest):
    out_ref, column, second = rest[-3:]
    has_low, has_high = flag(place_ref, 0, BLOCK), flag(place_ref, 1, BLOCK)
    for comp in range(6):
        for near in range(3):
            column[comp, near] = jnp.where(has_low, low_ref[comp, near], 0.0)
            column[comp, 19 + near] = jnp.where(has_high, high_ref[comp, near], 0.0)

    def copy_in(row, carry):
        for comp in range(6):
            column[comp, row + 3] = psi_ref[comp, row]
        return carry

    lax.fori_loop(0, BLOCK, copy_in, 0)

    def bend(row, carry):
        for comp in range(6):
            one, two, three = column[comp, row], column[comp, row + 1], column[comp, row + 2]
            second[comp, row] = (two - one) - (three - two)
        return carry

    lax.fori_loop(0, 20, bend, 0)

    def step(row, carry):
        blow = wind(velocity_ref, 1, row)
        tensor = [psi_ref[comp, row] for comp in range(6)]
        grown = sym_exp(tensor)
        peterlin = spring(grown)
        shrunk = sym_inverse(grown, tensor)
        for comp in range(6):
            back = shrunk[comp] - peterlin if DIAG[comp] else shrunk[comp]
            behind = tensor[comp] - column[comp, row + 2]
            change = advected(blow, behind, [second[comp, row + j] for j in range(5)])
            out_ref[comp, row] = (base_ref[comp, row] + (TIME_STEP / WEISSENBERG) * back) - change
        return carry

    lax.fori_loop(0, BLOCK, step, 0, unroll=STEP_UNROLL)


STEP_UNROLL = 2


def advect(kernel, name, scratch, arrays, after):
    return pl.pallas_call(
        kernel,
        out_shape=jax.ShapeDtypeStruct(FULL, jnp.float32),
        in_specs=[VMEM] * len(arrays) + [ANY] * len(after),
        out_specs=VMEM,
        scratch_shapes=[pltpu.VMEM(shape, jnp.float32) for shape in scratch],
        compiler_params=params(),
        cost_estimate=cost(2.5),
        name=name,
    )(*arrays, *after)


def ring(axis, step):
    count = lax.axis_size(axis)
    return [(i, (i + step) % count) for i in range(count)]


def exchange(to_next, to_previous, axis):
    return (
        lax.ppermute(to_next, axis, ring(axis, 1)),
        lax.ppermute(to_previous, axis, ring(axis, -1)),
    )


def trade(first, second, axis):
    count = lax.axis_size(axis)
    inner = [(i, i ^ 1) for i in range(count)]
    outer = [(i, (i - 1) % count if i % 2 == 0 else (i + 1) % count) for i in range(count)]
    second = lax.ppermute(second, axis, outer)
    return lax.ppermute(first, axis, inner), second


def shards(psi, velocity):
    radial, span = lax.axis_index("radial"), lax.axis_index("span")
    bits = (radial > 0) + 2 * (radial < 7) + 4 * (span > 0) + 8 * (span < 3) + 16 * (span % 2 == 0)
    number = lax.broadcasted_iota(jnp.int32, (16, LANES), 0)
    place = ((bits >> number) & (number < 8)) | (number == lax.axis_index("stream") + 8)
    place = place.astype(jnp.float32)
    wide = (6, BLOCK, 32, LANES)
    tall = [(6, 22, BLOCK, LANES), (6, 20, BLOCK, LANES)]
    send = local_source(psi)
    later, send = lax.optimization_barrier((psi, send))
    lines = lax.all_to_all(send, "stream", split_axis=0, concat_axis=0, tiled=True)
    to_left, to_right, to_first, to_second, to_high, to_low = messages(place, later)
    ends = exchange(to_right, to_left, "stream")
    sides = trade(to_first, to_second, "span")
    spectrum = transform(lines, (to_left,))
    own = lax.all_to_all(spectrum, "stream", split_axis=0, concat_axis=0, tiled=True)
    state = advect(stream_kernel, "advect_stream", [FULL], (psi, velocity) + ends, (spectrum,))
    below, above = exchange(*radial_messages(own), "radial")
    to_high, to_low = lax.optimization_barrier((to_high, to_low, spectrum))[:2]
    walls = exchange(to_high, to_low, "radial")
    state = advect(span_kernel, "advect_span", [wide, wide], (place, psi, velocity, state) + sides, (own,))
    rows, rows_first, rows_second = radial_assembly(place, own, below, above, state)
    first, second = trade(rows_first, rows_second, "span")
    state = advect(radial_kernel_step, "advect_radial", tall, (place, psi, velocity, state) + walls, (rows,))
    pressure, following = relaxation(place, rows, second, first, state)
    return following, pressure


def solution(mesh):
    return jax.shard_map(
        shards,
        mesh=mesh,
        in_specs=(P(None, "radial", "span", "stream"), P(None, "radial", "span", "stream")),
        out_specs=(P(None, "radial", "span", "stream"), P("radial", "span", "stream")),
        check_vma=False,
    )
```

```python
import functools
import math

import jax
import jax.numpy as jnp
import ml_dtypes
import numpy as np
from jax import lax
from jax.experimental import pallas as pl
from jax.experimental.pallas import tpu as pltpu
from jax.sharding import PartitionSpec as P

NX = 1024
LANES = 128
BLOCK = 16
PARTS = 8
FULL = (6, BLOCK, BLOCK, LANES)
LINES = 60
ROWS = 64

WEISSENBERG = 20.0
EXTENSIBILITY = 100.0
TIME_STEP = 2.0
EPSILON = 1e-06
COSINES = tuple((math.cos((2 * number + 1) * math.pi / 12.0) for number in range(6)))
VMEM_LIMIT = 16 * 1024 * 1024
SOURCE_VMEM = 62 * 1024 * 1024


def split_bf16(table):
    high = table.astype(np.float32).astype(ml_dtypes.bfloat16)
    low = (table - high.astype(np.float64)).astype(np.float32).astype(ml_dtypes.bfloat16)
    return high, low


def tables():
    ordinal = np.arange(NX)
    wave = np.where(ordinal <= NX // 2, ordinal, ordinal - NX // 2)
    angle = 2.0 * np.pi / NX * ((ordinal[:, None] * wave[None, :]) % NX)
    fourier = -np.where((ordinal <= NX // 2)[None, :], np.cos(angle), np.sin(angle)) * NX**-0.5
    return split_bf16(fourier[:LANES])


def mode_table():
    ordinal = np.arange(NX)
    wave = np.where(ordinal <= NX // 2, ordinal, ordinal - NX // 2)
    diagonal = 4.0 + 4.0 * np.sin(np.pi * wave / NX) ** 2
    ratio = 4.0 / diagonal
    upper = 1.0 + ratio
    lower = np.maximum(0.3, 1.0 - ratio)
    rows = []
    for cosine in COSINES:
        omega = 1.0 / (0.5 * (upper + lower) + 0.5 * (upper - lower) * cosine)
        rows += [omega / diagonal, 1.0 - omega]
    rows += [np.zeros(NX)] * 4
    return np.stack(rows).astype(np.float32).reshape(16, PARTS, LANES).transpose(1, 0, 2)


def flag(place_ref, number, rows=8):
    return jnp.broadcast_to(place_ref[number : number + 1], (rows, LANES)) > 0.5


TABLE = tables()
MODES = mode_table()


def params(limit=VMEM_LIMIT):
    return pltpu.CompilerParams(vmem_limit_bytes=limit)


def cost(microseconds):
    return pl.CostEstimate(
        flops=int(microseconds * 1.1e9), bytes_accessed=int(microseconds * 3.6e6), transcendentals=0
    )


VMEM = pl.BlockSpec(memory_space=pltpu.VMEM)
SMEM = pl.BlockSpec(memory_space=pltpu.SMEM)
HBM = pl.BlockSpec(memory_space=pltpu.HBM)
ANY = pl.BlockSpec(memory_space=pl.ANY)


def dot_nt(left, right):
    return lax.dot_general(left, right, (((1,), (1,)), ((), ())), preferred_element_type=jnp.float32)


def dot_tn(left, right):
    return lax.dot_general(left, right, (((0,), (0,)), ((), ())), preferred_element_type=jnp.float32)


def pieces(value, count):
    found = []
    for _ in range(count):
        found.append(value.astype(jnp.bfloat16))
        value = value - found[-1].astype(jnp.float32)
    return found


def selection(shape, pairs):
    row = lax.broadcasted_iota(jnp.int32, shape, 0)
    column = lax.broadcasted_iota(jnp.int32, shape, 1)
    hit = None
    for first, last, shift in pairs:
        here = (row >= first) & (row <= last) & (column == row + shift)
        hit = here if hit is None else hit | here
    return jnp.where(hit, 1.0, 0.0).astype(jnp.bfloat16)


def sym_square(m):
    a, b, c, d, e, f = m
    bb, cc, ee = b * b, c * c, e * e
    return [
        a * a + bb + cc,
        b * (a + d) + c * e,
        c * (a + f) + b * e,
        bb + d * d + ee,
        e * (d + f) + b * c,
        cc + ee + f * f,
    ]


def sym_times(m, n):
    a, b, c, d, e, f = m
    p, q, r, s, t, u = n
    return [
        a * p + b * q + c * r,
        a * q + b * s + c * t,
        a * r + b * t + c * u,
        b * q + d * s + e * t,
        b * r + d * t + e * u,
        c * r + e * t + f * u,
    ]


DIAG = (1.0, 0.0, 0.0, 1.0, 0.0, 1.0)


def with_diag(m, value):
    return [m[i] + value if DIAG[i] else m[i] for i in range(6)]


def sym_exp(psi):
    m = [0.125 * v for v in psi]
    m2 = sym_square(m)
    m3 = sym_times(m, m2)
    tail = [m[i] * (1.0 / 24) + m2[i] * (1.0 / 120) + m3[i] * (1.0 / 720) for i in range(6)]
    tail = sym_times(m3, with_diag(tail, 1.0 / 6))
    out = with_diag([m[i] + 0.5 * m2[i] + tail[i] for i in range(6)], 1.0)
    for _ in range(3):
        out = sym_square(out)
    return out


def sym_inverse(grown, psi):
    a, b, c, d, e, f = grown
    scale = jnp.exp(-(psi[0] + psi[3] + psi[5]))
    return [
        (d * f - e * e) * scale,
        (c * e - b * f) * scale,
        (b * e - c * d) * scale,
        (a * f - c * c) * scale,
        (b * c - a * e) * scale,
        (a * d - b * b) * scale,
    ]


def spring(grown):
    return (EXTENSIBILITY - 3.0) / (EXTENSIBILITY - (grown[0] + grown[3] + grown[5]))


def source_kernel(psi_hbm, send_ref, psi_ref, stress, field, wrapped, sems):
    chunk = BLOCK // SOURCE_CHUNKS
    arrivals = []
    for part in range(SOURCE_CHUNKS):
        rows = pl.ds(part * chunk, chunk)
        arrivals.append(pltpu.make_async_copy(psi_hbm.at[:, rows], psi_ref.at[:, rows], sems.at[part]))
        arrivals[-1].start()
    zero = jnp.zeros((24, LANES), jnp.float32)
    for comp in (1, 3, 4):
        for row in (0, 1, 2, 3, 20, 21, 22, 23):
            stress[comp, row] = zero

    def relax_row(row, carry):
        psi = [psi_ref[comp, row] for comp in range(6)]
        grown = sym_exp(psi)
        peterlin = spring(grown)
        pad = jnp.zeros((8, LANES), jnp.float32)
        for comp in range(6):
            value = peterlin * grown[comp]
            stress[comp, row + 4, 0:16] = value - 1.0 if DIAG[comp] else value
            stress[comp, row + 4, 16:24] = pad
        return carry

    for part in range(SOURCE_CHUNKS):
        arrivals[part].wait()
        lax.fori_loop(part * chunk, part * chunk + chunk, relax_row, 0, unroll=EXP_UNROLL)

    lane = lax.broadcasted_iota(jnp.int32, (24, LANES), 1)
    inner = [lane < LANES - 1, lane >= 1, lane < LANES - 2, lane >= 2]

    def along(value, shift):
        return pltpu.roll(value, shift % 24, 0)

    def shifted(value, shift):
        return pltpu.roll(value, shift % LANES, 1)

    def emit(row, plain, once, twice):
        parts = [shifted(once, -1), -shifted(once, 1), shifted(twice, -2), shifted(twice, 2)]
        total = plain - 2.0 * twice
        beyond = zero
        for part, mask in zip(parts, inner):
            kept = jnp.where(mask, part, 0.0)
            total = total + kept
            beyond = beyond + (part - kept)
        at = row * 24 if isinstance(row, int) else pl.multiple_of(row * 24, 8)
        field[pl.ds(at, 24)] = total
        wrapped[pl.ds(at, 24)] = beyond

    def body(row, carry):
        here = row + 2
        s11 = 0.25 * (stress[3, here + 2] - 2.0 * stress[3, here] + stress[3, here - 2])
        u12 = 0.5 * (stress[4, here + 1] - stress[4, here - 1])
        u01 = 0.5 * (stress[1, here + 1] - stress[1, here - 1])
        s22, s02, s00 = stress[5, here], stress[2, here], stress[0, here]
        c22 = 0.25 * (along(s22, -2) - 2.0 * s22 + along(s22, 2))
        c12 = along(u12, -1) - along(u12, 1)
        c02 = 0.5 * (along(s02, -1) - along(s02, 1))
        emit(row, s11 + c22 + c12, u01 + c02, 0.25 * s00)
        return carry

    lax.fori_loop(2, 18, body, 0, unroll=SOURCE_UNROLL)
    for row in (0, 1, 18, 19):
        here = row + 2
        other = here + 2 if row < 2 else here - 2
        s11 = 0.25 * stress[3, other]
        if row in (1, 18):
            near = here + 1 if row == 1 else here - 1
            sign = 0.5 if row == 1 else -0.5
            u12 = sign * stress[4, near]
            u01 = sign * stress[1, near]
            emit(row, s11 + along(u12, -1) - along(u12, 1), u01, zero)
        else:
            emit(row, s11, zero, zero)
    wrapped[480:488] = jnp.zeros((8, LANES), jnp.float32)
    pick = selection((8, 2 * LANES), ((0, 1, 126), (2, 3, -2)))
    pick = pick + selection((8, 2 * LANES), ((0, 1, 126 + LANES), (2, 3, LANES - 2)))
    for part in range(PARTS):
        send_ref[part, 0:LINES] = field[part * LINES : part * LINES + LINES]
        lines = jnp.concatenate(pieces(wrapped[part * LINES : part * LINES + ROWS], 2), axis=1)
        lines = dot_nt(pick, lines)
        send_ref[part, LINES:ROWS, 0:ROWS] = lines[0:4]
        send_ref[part, LINES:ROWS, ROWS:LANES] = jnp.zeros((4, LANES - ROWS), jnp.float32)


EXP_UNROLL = 2
SOURCE_CHUNKS = 4
SOURCE_UNROLL = 8


def local_source(psi):
    shape = jax.ShapeDtypeStruct
    return pl.pallas_call(
        source_kernel,
        out_shape=shape((PARTS, ROWS, LANES), jnp.float32),
        in_specs=[HBM],
        out_specs=VMEM,
        scratch_shapes=[
            pltpu.VMEM(FULL, jnp.float32),
            pltpu.VMEM((6, 24, 24, LANES), jnp.float32),
            pltpu.VMEM((480, LANES), jnp.float32),
            pltpu.VMEM((488, LANES), jnp.float32),
            pltpu.SemaphoreType.DMA((SOURCE_CHUNKS,)),
        ],
        compiler_params=params(SOURCE_VMEM),
        cost_estimate=cost(3.0),
        name="local_source",
    )(psi)


def message_kernel(place_ref, psi_ref, left_ref, right_ref, first_ref, second_ref, high_ref, low_ref):
    even = flag(place_ref, 4, BLOCK)
    ends = sum(
        (selection((8, 3 * LANES), ((0, 2, k * LANES), (4, 6, k * LANES + 121))) for k in range(1, 3)),
        selection((8, 3 * LANES), ((0, 2, 0), (4, 6, 121))),
    )
    for comp in range(6):
        lines = jnp.concatenate(pieces(psi_ref[comp].reshape(BLOCK * BLOCK, LANES), 3), axis=1)
        found = dot_nt(ends, lines)
        left_ref[comp * 4 : comp * 4 + 4] = found[0:4]
        right_ref[comp * 4 : comp * 4 + 4] = found[4:8]
        for near in range(3):
            down = psi_ref[comp, :, near]
            up = psi_ref[comp, :, BLOCK - 3 + near]
            first_ref[comp, near] = jnp.where(even, up, down)
            second_ref[comp, near] = jnp.where(even, down, up)
            low_ref[comp, near] = psi_ref[comp, near]
            high_ref[comp, near] = psi_ref[comp, BLOCK - 3 + near]


def messages(place, psi):
    shape = jax.ShapeDtypeStruct
    return pl.pallas_call(
        message_kernel,
        out_shape=[shape((24, BLOCK * BLOCK), jnp.float32)] * 2
        + [shape((6, 3, BLOCK, LANES), jnp.float32)] * 4,
        in_specs=[VMEM, VMEM],
        out_specs=[VMEM] * 6,
        compiler_params=params(),
        cost_estimate=cost(4.0),
        name="messages",
    )(place, psi)


def transform_kernel(lines_ref, high_ref, low_ref, *rest):
    out_ref = rest[-1]
    edges = jnp.concatenate([lines_ref[part, LINES:ROWS] for part in range(PARTS)], axis=0)
    edges = jnp.concatenate(pieces(jnp.transpose(edges)[0:ROWS], 2), axis=1)
    row = lax.broadcasted_iota(jnp.int32, (8 * PARTS, NX), 0) & (4 * PARTS - 1)
    lane = lax.broadcasted_iota(jnp.int32, (8 * PARTS, NX), 1)
    offset = jnp.where((row & 3) < 2, (row & 3) - 2, (row & 3) + LANES - 2)
    target = ((row >> 2) * LANES + offset + NX) & (NX - 1)
    target = jnp.where(lane == target, 1.0, 0.0).astype(jnp.bfloat16)
    beyond = jnp.dot(edges, target, preferred_element_type=jnp.float32)
    f = [lines_ref[part] + beyond[:, part * LANES : (part + 1) * LANES] for part in range(PARTS)]
    s = [f[k] + f[k + 4] for k in range(4)]
    o = [f[k] - f[k + 4] for k in range(4)]
    half = math.sqrt(0.5)
    p0, p1, q0, q1 = s[0] + s[2], s[1] + s[3], s[0] - s[2], s[1] - s[3]
    minus, plus = half * (o[1] - o[3]), half * (o[1] + o[3])
    left = [p0 + p1, p0 - p1, q0, o[0] + minus, o[0] - minus, q1, plus + o[2], plus - o[2]]
    high, low = pieces(jnp.concatenate(left, axis=0), 2)
    both = jnp.concatenate([high, low], axis=1)
    wide = 2 * LANES
    found = []
    for part in range(4):
        cols = slice(part * wide, (part + 1) * wide)
        table = jnp.concatenate([high_ref[:, cols]] * 2, axis=0)
        first = jnp.dot(both, table, preferred_element_type=jnp.float32)
        second = jnp.dot(high, low_ref[:, cols], preferred_element_type=jnp.float32)
        found.append([first[k * ROWS : (k + 1) * ROWS] + second[k * ROWS : (k + 1) * ROWS] for k in range(8)])
    phase = lax.broadcasted_iota(jnp.int32, (ROWS, wide), 1) % 8
    outer = (phase == 1) | (phase == 7)
    middle = phase % 4 == 2
    turn = jnp.where(phase % 4 == 0, 0.0, jnp.where(phase < 4, 1.0, -1.0))
    for part in range(4):
        here, there = found[part], found[(part + 2) % 4]
        straight = jnp.where(middle, here[2], jnp.where(outer, here[3], here[4]))
        straight = jnp.where(phase == 0, here[0], jnp.where(phase == 4, here[1], straight))
        crossed = turn * jnp.where(middle, there[5], jnp.where(outer, there[6], there[7]))
        total = straight - crossed if part < 2 else straight + crossed
        out_ref[2 * part] = total[:, 0:LANES]
        out_ref[2 * part + 1] = total[:, LANES:]


def transform(lines, after):
    return pl.pallas_call(
        transform_kernel,
        out_shape=jax.ShapeDtypeStruct((PARTS, ROWS, LANES), jnp.float32),
        in_specs=[VMEM] * 3 + [ANY] * len(after),
        out_specs=VMEM,
        compiler_params=params(),
        cost_estimate=cost(1.5),
        name="transform",
    )(lines, *(jnp.asarray(table) for table in TABLE), *after)


def radial_message_kernel(own_ref, up_ref, down_ref):
    def copy(to, at, line, count):
        while count:
            part, row = divmod(line, LINES)
            some = min(count, LINES - row)
            to[at : at + some] = own_ref[part, row : row + some]
            at, line, count = at + some, line + some, count - some

    for k in range(7):
        for to, row in ((down_ref, k), (up_ref, k + 13)):
            copy(to, k * 20, row * 24, 18)
            copy(to, k * 20 + 18, row * 24 + 22, 2)
    for to in (down_ref, up_ref):
        to[140:144] = jnp.zeros((4, LANES), jnp.float32)


def radial_messages(own):
    return pl.pallas_call(
        radial_message_kernel,
        out_shape=[jax.ShapeDtypeStruct((144, LANES), jnp.float32)] * 2,
        in_specs=[VMEM],
        out_specs=[VMEM] * 2,
        compiler_params=params(),
        cost_estimate=cost(0.3),
        name="radial_messages",
    )(own)


def radial_kernel(place_ref, own_ref, low_ref, high_ref, after_ref, out_ref, first_ref, second_ref, flat, flat_low, flat_high):
    for part in range(PARTS):
        flat[part * LINES : part * LINES + LINES] = own_ref[part, 0:LINES]
    flat_low[...] = jnp.zeros_like(flat_low)
    flat_high[...] = jnp.zeros_like(flat_high)
    for k in range(7):
        for to, message in ((flat_low, low_ref), (flat_high, high_ref)):
            to[k * 24 : k * 24 + 18] = message[k * 20 : k * 20 + 18]
            to[k * 24 + 22 : k * 24 + 24] = message[k * 20 + 18 : k * 20 + 20]
    has_low, has_high = flag(place_ref, 0, 24), flag(place_ref, 1, 24)
    even = flag(place_ref, 4)

    def own(row):
        return flat[row * 24 : row * 24 + 24]

    def low(row):
        at = (row - 13) * 24
        return jnp.where(has_low, flat_low[at : at + 24], 0.0)

    def high(row):
        return jnp.where(has_high, flat_high[row * 24 : row * 24 + 24], 0.0)

    for row in range(26):
        if row < 3:
            value = low(row + 13)
        elif row < 5:
            value = low(row + 13) + jnp.where(has_low, own(row - 3), 0.0)
        elif row < 7:
            value = low(row + 13) + own(row - 3)
        elif row < 19:
            value = own(row - 3)
        elif row < 21:
            value = own(row - 3) + high(row - 19)
        elif row < 23:
            value = jnp.where(has_high, own(row - 3), 0.0) + high(row - 19)
        else:
            value = high(row - 19)
        out_ref[row] = value
        up = pltpu.roll(value, 24 - 11, 0)[0:8]
        down = pltpu.roll(value, 2, 0)[0:8]
        first_ref[row] = jnp.where(even, up, down)
        second_ref[row] = jnp.where(even, down, up)


def radial_assembly(place, own, low, high, after):
    shape = jax.ShapeDtypeStruct
    return pl.pallas_call(
        radial_kernel,
        out_shape=(
            shape((26, 24, LANES), jnp.float32),
            shape((26, 8, LANES), jnp.float32),
            shape((26, 8, LANES), jnp.float32),
        ),
        in_specs=[VMEM] * 4 + [ANY],
        out_specs=[VMEM] * 3,
        scratch_shapes=[
            pltpu.VMEM((480, LANES), jnp.float32),
            pltpu.VMEM((168, LANES), jnp.float32),
            pltpu.VMEM((168, LANES), jnp.float32),
        ],
        compiler_params=params(),
        cost_estimate=cost(0.6),
        name="radial_assembly",
    )(place, own, low, high, after)


def relax_kernel(place_ref, modes_ref, rows_ref, second_ref, first_ref, *rest):
    whole_ref, out_hbm, following_hbm, out_ref, source, one, two, sems = rest
    copies = [pltpu.make_async_copy(whole_ref, following_hbm, sems.at[0])]
    copies[0].start()
    has_low, has_high, even_span = (flag(place_ref, number) for number in (2, 3, 4))
    open_low, open_high = flag(place_ref, 0, 32), flag(place_ref, 1, 32)
    sublane = lax.broadcasted_iota(jnp.int32, (8, LANES), 0)
    always = sublane >= 0
    inside = jnp.concatenate(
        [jnp.where(part, 1.0, 0.0) for part in (has_low, always, always, has_high)], axis=0
    )
    modes = sum(modes_ref[k] * jnp.broadcast_to(place_ref[8 + k : 9 + k], (16, LANES)) for k in range(PARTS))
    weights = [inside * jnp.broadcast_to(modes[2 * j : 2 * j + 1], (32, LANES)) for j in range(6)]
    keeps = [jnp.broadcast_to(modes[2 * j + 1 : 2 * j + 2], (32, LANES)) for j in range(6)]
    pad = jnp.zeros((8, LANES), jnp.float32)

    def walled(row, value):
        if row < 5:
            return jnp.where(open_low, value, 0.0)
        if row > 20:
            return jnp.where(open_high, value, 0.0)
        return value

    for row in range(26):
        own = rows_ref[row]
        tail = own[16:24]
        first, other = first_ref[row], second_ref[row]
        low = jnp.where(has_low, jnp.where(even_span, other, first), 0.0)
        high = jnp.where(has_high, jnp.where(even_span, first, other), 0.0)
        low = pltpu.roll(low, 3, 0)
        high = pltpu.roll(high, 6, 0)
        value = jnp.concatenate(
            [
                jnp.where(sublane >= 6, tail, 0.0) + jnp.where(sublane >= 3, low, 0.0),
                own[0:8] + jnp.where(sublane < 3, low, 0.0),
                own[8:16] + jnp.where(sublane >= 6, high, 0.0),
                jnp.where(sublane < 2, tail, 0.0) + jnp.where(sublane < 6, high, 0.0),
            ],
            axis=0,
        )
        source[row] = value
        one[row, 8:40] = walled(row, value * weights[0])
        for buffer in (one, two):
            buffer[row, 0:8] = pad
            buffer[row, 40:48] = pad

    old, new = one, two
    for sweep in range(1, 6):
        weight, keep = weights[sweep], keeps[sweep]
        for row in range(sweep, 26 - sweep):
            if sweep == 5:
                at, weight_here, keep_here, here = 16, weight[8:24], keep[8:24], source[row, 8:24]
            else:
                at, weight_here, keep_here, here = 8, weight, keep, source[row]
            end = 32 if sweep == 5 else 40
            beside = (old[row - 1, at:end] + old[row + 1, at:end]) + (
                old[row, at - 1 : end - 1] + old[row, at + 1 : end + 1]
            )
            value = keep_here * old[row, at:end] + weight_here * (here + beside)
            if sweep == 5:
                out_ref[row - 5] = value
                if row % 8 == 4:
                    rows = pl.ds(row - 12, 8)
                    copies.append(
                        pltpu.make_async_copy(out_ref.at[rows], out_hbm.at[rows], sems.at[len(copies)])
                    )
                    copies[-1].start()
            else:
                new[row, 8:40] = walled(row, value)
        old, new = new, old
    for copy in copies:
        copy.wait()


def relaxation(place, rows, low, high, whole):
    shape = jax.ShapeDtypeStruct
    return pl.pallas_call(
        relax_kernel,
        out_shape=(
            shape((BLOCK, BLOCK, LANES), jnp.float32),
            shape((6, BLOCK, BLOCK, LANES), jnp.float32),
        ),
        in_specs=[VMEM] * 6,
        out_specs=(HBM, HBM),
        scratch_shapes=[
            pltpu.VMEM((BLOCK, BLOCK, LANES), jnp.float32),
            pltpu.VMEM((26, 32, LANES), jnp.float32),
            pltpu.VMEM((26, 48, LANES), jnp.float32),
            pltpu.VMEM((26, 48, LANES), jnp.float32),
            pltpu.SemaphoreType.DMA((3,)),
        ],
        compiler_params=params(),
        cost_estimate=cost(1.8),
        name="relaxation",
    )(place, jnp.asarray(MODES), rows, low, high, whole)


def weno(positive, p):
    p0 = jnp.where(positive, p[0], p[4])
    p1 = jnp.where(positive, p[1], p[3])
    p2 = p[2]
    p3 = jnp.where(positive, p[3], p[1])
    k1 = (0.609375 * p1) * p1 + 0.75 * EPSILON
    k2 = (0.609375 * p2) * p2 + 0.75 * EPSILON
    r0 = p0 - 1.375 * p1
    r1 = p1 - 0.625 * p2
    r2 = p3 - 1.375 * p2
    q0, q1, q2 = r0 * r0 + k1, r1 * r1 + k2, r2 * r2 + k2
    q01, q02, q12 = q0 * q1, q0 * q2, q1 * q2
    w0, w1, w2 = q12 * q12, 6.0 * (q02 * q02), 3.0 * (q01 * q01)
    middle = p1 - p2
    t0 = (p0 - p1) - middle
    t2 = middle - (p2 - p3)
    total = (w0 + w1) + w2
    guess = pl_reciprocal(total, approx=True)
    inverse = guess * (2.0 - total * guess)
    return ((w0 + w0) * t0 + w2 * t2) * inverse - p1


pl_reciprocal = pltpu.reciprocal


def wind(velocity_ref, direction, row):
    speed = velocity_ref[direction, row]
    positive = speed > 0
    straight = TIME_STEP * speed
    bent = (TIME_STEP / 6) * jnp.abs(speed)
    return positive, straight, bent, jnp.where(positive, 1.0 / 3, 2.0 / 3)


def advected(blow, behind, p):
    positive, straight, bent, side = blow
    return straight * (behind - side * p[2]) + bent * weno(positive, p)


def stream_kernel(psi_ref, velocity_ref, left_ref, right_ref, *rest):
    out_ref, ahead = rest[-2:]
    spread = []
    for comp in range(6):
        ends = jnp.concatenate([right_ref[comp * 4 : comp * 4 + 4], left_ref[comp * 4 : comp * 4 + 4]], axis=0)
        spread += pieces(ends, 3)
    spread = jnp.concatenate([v.astype(jnp.float32) for v in spread], axis=0)
    spread = jnp.transpose(spread).astype(jnp.bfloat16)
    place = selection((8, LANES), ((0, 2, 0), (4, 6, 121))).astype(jnp.float32)
    for comp in range(6):
        rows = [place] * 3
        if comp > 0:
            rows = [jnp.zeros((comp * 24, LANES), jnp.float32)] + rows
        if comp < 5:
            rows = rows + [jnp.zeros((120 - comp * 24, LANES), jnp.float32)]
        rows = jnp.concatenate(rows, axis=0).astype(jnp.bfloat16)
        found = jnp.dot(spread, rows, preferred_element_type=jnp.float32)
        ahead[comp] = found.reshape(BLOCK, BLOCK, LANES)
    lane = lax.broadcasted_iota(jnp.int32, (BLOCK, LANES), 1)

    def step(row, carry):
        blow = wind(velocity_ref, 0, row)
        for comp in range(6):
            psi = psi_ref[comp, row]
            far = ahead[comp, row]
            lines = []
            for j in range(-3, 4):
                if j > 0:
                    mixed = jnp.where(lane < j, far, psi)
                else:
                    mixed = jnp.where(lane >= LANES + j, far, psi)
                lines.append(pltpu.roll(mixed, (-j) % LANES, 1) if j else psi)
            steps = [lines[j + 1] - lines[j] for j in range(6)]
            change = advected(blow, steps[2], [steps[j] - steps[j + 1] for j in range(5)])
            out_ref[comp, row] = psi - change
        return carry

    lax.fori_loop(0, BLOCK, step, 0, unroll=STEP_UNROLL)


def span_kernel(place_ref, psi_ref, velocity_ref, base_ref, first_ref, second_ref, *rest):
    out_ref, column, second = rest[-3:]
    has_down, has_up, even = (flag(place_ref, number, BLOCK) for number in (2, 3, 4))
    for comp in range(6):
        for near in range(3):
            first, other = first_ref[comp, near], second_ref[comp, near]
            column[comp, :, 5 + near] = jnp.where(has_down, jnp.where(even, other, first), 0.0)
            column[comp, :, 24 + near] = jnp.where(has_up, jnp.where(even, first, other), 0.0)

    def bend(row, carry):
        for comp in range(6):
            column[comp, row, 8:24] = psi_ref[comp, row]
            one, two, three = column[comp, row, 5:25], column[comp, row, 6:26], column[comp, row, 7:27]
            second[comp, row, 5:25] = (two - one) - (three - two)
        return carry

    lax.fori_loop(0, BLOCK, bend, 0)

    def step(row, carry):
        blow = wind(velocity_ref, 2, row)
        for comp in range(6):
            behind = psi_ref[comp, row] - column[comp, row, 7:23]
            change = advected(blow, behind, [second[comp, row, 5 + j : 21 + j] for j in range(5)])
            out_ref[comp, row] = base_ref[comp, row] - change
        return carry

    lax.fori_loop(0, BLOCK, step, 0, unroll=STEP_UNROLL)


def radial_kernel_step(place_ref, psi_ref, velocity_ref, base_ref, low_ref, high_ref, *rest):
    out_ref, column, second = rest[-3:]
    has_low, has_high = flag(place_ref, 0, BLOCK), flag(place_ref, 1, BLOCK)
    for comp in range(6):
        for near in range(3):
            column[comp, near] = jnp.where(has_low, low_ref[comp, near], 0.0)
            column[comp, 19 + near] = jnp.where(has_high, high_ref[comp, near], 0.0)

    def copy_in(row, carry):
        for comp in range(6):
            column[comp, row + 3] = psi_ref[comp, row]
        return carry

    lax.fori_loop(0, BLOCK, copy_in, 0)

    def bend(row, carry):
        for comp in range(6):
            one, two, three = column[comp, row], column[comp, row + 1], column[comp, row + 2]
            second[comp, row] = (two - one) - (three - two)
        return carry

    lax.fori_loop(0, 20, bend, 0)

    def step(row, carry):
        blow = wind(velocity_ref, 1, row)
        tensor = [psi_ref[comp, row] for comp in range(6)]
        grown = sym_exp(tensor)
        peterlin = spring(grown)
        shrunk = sym_inverse(grown, tensor)
        for comp in range(6):
            back = shrunk[comp] - peterlin if DIAG[comp] else shrunk[comp]
            behind = tensor[comp] - column[comp, row + 2]
            change = advected(blow, behind, [second[comp, row + j] for j in range(5)])
            out_ref[comp, row] = (base_ref[comp, row] + (TIME_STEP / WEISSENBERG) * back) - change
        return carry

    lax.fori_loop(0, BLOCK, step, 0, unroll=STEP_UNROLL)


STEP_UNROLL = 2


def advect(kernel, name, scratch, arrays, after):
    return pl.pallas_call(
        kernel,
        out_shape=jax.ShapeDtypeStruct(FULL, jnp.float32),
        in_specs=[VMEM] * len(arrays) + [ANY] * len(after),
        out_specs=VMEM,
        scratch_shapes=[pltpu.VMEM(shape, jnp.float32) for shape in scratch],
        compiler_params=params(),
        cost_estimate=cost(2.5),
        name=name,
    )(*arrays, *after)


def ring(axis, step):
    count = lax.axis_size(axis)
    return [(i, (i + step) % count) for i in range(count)]


def exchange(to_next, to_previous, axis):
    return (
        lax.ppermute(to_next, axis, ring(axis, 1)),
        lax.ppermute(to_previous, axis, ring(axis, -1)),
    )


def trade(first, second, axis):
    count = lax.axis_size(axis)
    inner = [(i, i ^ 1) for i in range(count)]
    outer = [(i, (i - 1) % count if i % 2 == 0 else (i + 1) % count) for i in range(count)]
    second = lax.ppermute(second, axis, outer)
    return lax.ppermute(first, axis, inner), second


def shards(psi, velocity):
    radial, span = lax.axis_index("radial"), lax.axis_index("span")
    bits = (radial > 0) + 2 * (radial < 7) + 4 * (span > 0) + 8 * (span < 3) + 16 * (span % 2 == 0)
    number = lax.broadcasted_iota(jnp.int32, (16, LANES), 0)
    place = ((bits >> number) & (number < 8)) | (number == lax.axis_index("stream") + 8)
    place = place.astype(jnp.float32)
    wide = (6, BLOCK, 32, LANES)
    tall = [(6, 22, BLOCK, LANES), (6, 20, BLOCK, LANES)]
    send = local_source(psi)
    later, send = lax.optimization_barrier((psi, send))
    lines = lax.all_to_all(send, "stream", split_axis=0, concat_axis=0, tiled=True)
    to_left, to_right, to_first, to_second, to_high, to_low = messages(place, later)
    ends = exchange(to_right, to_left, "stream")
    sides = trade(to_first, to_second, "span")
    spectrum = transform(lines, (to_left,))
    own = lax.all_to_all(spectrum, "stream", split_axis=0, concat_axis=0, tiled=True)
    state = advect(stream_kernel, "advect_stream", [FULL], (psi, velocity) + ends, (spectrum,))
    below, above = exchange(*radial_messages(own), "radial")
    to_high, to_low = lax.optimization_barrier((to_high, to_low, spectrum))[:2]
    walls = exchange(to_high, to_low, "radial")
    state = advect(span_kernel, "advect_span", [wide, wide], (place, psi, velocity, state) + sides, (own,))
    rows, rows_first, rows_second = radial_assembly(place, own, below, above, state)
    first, second = trade(rows_first, rows_second, "span")
    state = advect(radial_kernel_step, "advect_radial", tall, (place, psi, velocity, state) + walls, (rows,))
    pressure, following = relaxation(place, rows, second, first, state)
    return following, pressure


def solution(mesh):
    return jax.shard_map(
        shards,
        mesh=mesh,
        in_specs=(P(None, "radial", "span", "stream"), P(None, "radial", "span", "stream")),
        out_specs=(P(None, "radial", "span", "stream"), P("radial", "span", "stream")),
        check_vma=False,
    )
```

```python
import functools
import math

import jax
import jax.numpy as jnp
import ml_dtypes
import numpy as np
from jax import lax
from jax.experimental import pallas as pl
from jax.experimental.pallas import tpu as pltpu
from jax.sharding import PartitionSpec as P

NX = 1024
LANES = 128
BLOCK = 16
PARTS = 8
FULL = (6, BLOCK, BLOCK, LANES)
COLUMNS = 20
SIDE_ROWS = 184
LINES = 50
ROWS = 56

WEISSENBERG = 20.0
EXTENSIBILITY = 100.0
TIME_STEP = 2.0
EPSILON = 1e-06
COSINES = tuple((math.cos((2 * number + 1) * math.pi / 12.0) for number in range(6)))
VMEM_LIMIT = 16 * 1024 * 1024
SOURCE_VMEM = 62 * 1024 * 1024


def split_bf16(table):
    high = table.astype(np.float32).astype(ml_dtypes.bfloat16)
    low = (table - high.astype(np.float64)).astype(np.float32).astype(ml_dtypes.bfloat16)
    return high, low


def tables():
    ordinal = np.arange(NX)
    wave = np.where(ordinal <= NX // 2, ordinal, ordinal - NX // 2)
    angle = 2.0 * np.pi / NX * ((ordinal[:, None] * wave[None, :]) % NX)
    fourier = -np.where((ordinal <= NX // 2)[None, :], np.cos(angle), np.sin(angle)) * NX**-0.5
    return split_bf16(fourier[:LANES])


def mode_table():
    ordinal = np.arange(NX)
    wave = np.where(ordinal <= NX // 2, ordinal, ordinal - NX // 2)
    diagonal = 4.0 + 4.0 * np.sin(np.pi * wave / NX) ** 2
    ratio = 4.0 / diagonal
    upper = 1.0 + ratio
    lower = np.maximum(0.3, 1.0 - ratio)
    rows = []
    for cosine in COSINES:
        omega = 1.0 / (0.5 * (upper + lower) + 0.5 * (upper - lower) * cosine)
        rows += [omega / diagonal, 1.0 - omega]
    rows += [np.zeros(NX)] * 4
    return np.stack(rows).astype(np.float32).reshape(16, PARTS, LANES).transpose(1, 0, 2)


def flag(place_ref, number, rows=8):
    return jnp.broadcast_to(place_ref[number : number + 1], (rows, LANES)) > 0.5


TABLE = tables()
MODES = mode_table()


def params(limit=VMEM_LIMIT):
    return pltpu.CompilerParams(vmem_limit_bytes=limit)


def cost(microseconds):
    return pl.CostEstimate(
        flops=int(microseconds * 1.1e9), bytes_accessed=int(microseconds * 3.6e6), transcendentals=0
    )


VMEM = pl.BlockSpec(memory_space=pltpu.VMEM)
SMEM = pl.BlockSpec(memory_space=pltpu.SMEM)
HBM = pl.BlockSpec(memory_space=pltpu.HBM)
ANY = pl.BlockSpec(memory_space=pl.ANY)


def dot_nt(left, right):
    return lax.dot_general(left, right, (((1,), (1,)), ((), ())), preferred_element_type=jnp.float32)


def dot_tn(left, right):
    return lax.dot_general(left, right, (((0,), (0,)), ((), ())), preferred_element_type=jnp.float32)


def pieces(value, count):
    found = []
    for _ in range(count):
        found.append(value.astype(jnp.bfloat16))
        value = value - found[-1].astype(jnp.float32)
    return found


def selection(shape, pairs):
    row = lax.broadcasted_iota(jnp.int32, shape, 0)
    column = lax.broadcasted_iota(jnp.int32, shape, 1)
    hit = None
    for first, last, shift in pairs:
        here = (row >= first) & (row <= last) & (column == row + shift)
        hit = here if hit is None else hit | here
    return jnp.where(hit, 1.0, 0.0).astype(jnp.bfloat16)


def sym_square(m):
    a, b, c, d, e, f = m
    bb, cc, ee = b * b, c * c, e * e
    return [
        a * a + bb + cc,
        b * (a + d) + c * e,
        c * (a + f) + b * e,
        bb + d * d + ee,
        e * (d + f) + b * c,
        cc + ee + f * f,
    ]


def sym_times(m, n):
    a, b, c, d, e, f = m
    p, q, r, s, t, u = n
    return [
        a * p + b * q + c * r,
        a * q + b * s + c * t,
        a * r + b * t + c * u,
        b * q + d * s + e * t,
        b * r + d * t + e * u,
        c * r + e * t + f * u,
    ]


DIAG = (1.0, 0.0, 0.0, 1.0, 0.0, 1.0)


def with_diag(m, value):
    return [m[i] + value if DIAG[i] else m[i] for i in range(6)]


def sym_exp(psi):
    m = [0.125 * v for v in psi]
    m2 = sym_square(m)
    m3 = sym_times(m, m2)
    tail = [m[i] * (1.0 / 24) + m2[i] * (1.0 / 120) + m3[i] * (1.0 / 720) for i in range(6)]
    tail = sym_times(m3, with_diag(tail, 1.0 / 6))
    out = with_diag([m[i] + 0.5 * m2[i] + tail[i] for i in range(6)], 1.0)
    for _ in range(3):
        out = sym_square(out)
    return out


def sym_inverse(grown, psi):
    a, b, c, d, e, f = grown
    scale = jnp.exp(-(psi[0] + psi[3] + psi[5]))
    return [
        (d * f - e * e) * scale,
        (c * e - b * f) * scale,
        (b * e - c * d) * scale,
        (a * f - c * c) * scale,
        (b * c - a * e) * scale,
        (a * d - b * b) * scale,
    ]


def spring(grown):
    return (EXTENSIBILITY - 3.0) / (EXTENSIBILITY - (grown[0] + grown[3] + grown[5]))


def segments(first, count):
    at = 0
    while at < count:
        row, column = divmod(first + at, COLUMNS)
        own = column < 18
        some = min(count - at, (18 if own else COLUMNS) - column)
        yield at, row * 24 + column + (0 if own else 4), some
        at += some


def source_kernel(psi_hbm, send_ref, psi_ref, stress, field, wrapped, packed, sems):
    chunk = BLOCK // SOURCE_CHUNKS
    arrivals = []
    for part in range(SOURCE_CHUNKS):
        rows = pl.ds(part * chunk, chunk)
        arrivals.append(pltpu.make_async_copy(psi_hbm.at[:, rows], psi_ref.at[:, rows], sems.at[part]))
        arrivals[-1].start()
    zero = jnp.zeros((24, LANES), jnp.float32)
    for comp in (1, 3, 4):
        for row in (0, 1, 2, 3, 20, 21, 22, 23):
            stress[comp, row] = zero

    def relax_row(row, carry):
        psi = [psi_ref[comp, row] for comp in range(6)]
        grown = sym_exp(psi)
        peterlin = spring(grown)
        pad = jnp.zeros((8, LANES), jnp.float32)
        for comp in range(6):
            value = peterlin * grown[comp]
            stress[comp, row + 4, 0:16] = value - 1.0 if DIAG[comp] else value
            stress[comp, row + 4, 16:24] = pad
        return carry

    for part in range(SOURCE_CHUNKS):
        arrivals[part].wait()
        lax.fori_loop(part * chunk, part * chunk + chunk, relax_row, 0, unroll=EXP_UNROLL)

    lane = lax.broadcasted_iota(jnp.int32, (24, LANES), 1)
    inner = [lane < LANES - 1, lane >= 1, lane < LANES - 2, lane >= 2]

    def along(value, shift):
        return pltpu.roll(value, shift % 24, 0)

    def shifted(value, shift):
        return pltpu.roll(value, shift % LANES, 1)

    def emit(row, plain, once, twice):
        parts = [shifted(once, -1), -shifted(once, 1), shifted(twice, -2), shifted(twice, 2)]
        total = plain - 2.0 * twice
        beyond = zero
        for part, mask in zip(parts, inner):
            kept = jnp.where(mask, part, 0.0)
            total = total + kept
            beyond = beyond + (part - kept)
        at = row * 24 if isinstance(row, int) else pl.multiple_of(row * 24, 8)
        field[pl.ds(at, 24)] = total
        wrapped[pl.ds(at, 24)] = beyond

    def body(row, carry):
        here = row + 2
        s11 = 0.25 * (stress[3, here + 2] - 2.0 * stress[3, here] + stress[3, here - 2])
        u12 = 0.5 * (stress[4, here + 1] - stress[4, here - 1])
        u01 = 0.5 * (stress[1, here + 1] - stress[1, here - 1])
        s22, s02, s00 = stress[5, here], stress[2, here], stress[0, here]
        c22 = 0.25 * (along(s22, -2) - 2.0 * s22 + along(s22, 2))
        c12 = along(u12, -1) - along(u12, 1)
        c02 = 0.5 * (along(s02, -1) - along(s02, 1))
        emit(row, s11 + c22 + c12, u01 + c02, 0.25 * s00)
        return carry

    lax.fori_loop(2, 18, body, 0, unroll=SOURCE_UNROLL)
    for row in (0, 1, 18, 19):
        here = row + 2
        other = here + 2 if row < 2 else here - 2
        s11 = 0.25 * stress[3, other]
        if row in (1, 18):
            near = here + 1 if row == 1 else here - 1
            sign = 0.5 if row == 1 else -0.5
            u12 = sign * stress[4, near]
            u01 = sign * stress[1, near]
            emit(row, s11 + along(u12, -1) - along(u12, 1), u01, zero)
        else:
            emit(row, s11, zero, zero)
    pick = selection((8, 2 * LANES), ((0, 1, 126), (2, 3, -2)))
    pick = pick + selection((8, 2 * LANES), ((0, 1, 126 + LANES), (2, 3, LANES - 2)))
    for part in range(PARTS):
        send_ref[part, ROWS - 8 : ROWS] = jnp.zeros((8, LANES), jnp.float32)
        packed[part, 48:64] = jnp.zeros((16, LANES), jnp.float32)
        for at, line, count in segments(part * LINES, LINES):
            send_ref[part, at : at + count] = field[line : line + count]
            packed[part, at : at + count] = wrapped[line : line + count]
    for part in range(PARTS):
        lines = dot_nt(pick, jnp.concatenate(pieces(packed[part], 2), axis=1))
        send_ref[part, LINES : LINES + 4, 0:64] = lines[0:4]


EXP_UNROLL = 4
SOURCE_CHUNKS = 4
SOURCE_UNROLL = 16


def local_source(psi):
    shape = jax.ShapeDtypeStruct
    return pl.pallas_call(
        source_kernel,
        out_shape=shape((PARTS, ROWS, LANES), jnp.float32),
        in_specs=[HBM],
        out_specs=VMEM,
        scratch_shapes=[
            pltpu.VMEM(FULL, jnp.float32),
            pltpu.VMEM((6, 24, 24, LANES), jnp.float32),
            pltpu.VMEM((480, LANES), jnp.float32),
            pltpu.VMEM((480, LANES), jnp.float32),
            pltpu.VMEM((PARTS, 64, LANES), jnp.float32),
            pltpu.SemaphoreType.DMA((SOURCE_CHUNKS,)),
        ],
        compiler_params=params(SOURCE_VMEM),
        cost_estimate=cost(3.0),
        name="local_source",
    )(psi)


def message_kernel(place_ref, psi_ref, left_ref, right_ref, first_ref, second_ref, high_ref, low_ref):
    even = flag(place_ref, 4, BLOCK)
    ends = sum(
        (selection((8, 3 * LANES), ((0, 2, k * LANES), (4, 6, k * LANES + 121))) for k in range(1, 3)),
        selection((8, 3 * LANES), ((0, 2, 0), (4, 6, 121))),
    )
    for comp in range(6):
        lines = jnp.concatenate(pieces(psi_ref[comp].reshape(BLOCK * BLOCK, LANES), 3), axis=1)
        found = dot_nt(ends, lines)
        left_ref[comp * 4 : comp * 4 + 4] = found[0:4]
        right_ref[comp * 4 : comp * 4 + 4] = found[4:8]
        for near in range(3):
            down = psi_ref[comp, :, near]
            up = psi_ref[comp, :, BLOCK - 3 + near]
            first_ref[comp, near] = jnp.where(even, up, down)
            second_ref[comp, near] = jnp.where(even, down, up)
            low_ref[comp, near] = psi_ref[comp, near]
            high_ref[comp, near] = psi_ref[comp, BLOCK - 3 + near]


def messages(place, psi):
    shape = jax.ShapeDtypeStruct
    return pl.pallas_call(
        message_kernel,
        out_shape=[shape((24, BLOCK * BLOCK), jnp.float32)] * 2
        + [shape((6, 3, BLOCK, LANES), jnp.float32)] * 4,
        in_specs=[VMEM, VMEM],
        out_specs=[VMEM] * 6,
        compiler_params=params(),
        cost_estimate=cost(4.0),
        name="messages",
    )(place, psi)


def transform_kernel(lines_ref, high_ref, low_ref, *rest):
    out_ref = rest[-1]
    edges = jnp.concatenate([lines_ref[part, LINES : LINES + 4] for part in range(PARTS)], axis=0)
    edges = jnp.concatenate(pieces(jnp.transpose(edges)[0:64], 2), axis=1)
    row = lax.broadcasted_iota(jnp.int32, (8 * PARTS, NX), 0) & (4 * PARTS - 1)
    lane = lax.broadcasted_iota(jnp.int32, (8 * PARTS, NX), 1)
    offset = jnp.where((row & 3) < 2, (row & 3) - 2, (row & 3) + LANES - 2)
    target = ((row >> 2) * LANES + offset + NX) & (NX - 1)
    target = jnp.where(lane == target, 1.0, 0.0).astype(jnp.bfloat16)
    beyond = jnp.dot(edges, target, preferred_element_type=jnp.float32)
    f = [lines_ref[part] + beyond[0:ROWS, part * LANES : (part + 1) * LANES] for part in range(PARTS)]
    s = [f[k] + f[k + 4] for k in range(4)]
    o = [f[k] - f[k + 4] for k in range(4)]
    half = math.sqrt(0.5)
    p0, p1, q0, q1 = s[0] + s[2], s[1] + s[3], s[0] - s[2], s[1] - s[3]
    minus, plus = half * (o[1] - o[3]), half * (o[1] + o[3])
    left = [p0 + p1, p0 - p1, q0, o[0] + minus, o[0] - minus, q1, plus + o[2], plus - o[2]]
    high, low = pieces(jnp.concatenate(left, axis=0), 2)
    both = jnp.concatenate([high, low], axis=1)
    wide = 2 * LANES
    found = []
    for part in range(4):
        cols = slice(part * wide, (part + 1) * wide)
        table = jnp.concatenate([high_ref[:, cols]] * 2, axis=0)
        first = jnp.dot(both, table, preferred_element_type=jnp.float32)
        second = jnp.dot(high, low_ref[:, cols], preferred_element_type=jnp.float32)
        found.append([first[k * ROWS : (k + 1) * ROWS] + second[k * ROWS : (k + 1) * ROWS] for k in range(8)])
    phase = lax.broadcasted_iota(jnp.int32, (ROWS, wide), 1) % 8
    outer = (phase == 1) | (phase == 7)
    middle = phase % 4 == 2
    turn = jnp.where(phase % 4 == 0, 0.0, jnp.where(phase < 4, 1.0, -1.0))
    for part in range(4):
        here, there = found[part], found[(part + 2) % 4]
        straight = jnp.where(middle, here[2], jnp.where(outer, here[3], here[4]))
        straight = jnp.where(phase == 0, here[0], jnp.where(phase == 4, here[1], straight))
        crossed = turn * jnp.where(middle, there[5], jnp.where(outer, there[6], there[7]))
        total = straight - crossed if part < 2 else straight + crossed
        out_ref[2 * part] = total[:, 0:LANES]
        out_ref[2 * part + 1] = total[:, LANES:]


def transform(lines, after):
    return pl.pallas_call(
        transform_kernel,
        out_shape=jax.ShapeDtypeStruct((PARTS, ROWS, LANES), jnp.float32),
        in_specs=[VMEM] * 3 + [ANY] * len(after),
        out_specs=VMEM,
        compiler_params=params(),
        cost_estimate=cost(1.5),
        name="transform",
    )(lines, *(jnp.asarray(table) for table in TABLE), *after)


def radial_message_kernel(own_ref, up_ref, down_ref):
    for to, line in ((down_ref, 0), (up_ref, 13 * COLUMNS)):
        at = 0
        while at < 140:
            part, row = divmod(line + at, LINES)
            some = min(140 - at, LINES - row)
            to[at : at + some] = own_ref[part, row : row + some]
            at += some
    for to in (down_ref, up_ref):
        to[140:144] = jnp.zeros((4, LANES), jnp.float32)


def radial_messages(own):
    return pl.pallas_call(
        radial_message_kernel,
        out_shape=[jax.ShapeDtypeStruct((144, LANES), jnp.float32)] * 2,
        in_specs=[VMEM],
        out_specs=[VMEM] * 2,
        compiler_params=params(),
        cost_estimate=cost(0.3),
        name="radial_messages",
    )(own)


def radial_kernel(place_ref, own_ref, low_ref, high_ref, after_ref, out_ref, first_ref, second_ref, flat, flat_low, flat_high):
    flat[...] = jnp.zeros_like(flat)
    for part in range(PARTS):
        for at, line, count in segments(part * LINES, LINES):
            flat[line : line + count] = own_ref[part, at : at + count]
    flat_low[...] = jnp.zeros_like(flat_low)
    flat_high[...] = jnp.zeros_like(flat_high)
    for k in range(7):
        for to, message in ((flat_low, low_ref), (flat_high, high_ref)):
            to[k * 24 : k * 24 + 18] = message[k * 20 : k * 20 + 18]
            to[k * 24 + 22 : k * 24 + 24] = message[k * 20 + 18 : k * 20 + 20]
    has_low, has_high = flag(place_ref, 0, 24), flag(place_ref, 1, 24)
    even = flag(place_ref, 4)

    def own(row):
        return flat[row * 24 : row * 24 + 24]

    def low(row):
        at = (row - 13) * 24
        return jnp.where(has_low, flat_low[at : at + 24], 0.0)

    def high(row):
        return jnp.where(has_high, flat_high[row * 24 : row * 24 + 24], 0.0)

    for to in (first_ref, second_ref):
        to[SIDE_ROWS - 8 : SIDE_ROWS] = jnp.zeros((8, LANES), jnp.float32)
    for row in range(26):
        if row < 3:
            value = low(row + 13)
        elif row < 5:
            value = low(row + 13) + jnp.where(has_low, own(row - 3), 0.0)
        elif row < 7:
            value = low(row + 13) + own(row - 3)
        elif row < 19:
            value = own(row - 3)
        elif row < 21:
            value = own(row - 3) + high(row - 19)
        elif row < 23:
            value = jnp.where(has_high, own(row - 3), 0.0) + high(row - 19)
        else:
            value = high(row - 19)
        out_ref[row] = value
        up = pltpu.roll(value, 24 - 11, 0)[0:8]
        down = pltpu.roll(value, 2, 0)[0:8]
        at = slice(row * 7, row * 7 + 7)
        first_ref[at] = jnp.where(even, up, down)[0:7]
        second_ref[at] = jnp.where(even, down, up)[0:7]


def radial_assembly(place, own, low, high, after):
    shape = jax.ShapeDtypeStruct
    return pl.pallas_call(
        radial_kernel,
        out_shape=(
            shape((26, 24, LANES), jnp.float32),
            shape((SIDE_ROWS, LANES), jnp.float32),
            shape((SIDE_ROWS, LANES), jnp.float32),
        ),
        in_specs=[VMEM] * 4 + [ANY],
        out_specs=[VMEM] * 3,
        scratch_shapes=[
            pltpu.VMEM((480, LANES), jnp.float32),
            pltpu.VMEM((168, LANES), jnp.float32),
            pltpu.VMEM((168, LANES), jnp.float32),
        ],
        compiler_params=params(),
        cost_estimate=cost(0.6),
        name="radial_assembly",
    )(place, own, low, high, after)


def relax_kernel(place_ref, modes_ref, rows_ref, second_ref, first_ref, *rest):
    whole_ref, out_hbm, following_hbm, out_ref, source, one, two, sems = rest
    copies = [pltpu.make_async_copy(whole_ref, following_hbm, sems.at[0])]
    copies[0].start()
    has_low, has_high, even_span = (flag(place_ref, number) for number in (2, 3, 4))
    open_low, open_high = flag(place_ref, 0, 32), flag(place_ref, 1, 32)
    sublane = lax.broadcasted_iota(jnp.int32, (8, LANES), 0)
    always = sublane >= 0
    inside = jnp.concatenate(
        [jnp.where(part, 1.0, 0.0) for part in (has_low, always, always, has_high)], axis=0
    )
    modes = sum(modes_ref[k] * jnp.broadcast_to(place_ref[8 + k : 9 + k], (16, LANES)) for k in range(PARTS))
    weights = [inside * jnp.broadcast_to(modes[2 * j : 2 * j + 1], (32, LANES)) for j in range(6)]
    keeps = [jnp.broadcast_to(modes[2 * j + 1 : 2 * j + 2], (32, LANES)) for j in range(6)]
    pad = jnp.zeros((8, LANES), jnp.float32)

    def walled(row, value):
        if row < 5:
            return jnp.where(open_low, value, 0.0)
        if row > 20:
            return jnp.where(open_high, value, 0.0)
        return value

    for row in range(26):
        own = rows_ref[row]
        tail = own[16:24]
        first, other = (ref[row * 7 : row * 7 + 8] for ref in (first_ref, second_ref))
        low = jnp.where(has_low, jnp.where(even_span, other, first), 0.0)
        high = jnp.where(has_high, jnp.where(even_span, first, other), 0.0)
        low = pltpu.roll(low, 3, 0)
        high = pltpu.roll(high, 6, 0)
        value = jnp.concatenate(
            [
                jnp.where(sublane >= 6, tail, 0.0) + jnp.where(sublane >= 3, low, 0.0),
                own[0:8] + jnp.where(sublane < 2, low, 0.0),
                own[8:16] + jnp.where(sublane >= 6, high, 0.0),
                jnp.where(sublane < 2, tail, 0.0) + jnp.where(sublane < 6, high, 0.0),
            ],
            axis=0,
        )
        source[row] = value
        one[row, 8:40] = walled(row, value * weights[0])
        for buffer in (one, two):
            buffer[row, 0:8] = pad
            buffer[row, 40:48] = pad

    old, new = one, two
    for sweep in range(1, 6):
        weight, keep = weights[sweep], keeps[sweep]
        for row in range(sweep, 26 - sweep):
            if sweep == 5:
                at, weight_here, keep_here, here = 16, weight[8:24], keep[8:24], source[row, 8:24]
            else:
                at, weight_here, keep_here, here = 8, weight, keep, source[row]
            end = 32 if sweep == 5 else 40
            beside = (old[row - 1, at:end] + old[row + 1, at:end]) + (
                old[row, at - 1 : end - 1] + old[row, at + 1 : end + 1]
            )
            value = keep_here * old[row, at:end] + weight_here * (here + beside)
            if sweep == 5:
                out_ref[row - 5] = value
                if row % 8 == 4:
                    rows = pl.ds(row - 12, 8)
                    copies.append(
                        pltpu.make_async_copy(out_ref.at[rows], out_hbm.at[rows], sems.at[len(copies)])
                    )
                    copies[-1].start()
            else:
                new[row, 8:40] = walled(row, value)
        old, new = new, old
    for copy in copies:
        copy.wait()


def relaxation(place, rows, low, high, whole):
    shape = jax.ShapeDtypeStruct
    return pl.pallas_call(
        relax_kernel,
        out_shape=(
            shape((BLOCK, BLOCK, LANES), jnp.float32),
            shape((6, BLOCK, BLOCK, LANES), jnp.float32),
        ),
        in_specs=[VMEM] * 6,
        out_specs=(HBM, HBM),
        scratch_shapes=[
            pltpu.VMEM((BLOCK, BLOCK, LANES), jnp.float32),
            pltpu.VMEM((26, 32, LANES), jnp.float32),
            pltpu.VMEM((26, 48, LANES), jnp.float32),
            pltpu.VMEM((26, 48, LANES), jnp.float32),
            pltpu.SemaphoreType.DMA((3,)),
        ],
        compiler_params=params(),
        cost_estimate=cost(1.8),
        name="relaxation",
    )(place, jnp.asarray(MODES), rows, low, high, whole)


def weno(positive, p):
    p0 = jnp.where(positive, p[0], p[4])
    p1 = jnp.where(positive, p[1], p[3])
    p2 = p[2]
    p3 = jnp.where(positive, p[3], p[1])
    k1 = (0.609375 * p1) * p1 + 0.75 * EPSILON
    k2 = (0.609375 * p2) * p2 + 0.75 * EPSILON
    r0 = p0 - 1.375 * p1
    r1 = p1 - 0.625 * p2
    r2 = p3 - 1.375 * p2
    q0, q1, q2 = r0 * r0 + k1, r1 * r1 + k2, r2 * r2 + k2
    q01, q02, q12 = q0 * q1, q0 * q2, q1 * q2
    w0, w1, w2 = q12 * q12, 6.0 * (q02 * q02), 3.0 * (q01 * q01)
    middle = p1 - p2
    t0 = (p0 - p1) - middle
    t2 = middle - (p2 - p3)
    total = (w0 + w1) + w2
    guess = pl_reciprocal(total, approx=True)
    inverse = guess * (2.0 - total * guess)
    return ((w0 + w0) * t0 + w2 * t2) * inverse - p1


pl_reciprocal = pltpu.reciprocal


def wind(velocity_ref, direction, row):
    speed = velocity_ref[direction, row]
    positive = speed > 0
    straight = TIME_STEP * speed
    bent = (TIME_STEP / 6) * jnp.abs(speed)
    return positive, straight, bent, jnp.where(positive, 1.0 / 3, 2.0 / 3)


def advected(blow, behind, p):
    positive, straight, bent, side = blow
    return straight * (behind - side * p[2]) + bent * weno(positive, p)


def stream_kernel(psi_ref, velocity_ref, left_ref, right_ref, *rest):
    out_ref, ahead = rest[-2:]
    spread = []
    for comp in range(6):
        ends = jnp.concatenate([right_ref[comp * 4 : comp * 4 + 4], left_ref[comp * 4 : comp * 4 + 4]], axis=0)
        spread += pieces(ends, 2)
    spread = jnp.concatenate([v.astype(jnp.float32) for v in spread], axis=0)
    spread = jnp.transpose(spread).astype(jnp.bfloat16)
    place = selection((8, LANES), ((0, 2, 0), (4, 6, 121))).astype(jnp.float32)
    for comp in range(6):
        rows = [place] * 2
        if comp > 0:
            rows = [jnp.zeros((comp * 16, LANES), jnp.float32)] + rows
        if comp < 5:
            rows = rows + [jnp.zeros((80 - comp * 16, LANES), jnp.float32)]
        rows = jnp.concatenate(rows, axis=0).astype(jnp.bfloat16)
        found = jnp.dot(spread, rows, preferred_element_type=jnp.float32)
        ahead[comp] = found.reshape(BLOCK, BLOCK, LANES)
    lane = lax.broadcasted_iota(jnp.int32, (BLOCK, LANES), 1)

    def step(row, carry):
        blow = wind(velocity_ref, 0, row)
        for comp in range(6):
            psi = psi_ref[comp, row]
            far = ahead[comp, row]
            lines = []
            for j in range(-3, 4):
                if j > 0:
                    mixed = jnp.where(lane < j, far, psi)
                else:
                    mixed = jnp.where(lane >= LANES + j, far, psi)
                lines.append(pltpu.roll(mixed, (-j) % LANES, 1) if j else psi)
            steps = [lines[j + 1] - lines[j] for j in range(6)]
            change = advected(blow, steps[2], [steps[j] - steps[j + 1] for j in range(5)])
            out_ref[comp, row] = psi - change
        return carry

    lax.fori_loop(0, BLOCK, step, 0, unroll=STEP_UNROLL)


def span_kernel(place_ref, psi_ref, velocity_ref, base_ref, first_ref, second_ref, *rest):
    out_ref, column, second = rest[-3:]
    has_down, has_up, even = (flag(place_ref, number, BLOCK) for number in (2, 3, 4))
    for comp in range(6):
        for near in range(3):
            first, other = first_ref[comp, near], second_ref[comp, near]
            column[comp, :, 5 + near] = jnp.where(has_down, jnp.where(even, other, first), 0.0)
            column[comp, :, 24 + near] = jnp.where(has_up, jnp.where(even, first, other), 0.0)

    def bend(row, carry):
        for comp in range(6):
            column[comp, row, 8:24] = psi_ref[comp, row]
            one, two, three = column[comp, row, 5:25], column[comp, row, 6:26], column[comp, row, 7:27]
            second[comp, row, 5:25] = (two - one) - (three - two)
        return carry

    lax.fori_loop(0, BLOCK, bend, 0)

    def step(row, carry):
        blow = wind(velocity_ref, 2, row)
        for comp in range(6):
            behind = psi_ref[comp, row] - column[comp, row, 7:23]
            change = advected(blow, behind, [second[comp, row, 5 + j : 21 + j] for j in range(5)])
            out_ref[comp, row] = base_ref[comp, row] - change
        return carry

    lax.fori_loop(0, BLOCK, step, 0, unroll=STEP_UNROLL)


def radial_kernel_step(place_ref, psi_ref, velocity_ref, base_ref, low_ref, high_ref, *rest):
    out_ref, column, second = rest[-3:]
    has_low, has_high = flag(place_ref, 0, BLOCK), flag(place_ref, 1, BLOCK)
    for comp in range(6):
        for near in range(3):
            column[comp, near] = jnp.where(has_low, low_ref[comp, near], 0.0)
            column[comp, 19 + near] = jnp.where(has_high, high_ref[comp, near], 0.0)

    def copy_in(row, carry):
        for comp in range(6):
            column[comp, row + 3] = psi_ref[comp, row]
        return carry

    lax.fori_loop(0, BLOCK, copy_in, 0)

    def bend(row, carry):
        for comp in range(6):
            one, two, three = column[comp, row], column[comp, row + 1], column[comp, row + 2]
            second[comp, row] = (two - one) - (three - two)
        return carry

    lax.fori_loop(0, 20, bend, 0)

    def step(row, carry):
        blow = wind(velocity_ref, 1, row)
        tensor = [psi_ref[comp, row] for comp in range(6)]
        grown = sym_exp(tensor)
        peterlin = spring(grown)
        shrunk = sym_inverse(grown, tensor)
        for comp in range(6):
            back = shrunk[comp] - peterlin if DIAG[comp] else shrunk[comp]
            behind = tensor[comp] - column[comp, row + 2]
            change = advected(blow, behind, [second[comp, row + j] for j in range(5)])
            out_ref[comp, row] = (base_ref[comp, row] + (TIME_STEP / WEISSENBERG) * back) - change
        return carry

    lax.fori_loop(0, BLOCK, step, 0, unroll=STEP_UNROLL)


STEP_UNROLL = 2


def advect(kernel, name, scratch, arrays, after):
    return pl.pallas_call(
        kernel,
        out_shape=jax.ShapeDtypeStruct(FULL, jnp.float32),
        in_specs=[VMEM] * len(arrays) + [ANY] * len(after),
        out_specs=VMEM,
        scratch_shapes=[pltpu.VMEM(shape, jnp.float32) for shape in scratch],
        compiler_params=params(),
        cost_estimate=cost(2.5),
        name=name,
    )(*arrays, *after)


def ring(axis, step):
    count = lax.axis_size(axis)
    return [(i, (i + step) % count) for i in range(count)]


def exchange(to_next, to_previous, axis):
    return (
        lax.ppermute(to_next, axis, ring(axis, 1)),
        lax.ppermute(to_previous, axis, ring(axis, -1)),
    )


def trade(first, second, axis):
    count = lax.axis_size(axis)
    inner = [(i, i ^ 1) for i in range(count)]
    outer = [(i, (i - 1) % count if i % 2 == 0 else (i + 1) % count) for i in range(count)]
    second = lax.ppermute(second, axis, outer)
    return lax.ppermute(first, axis, inner), second


def shards(psi, velocity):
    radial, span = lax.axis_index("radial"), lax.axis_index("span")
    bits = (radial > 0) + 2 * (radial < 7) + 4 * (span > 0) + 8 * (span < 3) + 16 * (span % 2 == 0)
    number = lax.broadcasted_iota(jnp.int32, (16, LANES), 0)
    place = ((bits >> number) & (number < 8)) | (number == lax.axis_index("stream") + 8)
    place = place.astype(jnp.float32)
    wide = (6, BLOCK, 32, LANES)
    tall = [(6, 22, BLOCK, LANES), (6, 20, BLOCK, LANES)]
    send = local_source(psi)
    later, send = lax.optimization_barrier((psi, send))
    lines = lax.all_to_all(send, "stream", split_axis=0, concat_axis=0, tiled=True)
    to_left, to_right, to_first, to_second, to_high, to_low = messages(place, later)
    ends = exchange(to_right, to_left, "stream")
    sides = trade(to_first, to_second, "span")
    spectrum = transform(lines, (to_left,))
    own = lax.all_to_all(spectrum, "stream", split_axis=0, concat_axis=0, tiled=True)
    state = advect(stream_kernel, "advect_stream", [FULL], (psi, velocity) + ends, (spectrum,))
    below, above = exchange(*radial_messages(own), "radial")
    to_high, to_low = lax.optimization_barrier((to_high, to_low, spectrum))[:2]
    walls = exchange(to_high, to_low, "radial")
    state = advect(span_kernel, "advect_span", [wide, wide], (place, psi, velocity, state) + sides, (own,))
    rows, rows_first, rows_second = radial_assembly(place, own, below, above, state)
    first, second = trade(rows_first, rows_second, "span")
    state = advect(radial_kernel_step, "advect_radial", tall, (place, psi, velocity, state) + walls, (rows,))
    pressure, following = relaxation(place, rows, second, first, state)
    return following, pressure


def solution(mesh):
    return jax.shard_map(
        shards,
        mesh=mesh,
        in_specs=(P(None, "radial", "span", "stream"), P(None, "radial", "span", "stream")),
        out_specs=(P(None, "radial", "span", "stream"), P("radial", "span", "stream")),
        check_vma=False,
    )
```

```python
import functools
import math

import jax
import jax.numpy as jnp
import ml_dtypes
import numpy as np
from jax import lax
from jax.experimental import pallas as pl
from jax.experimental.pallas import tpu as pltpu
from jax.sharding import PartitionSpec as P

NX = 1024
LANES = 128
BLOCK = 16
PARTS = 8
FULL = (6, BLOCK, BLOCK, LANES)
COLUMNS = 20
SIDE_ROWS = 184
LINES = 50
ROWS = 56

WEISSENBERG = 20.0
EXTENSIBILITY = 100.0
TIME_STEP = 2.0
EPSILON = 1e-06
COSINES = tuple((math.cos((2 * number + 1) * math.pi / 12.0) for number in range(6)))
VMEM_LIMIT = 16 * 1024 * 1024
SOURCE_VMEM = 62 * 1024 * 1024


def split_bf16(table):
    high = table.astype(np.float32).astype(ml_dtypes.bfloat16)
    low = (table - high.astype(np.float64)).astype(np.float32).astype(ml_dtypes.bfloat16)
    return high, low


def tables():
    ordinal = np.arange(NX)
    wave = np.where(ordinal <= NX // 2, ordinal, ordinal - NX // 2)
    angle = 2.0 * np.pi / NX * ((ordinal[:, None] * wave[None, :]) % NX)
    fourier = -np.where((ordinal <= NX // 2)[None, :], np.cos(angle), np.sin(angle)) * NX**-0.5
    return split_bf16(fourier[:LANES])


def mode_table():
    ordinal = np.arange(NX)
    wave = np.where(ordinal <= NX // 2, ordinal, ordinal - NX // 2)
    diagonal = 4.0 + 4.0 * np.sin(np.pi * wave / NX) ** 2
    ratio = 4.0 / diagonal
    upper = 1.0 + ratio
    lower = np.maximum(0.3, 1.0 - ratio)
    rows = []
    for cosine in COSINES:
        omega = 1.0 / (0.5 * (upper + lower) + 0.5 * (upper - lower) * cosine)
        rows += [omega / diagonal, 1.0 - omega]
    rows += [np.zeros(NX)] * 4
    return np.stack(rows).astype(np.float32).reshape(16, PARTS, LANES).transpose(1, 0, 2)


def flag(place_ref, number, rows=8):
    return jnp.broadcast_to(place_ref[number : number + 1], (rows, LANES)) > 0.5


TABLE = tables()
MODES = mode_table()


def params(limit=VMEM_LIMIT):
    return pltpu.CompilerParams(vmem_limit_bytes=limit)


def cost(microseconds):
    return pl.CostEstimate(
        flops=int(microseconds * 1.1e9), bytes_accessed=int(microseconds * 3.6e6), transcendentals=0
    )


VMEM = pl.BlockSpec(memory_space=pltpu.VMEM)
SMEM = pl.BlockSpec(memory_space=pltpu.SMEM)
HBM = pl.BlockSpec(memory_space=pltpu.HBM)
ANY = pl.BlockSpec(memory_space=pl.ANY)


def dot_nt(left, right):
    return lax.dot_general(left, right, (((1,), (1,)), ((), ())), preferred_element_type=jnp.float32)


def dot_tn(left, right):
    return lax.dot_general(left, right, (((0,), (0,)), ((), ())), preferred_element_type=jnp.float32)


def pieces(value, count):
    found = []
    for _ in range(count):
        found.append(value.astype(jnp.bfloat16))
        value = value - found[-1].astype(jnp.float32)
    return found


def selection(shape, pairs):
    row = lax.broadcasted_iota(jnp.int32, shape, 0)
    column = lax.broadcasted_iota(jnp.int32, shape, 1)
    hit = None
    for first, last, shift in pairs:
        here = (row >= first) & (row <= last) & (column == row + shift)
        hit = here if hit is None else hit | here
    return jnp.where(hit, 1.0, 0.0).astype(jnp.bfloat16)


def sym_square(m):
    a, b, c, d, e, f = m
    bb, cc, ee = b * b, c * c, e * e
    return [
        a * a + bb + cc,
        b * (a + d) + c * e,
        c * (a + f) + b * e,
        bb + d * d + ee,
        e * (d + f) + b * c,
        cc + ee + f * f,
    ]


def sym_times(m, n):
    a, b, c, d, e, f = m
    p, q, r, s, t, u = n
    return [
        a * p + b * q + c * r,
        a * q + b * s + c * t,
        a * r + b * t + c * u,
        b * q + d * s + e * t,
        b * r + d * t + e * u,
        c * r + e * t + f * u,
    ]


DIAG = (1.0, 0.0, 0.0, 1.0, 0.0, 1.0)


def with_diag(m, value):
    return [m[i] + value if DIAG[i] else m[i] for i in range(6)]


def sym_exp(psi):
    m = [0.125 * v for v in psi]
    m2 = sym_square(m)
    m3 = sym_times(m, m2)
    tail = [m[i] * (1.0 / 24) + m2[i] * (1.0 / 120) + m3[i] * (1.0 / 720) for i in range(6)]
    tail = sym_times(m3, with_diag(tail, 1.0 / 6))
    out = with_diag([m[i] + 0.5 * m2[i] + tail[i] for i in range(6)], 1.0)
    for _ in range(3):
        out = sym_square(out)
    return out


def sym_inverse(grown, psi):
    a, b, c, d, e, f = grown
    scale = jnp.exp(-(psi[0] + psi[3] + psi[5]))
    return [
        (d * f - e * e) * scale,
        (c * e - b * f) * scale,
        (b * e - c * d) * scale,
        (a * f - c * c) * scale,
        (b * c - a * e) * scale,
        (a * d - b * b) * scale,
    ]


def spring(grown):
    return (EXTENSIBILITY - 3.0) / (EXTENSIBILITY - (grown[0] + grown[3] + grown[5]))


def segments(first, count):
    at = 0
    while at < count:
        row, column = divmod(first + at, COLUMNS)
        own = column < 18
        some = min(count - at, (18 if own else COLUMNS) - column)
        yield at, row * 24 + column + (0 if own else 4), some
        at += some


def source_kernel(psi_hbm, send_ref, psi_ref, stress, field, wrapped, packed, sems):
    chunk = BLOCK // SOURCE_CHUNKS
    arrivals = []
    for part in range(SOURCE_CHUNKS):
        rows = pl.ds(part * chunk, chunk)
        arrivals.append(pltpu.make_async_copy(psi_hbm.at[:, rows], psi_ref.at[:, rows], sems.at[part]))
        arrivals[-1].start()
    zero = jnp.zeros((24, LANES), jnp.float32)
    for comp in (1, 3, 4):
        for row in (0, 1, 2, 3, 20, 21, 22, 23):
            stress[comp, row] = zero

    def relax_row(row, carry):
        psi = [psi_ref[comp, row] for comp in range(6)]
        grown = sym_exp(psi)
        peterlin = spring(grown)
        pad = jnp.zeros((8, LANES), jnp.float32)
        for comp in range(6):
            value = peterlin * grown[comp]
            stress[comp, row + 4, 0:16] = value - 1.0 if DIAG[comp] else value
            stress[comp, row + 4, 16:24] = pad
        return carry

    for part in range(SOURCE_CHUNKS):
        arrivals[part].wait()
        lax.fori_loop(part * chunk, part * chunk + chunk, relax_row, 0, unroll=EXP_UNROLL)

    lane = lax.broadcasted_iota(jnp.int32, (24, LANES), 1)
    inner = [lane < LANES - 1, lane >= 1, lane < LANES - 2, lane >= 2]

    def along(value, shift):
        return pltpu.roll(value, shift % 24, 0)

    def shifted(value, shift):
        return pltpu.roll(value, shift % LANES, 1)

    def emit(row, plain, once, twice):
        parts = [shifted(once, -1), -shifted(once, 1), shifted(twice, -2), shifted(twice, 2)]
        total = plain - 2.0 * twice
        beyond = zero
        for part, mask in zip(parts, inner):
            kept = jnp.where(mask, part, 0.0)
            total = total + kept
            beyond = beyond + (part - kept)
        at = row * 24 if isinstance(row, int) else pl.multiple_of(row * 24, 8)
        field[pl.ds(at, 24)] = total
        wrapped[pl.ds(at, 24)] = beyond

    def body(row, carry):
        here = row + 2
        s11 = 0.25 * (stress[3, here + 2] - 2.0 * stress[3, here] + stress[3, here - 2])
        u12 = 0.5 * (stress[4, here + 1] - stress[4, here - 1])
        u01 = 0.5 * (stress[1, here + 1] - stress[1, here - 1])
        s22, s02, s00 = stress[5, here], stress[2, here], stress[0, here]
        c22 = 0.25 * (along(s22, -2) - 2.0 * s22 + along(s22, 2))
        c12 = along(u12, -1) - along(u12, 1)
        c02 = 0.5 * (along(s02, -1) - along(s02, 1))
        emit(row, s11 + c22 + c12, u01 + c02, 0.25 * s00)
        return carry

    lax.fori_loop(2, 18, body, 0, unroll=SOURCE_UNROLL)
    for row in (0, 1, 18, 19):
        here = row + 2
        other = here + 2 if row < 2 else here - 2
        s11 = 0.25 * stress[3, other]
        if row in (1, 18):
            near = here + 1 if row == 1 else here - 1
            sign = 0.5 if row == 1 else -0.5
            u12 = sign * stress[4, near]
            u01 = sign * stress[1, near]
            emit(row, s11 + along(u12, -1) - along(u12, 1), u01, zero)
        else:
            emit(row, s11, zero, zero)
    pick = selection((8, 2 * LANES), ((0, 1, 126), (2, 3, -2)))
    pick = pick + selection((8, 2 * LANES), ((0, 1, 126 + LANES), (2, 3, LANES - 2)))
    for part in range(PARTS):
        send_ref[part, ROWS - 8 : ROWS] = jnp.zeros((8, LANES), jnp.float32)
        packed[part, 48:64] = jnp.zeros((16, LANES), jnp.float32)
        for at, line, count in segments(part * LINES, LINES):
            send_ref[part, at : at + count] = field[line : line + count]
            packed[part, at : at + count] = wrapped[line : line + count]
    for part in range(PARTS):
        lines = dot_nt(pick, jnp.concatenate(pieces(packed[part], 2), axis=1))
        send_ref[part, LINES : LINES + 4, 0:64] = lines[0:4]


EXP_UNROLL = 4
SOURCE_CHUNKS = 4
SOURCE_UNROLL = 16


def local_source(psi):
    shape = jax.ShapeDtypeStruct
    return pl.pallas_call(
        source_kernel,
        out_shape=shape((PARTS, ROWS, LANES), jnp.float32),
        in_specs=[HBM],
        out_specs=VMEM,
        scratch_shapes=[
            pltpu.VMEM(FULL, jnp.float32),
            pltpu.VMEM((6, 24, 24, LANES), jnp.float32),
            pltpu.VMEM((480, LANES), jnp.float32),
            pltpu.VMEM((480, LANES), jnp.float32),
            pltpu.VMEM((PARTS, 64, LANES), jnp.float32),
            pltpu.SemaphoreType.DMA((SOURCE_CHUNKS,)),
        ],
        compiler_params=params(SOURCE_VMEM),
        cost_estimate=cost(3.0),
        name="local_source",
    )(psi)


def message_kernel(place_ref, psi_ref, left_ref, right_ref, first_ref, second_ref, high_ref, low_ref):
    even = flag(place_ref, 4, BLOCK)
    ends = sum(
        (selection((8, 2 * LANES), ((0, 2, k * LANES), (4, 6, k * LANES + 121))) for k in range(1, 2)),
        selection((8, 2 * LANES), ((0, 2, 0), (4, 6, 121))),
    )
    for comp in range(6):
        lines = jnp.concatenate(pieces(psi_ref[comp].reshape(BLOCK * BLOCK, LANES), 2), axis=1)
        found = dot_nt(ends, lines)
        left_ref[comp * 4 : comp * 4 + 4] = found[0:4]
        right_ref[comp * 4 : comp * 4 + 4] = found[4:8]
        for near in range(3):
            down = psi_ref[comp, :, near]
            up = psi_ref[comp, :, BLOCK - 3 + near]
            first_ref[comp, near] = jnp.where(even, up, down)
            second_ref[comp, near] = jnp.where(even, down, up)
            low_ref[comp, near] = psi_ref[comp, near]
            high_ref[comp, near] = psi_ref[comp, BLOCK - 3 + near]


def messages(place, psi):
    shape = jax.ShapeDtypeStruct
    return pl.pallas_call(
        message_kernel,
        out_shape=[shape((24, BLOCK * BLOCK), jnp.float32)] * 2
        + [shape((6, 3, BLOCK, LANES), jnp.float32)] * 4,
        in_specs=[VMEM, VMEM],
        out_specs=[VMEM] * 6,
        compiler_params=params(),
        cost_estimate=cost(4.0),
        name="messages",
    )(place, psi)


def transform_kernel(lines_ref, high_ref, low_ref, *rest):
    out_ref = rest[-1]
    edges = jnp.concatenate([lines_ref[part, LINES : LINES + 4] for part in range(PARTS)], axis=0)
    edges = jnp.concatenate(pieces(jnp.transpose(edges)[0:64], 2), axis=1)
    row = lax.broadcasted_iota(jnp.int32, (8 * PARTS, NX), 0) & (4 * PARTS - 1)
    lane = lax.broadcasted_iota(jnp.int32, (8 * PARTS, NX), 1)
    offset = jnp.where((row & 3) < 2, (row & 3) - 2, (row & 3) + LANES - 2)
    target = ((row >> 2) * LANES + offset + NX) & (NX - 1)
    target = jnp.where(lane == target, 1.0, 0.0).astype(jnp.bfloat16)
    beyond = jnp.dot(edges, target, preferred_element_type=jnp.float32)
    f = [lines_ref[part] + beyond[0:ROWS, part * LANES : (part + 1) * LANES] for part in range(PARTS)]
    s = [f[k] + f[k + 4] for k in range(4)]
    o = [f[k] - f[k + 4] for k in range(4)]
    half = math.sqrt(0.5)
    p0, p1, q0, q1 = s[0] + s[2], s[1] + s[3], s[0] - s[2], s[1] - s[3]
    minus, plus = half * (o[1] - o[3]), half * (o[1] + o[3])
    left = [p0 + p1, p0 - p1, q0, o[0] + minus, o[0] - minus, q1, plus + o[2], plus - o[2]]
    high, low = pieces(jnp.concatenate(left, axis=0), 2)
    both = jnp.concatenate([high, low], axis=1)
    wide = 2 * LANES
    found = []
    for part in range(4):
        cols = slice(part * wide, (part + 1) * wide)
        table = jnp.concatenate([high_ref[:, cols]] * 2, axis=0)
        first = jnp.dot(both, table, preferred_element_type=jnp.float32)
        second = jnp.dot(high, low_ref[:, cols], preferred_element_type=jnp.float32)
        found.append([first[k * ROWS : (k + 1) * ROWS] + second[k * ROWS : (k + 1) * ROWS] for k in range(8)])
    phase = lax.broadcasted_iota(jnp.int32, (ROWS, wide), 1) % 8
    outer = (phase == 1) | (phase == 7)
    middle = phase % 4 == 2
    turn = jnp.where(phase % 4 == 0, 0.0, jnp.where(phase < 4, 1.0, -1.0))
    for part in range(4):
        here, there = found[part], found[(part + 2) % 4]
        straight = jnp.where(middle, here[2], jnp.where(outer, here[3], here[4]))
        straight = jnp.where(phase == 0, here[0], jnp.where(phase == 4, here[1], straight))
        crossed = turn * jnp.where(middle, there[5], jnp.where(outer, there[6], there[7]))
        total = straight - crossed if part < 2 else straight + crossed
        out_ref[2 * part] = total[:, 0:LANES]
        out_ref[2 * part + 1] = total[:, LANES:]


def transform(lines, after):
    return pl.pallas_call(
        transform_kernel,
        out_shape=jax.ShapeDtypeStruct((PARTS, ROWS, LANES), jnp.float32),
        in_specs=[VMEM] * 3 + [ANY] * len(after),
        out_specs=VMEM,
        compiler_params=params(),
        cost_estimate=cost(1.5),
        name="transform",
    )(lines, *(jnp.asarray(table) for table in TABLE), *after)


def radial_message_kernel(own_ref, up_ref, down_ref):
    for to, line in ((down_ref, 0), (up_ref, 13 * COLUMNS)):
        at = 0
        while at < 140:
            part, row = divmod(line + at, LINES)
            some = min(140 - at, LINES - row)
            to[at : at + some] = own_ref[part, row : row + some]
            at += some
    for to in (down_ref, up_ref):
        to[140:144] = jnp.zeros((4, LANES), jnp.float32)


def radial_messages(own):
    return pl.pallas_call(
        radial_message_kernel,
        out_shape=[jax.ShapeDtypeStruct((144, LANES), jnp.float32)] * 2,
        in_specs=[VMEM],
        out_specs=[VMEM] * 2,
        compiler_params=params(),
        cost_estimate=cost(0.3),
        name="radial_messages",
    )(own)


def radial_kernel(place_ref, own_ref, low_ref, high_ref, after_ref, out_ref, first_ref, second_ref, flat, flat_low, flat_high):
    flat[...] = jnp.zeros_like(flat)
    for part in range(PARTS):
        for at, line, count in segments(part * LINES, LINES):
            flat[line : line + count] = own_ref[part, at : at + count]
    flat_low[...] = jnp.zeros_like(flat_low)
    flat_high[...] = jnp.zeros_like(flat_high)
    for k in range(7):
        for to, message in ((flat_low, low_ref), (flat_high, high_ref)):
            to[k * 24 : k * 24 + 18] = message[k * 20 : k * 20 + 18]
            to[k * 24 + 22 : k * 24 + 24] = message[k * 20 + 18 : k * 20 + 20]
    has_low, has_high = flag(place_ref, 0, 24), flag(place_ref, 1, 24)
    even = flag(place_ref, 4)

    def own(row):
        return flat[row * 24 : row * 24 + 24]

    def low(row):
        at = (row - 13) * 24
        return jnp.where(has_low, flat_low[at : at + 24], 0.0)

    def high(row):
        return jnp.where(has_high, flat_high[row * 24 : row * 24 + 24], 0.0)

    for to in (first_ref, second_ref):
        to[SIDE_ROWS - 8 : SIDE_ROWS] = jnp.zeros((8, LANES), jnp.float32)
    for row in range(26):
        if row < 3:
            value = low(row + 13)
        elif row < 5:
            value = low(row + 13) + jnp.where(has_low, own(row - 3), 0.0)
        elif row < 7:
            value = low(row + 13) + own(row - 3)
        elif row < 19:
            value = own(row - 3)
        elif row < 21:
            value = own(row - 3) + high(row - 19)
        elif row < 23:
            value = jnp.where(has_high, own(row - 3), 0.0) + high(row - 19)
        else:
            value = high(row - 19)
        out_ref[row] = value
        up = pltpu.roll(value, 24 - 11, 0)[0:8]
        down = pltpu.roll(value, 2, 0)[0:8]
        at = slice(row * 7, row * 7 + 7)
        first_ref[at] = jnp.where(even, up, down)[0:7]
        second_ref[at] = jnp.where(even, down, up)[0:7]


def radial_assembly(place, own, low, high, after):
    shape = jax.ShapeDtypeStruct
    return pl.pallas_call(
        radial_kernel,
        out_shape=(
            shape((26, 24, LANES), jnp.float32),
            shape((SIDE_ROWS, LANES), jnp.float32),
            shape((SIDE_ROWS, LANES), jnp.float32),
        ),
        in_specs=[VMEM] * 4 + [ANY],
        out_specs=[VMEM] * 3,
        scratch_shapes=[
            pltpu.VMEM((480, LANES), jnp.float32),
            pltpu.VMEM((168, LANES), jnp.float32),
            pltpu.VMEM((168, LANES), jnp.float32),
        ],
        compiler_params=params(),
        cost_estimate=cost(0.6),
        name="radial_assembly",
    )(place, own, low, high, after)


def relax_kernel(place_ref, modes_ref, rows_ref, second_ref, first_ref, *rest):
    whole_ref, out_hbm, following_hbm, out_ref, source, one, two, sems = rest
    copies = [pltpu.make_async_copy(whole_ref, following_hbm, sems.at[0])]
    copies[0].start()
    has_low, has_high, even_span = (flag(place_ref, number) for number in (2, 3, 4))
    open_low, open_high = flag(place_ref, 0, 32), flag(place_ref, 1, 32)
    sublane = lax.broadcasted_iota(jnp.int32, (8, LANES), 0)
    always = sublane >= 0
    inside = jnp.concatenate(
        [jnp.where(part, 1.0, 0.0) for part in (has_low, always, always, has_high)], axis=0
    )
    modes = sum(modes_ref[k] * jnp.broadcast_to(place_ref[8 + k : 9 + k], (16, LANES)) for k in range(PARTS))
    weights = [inside * jnp.broadcast_to(modes[2 * j : 2 * j + 1], (32, LANES)) for j in range(6)]
    keeps = [jnp.broadcast_to(modes[2 * j + 1 : 2 * j + 2], (32, LANES)) for j in range(6)]
    pad = jnp.zeros((8, LANES), jnp.float32)

    def walled(row, value):
        if row < 5:
            return jnp.where(open_low, value, 0.0)
        if row > 20:
            return jnp.where(open_high, value, 0.0)
        return value

    for row in range(26):
        own = rows_ref[row]
        tail = own[16:24]
        first, other = (ref[row * 7 : row * 7 + 8] for ref in (first_ref, second_ref))
        low = jnp.where(has_low, jnp.where(even_span, other, first), 0.0)
        high = jnp.where(has_high, jnp.where(even_span, first, other), 0.0)
        low = pltpu.roll(low, 3, 0)
        high = pltpu.roll(high, 6, 0)
        value = jnp.concatenate(
            [
                jnp.where(sublane >= 6, tail, 0.0) + jnp.where(sublane >= 3, low, 0.0),
                own[0:8] + jnp.where(sublane < 2, low, 0.0),
                own[8:16] + jnp.where(sublane >= 6, high, 0.0),
                jnp.where(sublane < 2, tail, 0.0) + jnp.where(sublane < 6, high, 0.0),
            ],
            axis=0,
        )
        source[row] = value
        one[row, 8:40] = walled(row, value * weights[0])
        for buffer in (one, two):
            buffer[row, 0:8] = pad
            buffer[row, 40:48] = pad

    old, new = one, two
    for sweep in range(1, 6):
        weight, keep = weights[sweep], keeps[sweep]
        for row in range(sweep, 26 - sweep):
            if sweep == 5:
                at, weight_here, keep_here, here = 16, weight[8:24], keep[8:24], source[row, 8:24]
            else:
                at, weight_here, keep_here, here = 8, weight, keep, source[row]
            end = 32 if sweep == 5 else 40
            beside = (old[row - 1, at:end] + old[row + 1, at:end]) + (
                old[row, at - 1 : end - 1] + old[row, at + 1 : end + 1]
            )
            value = keep_here * old[row, at:end] + weight_here * (here + beside)
            if sweep == 5:
                out_ref[row - 5] = value
                if row % 8 == 4:
                    rows = pl.ds(row - 12, 8)
                    copies.append(
                        pltpu.make_async_copy(out_ref.at[rows], out_hbm.at[rows], sems.at[len(copies)])
                    )
                    copies[-1].start()
            else:
                new[row, 8:40] = walled(row, value)
        old, new = new, old
    for copy in copies:
        copy.wait()


def relaxation(place, rows, low, high, whole):
    shape = jax.ShapeDtypeStruct
    return pl.pallas_call(
        relax_kernel,
        out_shape=(
            shape((BLOCK, BLOCK, LANES), jnp.float32),
            shape((6, BLOCK, BLOCK, LANES), jnp.float32),
        ),
        in_specs=[VMEM] * 6,
        out_specs=(HBM, HBM),
        scratch_shapes=[
            pltpu.VMEM((BLOCK, BLOCK, LANES), jnp.float32),
            pltpu.VMEM((26, 32, LANES), jnp.float32),
            pltpu.VMEM((26, 48, LANES), jnp.float32),
            pltpu.VMEM((26, 48, LANES), jnp.float32),
            pltpu.SemaphoreType.DMA((3,)),
        ],
        compiler_params=params(),
        cost_estimate=cost(1.8),
        name="relaxation",
    )(place, jnp.asarray(MODES), rows, low, high, whole)


def weno(positive, p):
    p0 = jnp.where(positive, p[0], p[4])
    p1 = jnp.where(positive, p[1], p[3])
    p2 = p[2]
    p3 = jnp.where(positive, p[3], p[1])
    k1 = (0.609375 * p1) * p1 + 0.75 * EPSILON
    k2 = (0.609375 * p2) * p2 + 0.75 * EPSILON
    r0 = p0 - 1.375 * p1
    r1 = p1 - 0.625 * p2
    r2 = p3 - 1.375 * p2
    q0, q1, q2 = r0 * r0 + k1, r1 * r1 + k2, r2 * r2 + k2
    q01, q02, q12 = q0 * q1, q0 * q2, q1 * q2
    w0, w1, w2 = q12 * q12, 6.0 * (q02 * q02), 3.0 * (q01 * q01)
    middle = p1 - p2
    t0 = (p0 - p1) - middle
    t2 = middle - (p2 - p3)
    total = (w0 + w1) + w2
    guess = pl_reciprocal(total, approx=True)
    inverse = guess * (2.0 - total * guess)
    return ((w0 + w0) * t0 + w2 * t2) * inverse - p1


pl_reciprocal = pltpu.reciprocal


def wind(velocity_ref, direction, row):
    speed = velocity_ref[direction, row]
    positive = speed > 0
    straight = TIME_STEP * speed
    bent = (TIME_STEP / 6) * jnp.abs(speed)
    return positive, straight, bent, jnp.where(positive, 1.0 / 3, 2.0 / 3)


def advected(blow, behind, p):
    positive, straight, bent, side = blow
    return straight * (behind - side * p[2]) + bent * weno(positive, p)


def stream_kernel(psi_ref, velocity_ref, left_ref, right_ref, *rest):
    out_ref, ahead = rest[-2:]
    spread = []
    for comp in range(6):
        ends = jnp.concatenate([right_ref[comp * 4 : comp * 4 + 4], left_ref[comp * 4 : comp * 4 + 4]], axis=0)
        spread += pieces(ends, 2)
    spread = jnp.concatenate([v.astype(jnp.float32) for v in spread], axis=0)
    spread = jnp.transpose(spread).astype(jnp.bfloat16)
    place = selection((8, LANES), ((0, 2, 0), (4, 6, 121))).astype(jnp.float32)
    for comp in range(6):
        rows = [place] * 2
        if comp > 0:
            rows = [jnp.zeros((comp * 16, LANES), jnp.float32)] + rows
        if comp < 5:
            rows = rows + [jnp.zeros((80 - comp * 16, LANES), jnp.float32)]
        rows = jnp.concatenate(rows, axis=0).astype(jnp.bfloat16)
        found = jnp.dot(spread, rows, preferred_element_type=jnp.float32)
        ahead[comp] = found.reshape(BLOCK, BLOCK, LANES)
    lane = lax.broadcasted_iota(jnp.int32, (BLOCK, LANES), 1)

    def step(row, carry):
        blow = wind(velocity_ref, 0, row)
        for comp in range(6):
            psi = psi_ref[comp, row]
            far = ahead[comp, row]
            lines = []
            for j in range(-3, 4):
                if j > 0:
                    mixed = jnp.where(lane < j, far, psi)
                else:
                    mixed = jnp.where(lane >= LANES + j, far, psi)
                lines.append(pltpu.roll(mixed, (-j) % LANES, 1) if j else psi)
            steps = [lines[j + 1] - lines[j] for j in range(6)]
            change = advected(blow, steps[2], [steps[j] - steps[j + 1] for j in range(5)])
            out_ref[comp, row] = psi - change
        return carry

    lax.fori_loop(0, BLOCK, step, 0, unroll=STREAM_UNROLL)


def span_kernel(place_ref, psi_ref, velocity_ref, base_ref, first_ref, second_ref, *rest):
    out_ref, column, second = rest[-3:]
    has_down, has_up, even = (flag(place_ref, number, BLOCK) for number in (2, 3, 4))
    for comp in range(6):
        for near in range(3):
            first, other = first_ref[comp, near], second_ref[comp, near]
            column[comp, :, 5 + near] = jnp.where(has_down, jnp.where(even, other, first), 0.0)
            column[comp, :, 24 + near] = jnp.where(has_up, jnp.where(even, first, other), 0.0)

    def bend(row, carry):
        for comp in range(6):
            column[comp, row, 8:24] = psi_ref[comp, row]
            one, two, three = column[comp, row, 5:25], column[comp, row, 6:26], column[comp, row, 7:27]
            second[comp, row, 5:25] = (two - one) - (three - two)
        return carry

    lax.fori_loop(0, BLOCK, bend, 0)

    def step(row, carry):
        blow = wind(velocity_ref, 2, row)
        for comp in range(6):
            behind = psi_ref[comp, row] - column[comp, row, 7:23]
            change = advected(blow, behind, [second[comp, row, 5 + j : 21 + j] for j in range(5)])
            out_ref[comp, row] = base_ref[comp, row] - change
        return carry

    lax.fori_loop(0, BLOCK, step, 0, unroll=STEP_UNROLL)


def radial_kernel_step(place_ref, psi_ref, velocity_ref, base_ref, low_ref, high_ref, *rest):
    out_ref, column, second = rest[-3:]
    has_low, has_high = flag(place_ref, 0, BLOCK), flag(place_ref, 1, BLOCK)
    for comp in range(6):
        for near in range(3):
            column[comp, near] = jnp.where(has_low, low_ref[comp, near], 0.0)
            column[comp, 19 + near] = jnp.where(has_high, high_ref[comp, near], 0.0)

    def copy_in(row, carry):
        for comp in range(6):
            column[comp, row + 3] = psi_ref[comp, row]
        return carry

    lax.fori_loop(0, BLOCK, copy_in, 0)

    def bend(row, carry):
        for comp in range(6):
            one, two, three = column[comp, row], column[comp, row + 1], column[comp, row + 2]
            second[comp, row] = (two - one) - (three - two)
        return carry

    lax.fori_loop(0, 20, bend, 0)

    def step(row, carry):
        blow = wind(velocity_ref, 1, row)
        tensor = [psi_ref[comp, row] for comp in range(6)]
        grown = sym_exp(tensor)
        peterlin = spring(grown)
        shrunk = sym_inverse(grown, tensor)
        for comp in range(6):
            back = shrunk[comp] - peterlin if DIAG[comp] else shrunk[comp]
            behind = tensor[comp] - column[comp, row + 2]
            change = advected(blow, behind, [second[comp, row + j] for j in range(5)])
            out_ref[comp, row] = (base_ref[comp, row] + (TIME_STEP / WEISSENBERG) * back) - change
        return carry

    lax.fori_loop(0, BLOCK, step, 0, unroll=STEP_UNROLL)


STEP_UNROLL = 2
STREAM_UNROLL = 8


def advect(kernel, name, scratch, arrays, after):
    return pl.pallas_call(
        kernel,
        out_shape=jax.ShapeDtypeStruct(FULL, jnp.float32),
        in_specs=[VMEM] * len(arrays) + [ANY] * len(after),
        out_specs=VMEM,
        scratch_shapes=[pltpu.VMEM(shape, jnp.float32) for shape in scratch],
        compiler_params=params(),
        cost_estimate=cost(2.5),
        name=name,
    )(*arrays, *after)


def ring(axis, step):
    count = lax.axis_size(axis)
    return [(i, (i + step) % count) for i in range(count)]


def exchange(to_next, to_previous, axis):
    return (
        lax.ppermute(to_next, axis, ring(axis, 1)),
        lax.ppermute(to_previous, axis, ring(axis, -1)),
    )


def trade(first, second, axis):
    count = lax.axis_size(axis)
    inner = [(i, i ^ 1) for i in range(count)]
    outer = [(i, (i - 1) % count if i % 2 == 0 else (i + 1) % count) for i in range(count)]
    second = lax.ppermute(second, axis, outer)
    return lax.ppermute(first, axis, inner), second


def shards(psi, velocity):
    radial, span = lax.axis_index("radial"), lax.axis_index("span")
    bits = (radial > 0) + 2 * (radial < 7) + 4 * (span > 0) + 8 * (span < 3) + 16 * (span % 2 == 0)
    number = lax.broadcasted_iota(jnp.int32, (16, LANES), 0)
    place = ((bits >> number) & (number < 8)) | (number == lax.axis_index("stream") + 8)
    place = place.astype(jnp.float32)
    wide = (6, BLOCK, 32, LANES)
    tall = [(6, 22, BLOCK, LANES), (6, 20, BLOCK, LANES)]
    send = local_source(psi)
    later, send = lax.optimization_barrier((psi, send))
    lines = lax.all_to_all(send, "stream", split_axis=0, concat_axis=0, tiled=True)
    to_left, to_right, to_first, to_second, to_high, to_low = messages(place, later)
    ends = exchange(to_right, to_left, "stream")
    sides = trade(to_first, to_second, "span")
    spectrum = transform(lines, (to_left,))
    own = lax.all_to_all(spectrum, "stream", split_axis=0, concat_axis=0, tiled=True)
    state = advect(stream_kernel, "advect_stream", [FULL], (psi, velocity) + ends, (spectrum,))
    below, above = exchange(*radial_messages(own), "radial")
    to_high, to_low = lax.optimization_barrier((to_high, to_low, spectrum))[:2]
    walls = exchange(to_high, to_low, "radial")
    state = advect(span_kernel, "advect_span", [wide, wide], (place, psi, velocity, state) + sides, (own,))
    rows, rows_first, rows_second = radial_assembly(place, own, below, above, state)
    first, second = trade(rows_first, rows_second, "span")
    state = advect(radial_kernel_step, "advect_radial", tall, (place, psi, velocity, state) + walls, (rows,))
    pressure, following = relaxation(place, rows, second, first, state)
    return following, pressure


def solution(mesh):
    return jax.shard_map(
        shards,
        mesh=mesh,
        in_specs=(P(None, "radial", "span", "stream"), P(None, "radial", "span", "stream")),
        out_specs=(P(None, "radial", "span", "stream"), P("radial", "span", "stream")),
        check_vma=False,
    )
```
